32 devices in a mesh: dp: 4 (over z), trow: 2 (over y), tcol: 4 (over x, core).
Axes of the slice: x: 2, y: 2, z: 4, core: 2. Of those that a mesh axis runs over, the one named last changes fastest.
Arguments:
- embeddings: bfloat16 [1024, 4, 2, 768], P('dp', 'tcol', 'trow'), may hold values from -21.5 to 21.5
- targets: bfloat16 [1024, 256], P('dp'), may hold values from -384 to 384
- gram_prior: float32 [4, 2, 4, 192, 6144], P(None, 'trow', 'dp', None, 'tcol'), may hold values from -0.2 to 4.2, as said below
- penalty: float32 [4, 2, 4, 192], P('tcol', 'trow', 'dp'), may hold values from 0.3 to 3
Outputs:
- gram: float32 [4, 2, 4, 192, 6144], P(None, 'trow', 'dp', None, 'tcol')
- weights: float32 [4, 2, 4, 192, 256], P('tcol', 'trow', 'dp')
- residual: float32 [4, 2, 4, 192, 256], P('tcol', 'trow', 'dp')
The draws below stay inside these ranges and needn't reach their ends.
Inputs may be any that keep to these rules, and one draw needn't show every extreme that they name: `gram_prior`: symmetric and positive definite as a 6144 x 6144 matrix.
All inputs are finite; a program needn't handle non-finite values.
Results may differ from the reference program's by a relative error of at most 0.0003.
Values may be sent and summed in bfloat16 or wider, within the bound.
No kernel may reach another device: no remote copies, remote signals or barrier semaphores. Data moves between devices by JAX's collectives and lax.ppermute only.
A program may use at most 64 MiB of HBM per device.

```python
import math
import jax
import jax.numpy as jnp
from jax import lax

HEADS = 256
ITERS = 2
D = 6144
ROWS = 1024
XB = 768
GR = 192
N_DP = 4
N_TROW = 2
N_TCOL = 4


def draw_embeddings(key, part):
    key_spread = jax.random.fold_in(key, 11)
    key_values = jax.random.fold_in(key, 12)
    within = (jnp.arange(D) % XB).astype(jnp.float32)
    rising = 3.0 ** (within / XB)
    spread = jax.random.uniform(key_spread, (D,), jnp.float32, 0.0, 1.0)
    column_scale = rising * 4.0 ** spread / 3.0
    samples = jnp.clip(jax.random.normal(key_values, (ROWS, D), jnp.float32), -5.0, 5.0)
    values = samples * column_scale
    return values.reshape(ROWS, N_TCOL, N_TROW, XB).astype(jnp.bfloat16)


def draw_gram_prior(key, part):
    key_level = jax.random.fold_in(key, 21)
    key_noise = jax.random.fold_in(key, 22)
    diagonal = 4.0 ** jax.random.uniform(key_level, (D,), jnp.float32, 0.0, 1.0)
    fluctuation = jnp.clip(jax.random.normal(key_noise, (D, D), jnp.float32), -4.0, 4.0)
    symmetric = (fluctuation + fluctuation.T) * (0.25 / D ** 0.5)
    matrix = symmetric + jnp.diag(diagonal)
    return matrix.reshape(N_TCOL, N_TROW, N_DP, GR, D)


def shard_levels(key, shape, cuts, least, top_value):
    gain = 1.0
    for position, parts in cuts:
        heights = jax.random.uniform(jax.random.fold_in(jax.random.fold_in(key, 6), position), (parts,), jnp.float32, least / len(cuts), top_value / len(cuts))
        gain = gain * jnp.repeat(jnp.exp(heights), shape[position] // parts).reshape((-1,) + (1,) * (len(shape) - 1 - position))
    return gain


def normal_values(own_key, shape, scale, limit, pieces=(), held_as=jnp.bfloat16):
    gain = shard_levels(own_key, shape, pieces, -0.22, 0.18) if pieces else 1.0
    drawn = jax.random.normal(own_key, shape, jnp.float32) * scale * gain
    return jnp.minimum(jnp.maximum(drawn, -limit), limit).astype(held_as)


def setup_inputs(seed: int = 0) -> dict:
    keys = jax.random.split(jax.random.key(seed), 5)
    return {
        "embeddings": draw_embeddings(jax.random.fold_in(keys[4], 71), 0),
        "targets": normal_values(keys[1], (ROWS, HEADS), (2 * ROWS ** 0.5), 384.0, ((0, 4),)),
        "gram_prior": draw_gram_prior(jax.random.fold_in(keys[4], 71), 0),
        "penalty": jnp.clip(jnp.exp(math.log(3.0) - 2.3025851 * jax.random.uniform(keys[3], (N_TCOL, N_TROW, N_DP, GR), jnp.float32) ** shard_levels(keys[3], (N_TCOL, N_TROW, N_DP, GR), ((0, 4), (1, 2), (2, 4)), -0.2, 0.2)), 0.3, 3.0),
    }


def apply_operator(gram_full, penalty_rows, vector):
    product = jnp.dot(gram_full, vector, precision=lax.Precision.HIGHEST, preferred_element_type=jnp.float32)
    return product + penalty_rows[:, None] * vector


def reference(embeddings, targets, gram_prior, penalty):
    features = embeddings.reshape(ROWS, D)
    increment = jnp.dot(features.T, features, preferred_element_type=jnp.float32)
    gram_full = gram_prior.reshape(D, D) + increment / ROWS
    right_side = jnp.dot(features.T, targets, preferred_element_type=jnp.float32) / ROWS
    penalty_rows = penalty.reshape(D)
    weights = jnp.zeros((D, HEADS), jnp.float32)
    residual = right_side
    direction = right_side
    norm_now = jnp.sum(residual * residual, axis=0)
    for iteration in range(ITERS):
        applied = apply_operator(gram_full, penalty_rows, direction)
        step_size = norm_now / jnp.sum(direction * applied, axis=0)
        weights = weights + step_size * direction
        residual = residual - step_size * applied
        if iteration + 1 < ITERS:
            norm_next = jnp.sum(residual * residual, axis=0)
            direction = residual + (norm_next / norm_now) * direction
            norm_now = norm_next
    block_shape = (N_TCOL, N_TROW, N_DP, GR)
    return (gram_full.reshape(block_shape + (D,)), weights.reshape(block_shape + (HEADS,)), residual.reshape(block_shape + (HEADS,)))
```

```python
import jax
import jax.numpy as jnp
from jax import lax
from jax.sharding import PartitionSpec as P

ITERS = 2
NT = (((1,), (1,)), ((), ()))


def turn(count, shift):
    return [(place, (place + shift) % count) for place in range(count)]


def swap(count, bit):
    return [(place, place ^ bit) for place in range(count)]


def all_sum(value, axis_names):
    count = 1
    for name in axis_names:
        count *= lax.axis_size(name)
    spread = jnp.broadcast_to(value[None], (count,) + value.shape)
    return jnp.sum(lax.all_to_all(spread, axis_names, split_axis=0, concat_axis=0, tiled=True), axis=0)


def pair_order(own, other, upper):
    first = jnp.where(upper, other, own)
    second = jnp.where(upper, own, other)
    return jnp.concatenate([first, second], axis=0)


def gather_pairs(value, axis, count):
    place = lax.axis_index(axis)
    bit = count // 2
    held = value[None]
    bits = []
    while bit >= 1:
        other = lax.ppermute(held, axis, swap(count, bit))
        upper = (place & bit) != 0
        first = jnp.where(upper, other, held)
        second = jnp.where(upper, held, other)
        held = jnp.stack([first, second], axis=1).reshape((2 * held.shape[0],) + held.shape[1:])
        bits.append(bit)
        bit //= 2
    return held


def sum_pairs(value, axis, count):
    if count == 1:
        return value
    place = lax.axis_index(axis)
    upper = (place & 1) != 0
    half = value.shape[0] // 2
    low, high = value[:half], value[half:]
    kept = jnp.where(upper, high, low)
    held = kept + lax.ppermute(jnp.where(upper, low, high), axis, swap(count, 1))
    bit = 2
    while bit < count:
        held = held + lax.ppermute(held, axis, swap(count, bit))
        bit *= 2
    other = lax.ppermute(held, axis, swap(count, 1))
    return pair_order(held, other, upper)


def scatter_sum(value, axis, count):
    place = lax.axis_index(axis)
    total = lax.dynamic_index_in_dim(value, place, 0, keepdims=False)
    for shift in range(1, count):
        target = lax.rem(place + shift, count)
        part = lax.dynamic_index_in_dim(value, target, 0, keepdims=False)
        total = total + lax.ppermute(part, axis, turn(count, shift))
    return total


def shards(embeddings, targets, gram_prior, penalty):
    row_count = embeddings.shape[0]
    block_width = embeddings.shape[3]
    head_count = targets.shape[1]
    data_count = lax.axis_size("dp")
    trow_count = lax.axis_size("trow")
    tcol_count = lax.axis_size("tcol")
    piece_rows = block_width // data_count
    total_rows = row_count * data_count
    tile_rows = tcol_count * piece_rows
    data_place = lax.axis_index("dp")
    trow_place = lax.axis_index("trow")
    tcol_place = lax.axis_index("tcol")
    upper = (tcol_place & 1) != 0
    head_half = head_count // 2

    own = embeddings.reshape(row_count, block_width).T
    heads = targets.T
    head_part = jnp.where(upper, heads[head_half:], heads[:head_half])
    carried = jnp.concatenate([own, head_part], axis=0)
    groups = [carried]
    for _ in range(1, data_count):
        groups.append(lax.ppermute(groups[-1], "dp", turn(data_count, 1)))
    own_groups = [group[:block_width] for group in groups]
    blocks = [jnp.concatenate(own_groups, axis=1)]
    for shift in range(1, trow_count):
        blocks.append(
            jnp.concatenate(
                [lax.ppermute(group, "trow", turn(trow_count, shift)) for group in own_groups], axis=1
            )
        )
    head_own = jnp.concatenate([group[block_width:] for group in groups], axis=1)
    head_other = lax.ppermute(head_own, "tcol", swap(tcol_count, 1))
    all_heads = pair_order(head_own, head_other, upper)
    stacked = jnp.stack(blocks)
    order = lax.rem(trow_place - jnp.arange(trow_count) + trow_count, trow_count)
    columns = jnp.take(stacked, order, axis=0).reshape(trow_count * block_width, total_rows)
    piece = lax.dynamic_slice_in_dim(blocks[0], data_place * piece_rows, piece_rows, axis=0)
    panel = gather_pairs(piece, "tcol", tcol_count).reshape(tile_rows, total_rows)

    summed = lax.dot_general(panel, columns, NT, preferred_element_type=jnp.float32)
    gram_tile = gram_prior.reshape(tile_rows, trow_count * block_width) + summed / total_rows
    right_columns = lax.dot_general(columns, all_heads, NT, preferred_element_type=jnp.float32) / total_rows
    right_rows = lax.dot_general(panel, all_heads, NT, preferred_element_type=jnp.float32) / total_rows

    def own_rows(value):
        return lax.dynamic_slice_in_dim(value, tcol_place * piece_rows, piece_rows, axis=0)

    penalty_rows = penalty.reshape(piece_rows, 1)
    start = own_rows(right_rows)
    rows_part = jnp.dot(gram_tile, right_columns, precision=lax.Precision.HIGH)
    rows_part = lax.dynamic_update_slice_in_dim(
        rows_part, own_rows(rows_part) + penalty_rows * start, tcol_place * piece_rows, axis=0
    )
    image_rows = sum_pairs(rows_part, "tcol", tcol_count)
    image = own_rows(image_rows)
    partial = lax.dot_general(
        gram_tile, image_rows, (((0,), (0,)), ((), ())), precision=lax.Precision.HIGH
    )
    partial = partial.reshape(trow_count, data_count * piece_rows, head_count)
    second = scatter_sum(partial, "trow", trow_count).reshape(data_count, piece_rows, head_count)
    second = scatter_sum(second, "dp", data_count) + penalty_rows * image

    def sums(*pairs):
        return jnp.stack([jnp.sum(a * b, axis=0) for a, b in pairs])

    early = all_sum(sums((start, start), (start, image)), ("dp", "trow", "tcol"))
    norm, curvature = early[0], early[1]
    step = norm / curvature
    residual = start - step * image
    applied = image - step * second
    late = all_sum(sums((residual, residual), (residual, applied), (residual, image)), ("dp", "trow", "tcol"))
    ratio = late[0] / norm
    direction = residual + ratio * start
    moved = applied + ratio * image
    next_step = late[0] / (late[1] + ratio * late[2])
    weights = step * start + next_step * direction
    residual = residual - next_step * moved
    out_shape = (1, 1, 1, piece_rows, head_count)
    return (gram_tile.reshape(gram_prior.shape), weights.reshape(out_shape), residual.reshape(out_shape))


def solution(mesh):
    placed = (
        P("dp", "tcol", "trow", None),
        P("dp", None),
        P(None, "trow", "dp", None, "tcol"),
        P("tcol", "trow", "dp", None),
    )
    return jax.shard_map(
        shards,
        mesh=mesh,
        in_specs=placed,
        out_specs=(
            P(None, "trow", "dp", None, "tcol"),
            P("tcol", "trow", "dp", None, None),
            P("tcol", "trow", "dp", None, None),
        ),
        check_vma=False,
    )
```

```python
import functools

import jax
import jax.numpy as jnp
import numpy as np
from jax import lax
from jax.experimental import pallas as pl
from jax.experimental.pallas import tpu as pltpu
from jax.sharding import PartitionSpec as P

NT = (((1,), (1,)), ((), ()))
NN = (((1,), (0,)), ((), ()))
VMEM = pl.BlockSpec(memory_space=pltpu.VMEM)
VMEM_BYTES = 40 * 2**20


def swap(count, bit):
    return [(place, place ^ bit) for place in range(count)]


class Ring:
    def __init__(self, data_count, trow_count):
        self.data_count = data_count
        self.count = data_count * trow_count
        self.cells = []
        for trow in range(trow_count):
            along = range(data_count) if trow % 2 == 0 else reversed(range(data_count))
            self.cells += [(data, trow) for data in along]
        flat = [data * trow_count + trow for data, trow in self.cells]
        self.ahead = [(flat[i], flat[(i + 1) % self.count]) for i in range(self.count)]
        self.back = [(target, source) for source, target in self.ahead]
        self.far = self.count // 2
        self.offsets = [0]
        for distance in range(1, self.far):
            self.offsets += [-distance, distance]
        self.offsets.append(self.far)
        self.place = np.zeros((data_count, trow_count), np.int32)
        for position, (data, trow) in enumerate(self.cells):
            self.place[data, trow] = position
        self.rounds = np.zeros((self.count, data_count), np.int32)
        self.row_chunk = np.zeros((self.count, self.count), np.int32)
        self.row_trow = np.zeros((self.count, self.count), np.int32)
        self.row_data = np.zeros((self.count, self.count), np.int32)
        for position, (data, trow) in enumerate(self.cells):
            first = trow * data_count
            near = sorted(range(first, first + data_count), key=lambda q: (abs(q - position), q))
            chunk_of = {}
            for turn, other in enumerate(near):
                self.rounds[position, turn] = self.offsets.index(other - position)
                chunk_of[self.cells[other][0]] = turn
            for index, offset in enumerate(self.offsets):
                other_data, other_trow = self.cells[(position + offset) % self.count]
                self.row_chunk[position, index] = chunk_of[other_data]
                self.row_trow[position, index] = other_trow
                self.row_data[position, index] = other_data

    def gather(self, value, split_rows):
        ahead = back = value
        shards = [value]
        for _ in range(1, self.far):
            ahead = lax.ppermute(ahead, ("dp", "trow"), self.ahead)
            back = lax.ppermute(back, ("dp", "trow"), self.back)
            shards += [ahead, back]
        half = (split_rows // 2 + 15) // 16 * 16
        low = lax.ppermute(ahead[:half], ("dp", "trow"), self.ahead)
        high = lax.ppermute(back[half:split_rows], ("dp", "trow"), self.back)
        return shards + [low, high]


def split(value):
    high = value.astype(jnp.bfloat16)
    return high, (value - high.astype(jnp.float32)).astype(jnp.bfloat16)


def dot(a, b, dims):
    return lax.dot_general(a, b, dims, preferred_element_type=jnp.float32)


def product(a, b):
    (a_high, a_low), (b_high, b_low) = a, b
    return dot(a_high, b_high, NN) + (dot(a_high, b_low, NN) + dot(a_low, b_high, NN))


def gram_kernel(sizes, meta, *refs):
    n, data_count, trow_count, tcol_count, piece, width, head_part, block, total_rows, groups = sizes
    heads = head_part * tcol_count
    shard_refs = refs[: n + 1]
    round_refs = refs[n + 1 : n + 1 + 3 * groups]
    prior_ref, gram_ref, right_ref, image_ref, columns, rows, target = refs[n + 1 + 3 * groups :]
    step = pl.program_id(0)
    me = meta[2 * n]

    @pl.when(step == 0)
    def _():
        for index in range(n):
            chunk = meta[index]
            base = pl.multiple_of(meta[n + index] * width, 16)
            if index < n - 1:
                columns[chunk, pl.ds(base, width), :] = shard_refs[index][:width, :]
            else:
                half = shard_refs[n - 1].shape[0]
                columns[chunk, pl.ds(base, half), :] = shard_refs[n - 1][...]
                columns[chunk, pl.ds(pl.multiple_of(base + half, 16), width - half), :] = shard_refs[n][...]
        turn = 0
        for group in range(groups):
            own, far, near = round_refs[3 * group : 3 * group + 3]
            for inner in range(own.shape[0]):
                parts = [own[inner]]
                if tcol_count > 1:
                    parts = [own[inner], near[0, inner], far[inner], near[1, inner]]
                for j, part in enumerate(parts):
                    at = pl.multiple_of(jnp.bitwise_xor(me, j) * head_part, 16)
                    target[turn, pl.ds(at, head_part), :] = part[:head_part, :]
                rows[turn] = jnp.concatenate([part[head_part:, :] for part in parts], axis=0)
                turn += 1
        right = dot(rows[0, :piece, :], target[0], NT)
        for chunk in range(1, data_count):
            right += dot(rows[chunk, :piece, :], target[chunk], NT)
        right_ref[...] = right * (1.0 / total_rows)
        image_ref[...] = jnp.zeros_like(image_ref)

    at = pl.ds(pl.multiple_of(step * block, 128), block)
    column_side = dot(columns[0, at, :], target[0], NT)
    summed = dot(rows[0], columns[0, at, :], NT)
    for chunk in range(1, data_count):
        column_side += dot(columns[chunk, at, :], target[chunk], NT)
        summed += dot(rows[chunk], columns[chunk, at, :], NT)
    side = split(column_side * (1.0 / total_rows))
    summed = summed * (1.0 / total_rows)
    tile = []
    for j in range(tcol_count):
        place = pl.ds(pl.multiple_of(jnp.bitwise_xor(me, j) * piece, 8), piece)
        part = prior_ref[place, :] + summed[j * piece : (j + 1) * piece]
        gram_ref[place, :] = part
        tile.append(part)
    image_ref[...] += product(split(jnp.concatenate(tile, axis=0)), side)


def image_kernel(sizes, meta, *refs):
    n, data_count, tcol_count, piece, block = sizes
    shard_refs = refs[: n + 1]
    gram_ref, start_ref, near_ref, far_ref, penalty_ref, out_ref, sums_ref, high, low, total = refs[n + 1 :]
    step = pl.program_id(0)
    me = meta[2 * n]

    @pl.when(step == 0)
    def _():
        for index in range(n):
            base = pl.multiple_of((meta[n + index] * data_count + meta[index]) * piece, 8)
            if index < n - 1:
                parts = [(base, shard_refs[index][...])]
            else:
                half = shard_refs[n - 1].shape[0]
                parts = [(base, shard_refs[n - 1][...]), (base + half, shard_refs[n][...])]
            for start, value in parts:
                place = pl.ds(pl.multiple_of(start, 8), value.shape[0])
                high[place, :] = value.astype(jnp.bfloat16).astype(jnp.float32)
                low[place, :] = value - high[place, :]
        total[...] = jnp.zeros_like(total)

    at = pl.ds(pl.multiple_of(step * block, 128), block)
    side = high[at, :].astype(jnp.bfloat16), low[at, :].astype(jnp.bfloat16)
    total[...] += product(split(gram_ref[...]), side)

    @pl.when(step == pl.num_programs(0) - 1)
    def _():
        own = shard_refs[0][...]
        others = [own, near_ref[0], far_ref[...], near_ref[1]]
        late = jnp.zeros((1, own.shape[1]), jnp.float32)
        for j in range(tcol_count):
            place = pl.ds(pl.multiple_of(jnp.bitwise_xor(me, j) * piece, 8), piece)
            value = total[place, :]
            if j == 0:
                value = value + penalty_ref[...] * own
            out_ref[j] = value
            late = late + jnp.sum(value * others[j], axis=0, keepdims=True)
        start = start_ref[...]
        early = [jnp.sum(a * b, axis=0, keepdims=True) for a, b in ((start, start), (start, own), (own, own))]
        sums_ref[...] = jnp.concatenate(early + [late], axis=0)


def call(body, meta, inputs, grid, in_specs, out_specs, out_shape, scratch, flops, read):
    return pl.pallas_call(
        body,
        grid_spec=pltpu.PrefetchScalarGridSpec(
            num_scalar_prefetch=1,
            grid=(grid,),
            in_specs=in_specs,
            out_specs=out_specs,
            scratch_shapes=scratch,
        ),
        out_shape=out_shape,
        compiler_params=pltpu.CompilerParams(vmem_limit_bytes=VMEM_BYTES),
        cost_estimate=pl.CostEstimate(flops=flops, bytes_accessed=read, transcendentals=0),
    )(meta, *inputs)


def all_sum(value, axis_names):
    count = 1
    for name in axis_names:
        count *= lax.axis_size(name)
    spread = jnp.broadcast_to(value[None], (count,) + value.shape)
    return jnp.sum(lax.all_to_all(spread, axis_names, split_axis=0, concat_axis=0, tiled=True), axis=0)


def shards(embeddings, targets, gram_prior, penalty):
    row_count = embeddings.shape[0]
    width = embeddings.shape[3]
    heads = targets.shape[1]
    data_count = lax.axis_size("dp")
    trow_count = lax.axis_size("trow")
    tcol_count = lax.axis_size("tcol")
    piece = width // data_count
    total_rows = row_count * data_count
    tile_rows = tcol_count * piece
    tile_columns = trow_count * width
    head_part = heads // tcol_count
    data_place = lax.axis_index("dp")
    me = lax.axis_index("tcol")
    ring = Ring(data_count, trow_count)
    n = ring.count
    position = jnp.asarray(ring.place)[data_place, lax.axis_index("trow")]
    chunk_meta = jnp.asarray(ring.row_chunk)[position]
    trow_meta = jnp.asarray(ring.row_trow)[position]
    data_meta = jnp.asarray(ring.row_data)[position]
    rounds = jnp.asarray(ring.rounds)[position]
    me_meta = jnp.reshape(me, (1,)).astype(jnp.int32)

    own = embeddings.reshape(row_count, width).T
    head_rows = lax.dynamic_slice_in_dim(targets, me * head_part, head_part, axis=1).T
    gathered = ring.gather(jnp.concatenate([own, head_rows], axis=0), width)

    def piece_of(shard):
        features = lax.dynamic_slice_in_dim(shard, data_place * piece, piece, axis=0)
        return jnp.concatenate([shard[width:], features], axis=0)

    def round_piece(turn):
        choices = sorted(set(ring.rounds[:, turn].tolist()))
        value = piece_of(gathered[choices[0]])
        for choice in choices[1:]:
            value = jnp.where(rounds[turn] == choice, piece_of(gathered[choice]), value)
        return value

    split_turns = [[0], list(range(1, data_count - 1)), [data_count - 1]]
    groups = []
    for turns in split_turns:
        mine = jnp.stack([round_piece(turn) for turn in turns])
        far = lax.ppermute(mine, "tcol", swap(tcol_count, 2))
        near = lax.ppermute(jnp.stack([mine, far]), "tcol", swap(tcol_count, 1))
        groups += [mine, far, near]

    block = 384 if tile_columns % 384 == 0 else 128
    grid = tile_columns // block
    tile = pl.BlockSpec((tile_rows, block), lambda i, meta: (0, i))

    def whole(*shape):
        return pl.BlockSpec(shape, lambda i, meta: (0,) * len(shape))

    f32, bf16 = jnp.float32, jnp.bfloat16
    gram, start, partial = call(
        functools.partial(
            gram_kernel,
            (n, data_count, trow_count, tcol_count, piece, width, head_part, block, total_rows, len(split_turns)),
        ),
        jnp.concatenate([chunk_meta, trow_meta, me_meta]),
        [*gathered, *groups, gram_prior.reshape(tile_rows, tile_columns)],
        grid,
        [VMEM] * (n + 1 + len(groups)) + [tile],
        [tile, whole(piece, heads), whole(tile_rows, heads)],
        [
            jax.ShapeDtypeStruct((tile_rows, tile_columns), f32),
            jax.ShapeDtypeStruct((piece, heads), f32),
            jax.ShapeDtypeStruct((tile_rows, heads), f32),
        ],
        [
            pltpu.VMEM((data_count, tile_columns, row_count), bf16),
            pltpu.VMEM((data_count, tile_rows, row_count), bf16),
            pltpu.VMEM((data_count, heads, row_count), bf16),
        ],
        2 * tile_rows * tile_columns * (total_rows + 3 * heads),
        8 * tile_rows * tile_columns,
    )
    penalty_rows = penalty.reshape(piece, 1)

    def owner_sum(value):
        kept = [value[j] for j in range(tcol_count)]
        received = lax.ppermute(jnp.stack(kept[1::2]), "tcol", swap(tcol_count, 1))
        kept = [a + received[i] for i, a in enumerate(kept[0::2])]
        return kept[0] + lax.ppermute(kept[1], "tcol", swap(tcol_count, 2))

    image = owner_sum(partial.reshape(tcol_count, piece, heads)) + penalty_rows * start
    far_image = lax.ppermute(image, "tcol", swap(tcol_count, 2))
    near_images = lax.ppermute(jnp.stack([image, far_image]), "tcol", swap(tcol_count, 1))
    images = ring.gather(image, piece)
    second, sums = call(
        functools.partial(image_kernel, (n, data_count, tcol_count, piece, block)),
        jnp.concatenate([data_meta, trow_meta, me_meta]),
        [*images, gram, start, near_images, far_image, penalty_rows],
        grid,
        [VMEM] * (n + 1) + [tile] + [VMEM] * 4,
        [whole(tcol_count, piece, heads), whole(4, heads)],
        [jax.ShapeDtypeStruct((tcol_count, piece, heads), f32), jax.ShapeDtypeStruct((4, heads), f32)],
        [
            pltpu.VMEM((tile_columns, heads), f32),
            pltpu.VMEM((tile_columns, heads), f32),
            pltpu.VMEM((tile_rows, heads), f32),
        ],
        6 * tile_rows * tile_columns * heads,
        4 * tile_rows * tile_columns,
    )
    sums = all_sum(sums, ("dp", "trow", "tcol"))
    second = owner_sum(second)

    norm, curvature, image_norm, image_curvature = sums[0], sums[1], sums[2], sums[3]
    step = norm / curvature
    norm_next = step * step * image_norm - norm
    ratio = norm_next / norm
    moved_curvature = step * (step * image_curvature - (1.0 + ratio) * image_norm)
    next_step = norm_next / moved_curvature
    residual = start - step * image
    direction = residual + ratio * start
    weights = step * start + next_step * direction
    residual = residual - next_step * ((1.0 + ratio) * image - step * second)
    out_shape = (1, 1, 1, piece, heads)
    return (gram.reshape(gram_prior.shape), weights.reshape(out_shape), residual.reshape(out_shape))


def solution(mesh):
    placed = (
        P("dp", "tcol", "trow", None),
        P("dp", None),
        P(None, "trow", "dp", None, "tcol"),
        P("tcol", "trow", "dp", None),
    )
    return jax.shard_map(
        shards,
        mesh=mesh,
        in_specs=placed,
        out_specs=(
            P(None, "trow", "dp", None, "tcol"),
            P("tcol", "trow", "dp", None, None),
            P("tcol", "trow", "dp", None, None),
        ),
        check_vma=False,
    )
```

```python
import functools

import jax
import jax.numpy as jnp
import numpy as np
from jax import lax
from jax.experimental import pallas as pl
from jax.experimental.pallas import tpu as pltpu
from jax.sharding import PartitionSpec as P

NT = (((1,), (1,)), ((), ()))
NN = (((1,), (0,)), ((), ()))
VMEM = pl.BlockSpec(memory_space=pltpu.VMEM)
HBM = pl.BlockSpec(memory_space=pltpu.HBM)
GRAM_BYTES = 24 * 2**20
IMAGE_BYTES = 20 * 2**20


def swap(count, bit):
    return [(place, place ^ bit) for place in range(count)]


class Ring:
    def __init__(self, data_count, trow_count):
        self.data_count = data_count
        self.count = data_count * trow_count
        self.cells = []
        for trow in range(trow_count):
            along = range(data_count) if trow % 2 == 0 else reversed(range(data_count))
            self.cells += [(data, trow) for data in along]
        flat = [data * trow_count + trow for data, trow in self.cells]
        self.ahead = [(flat[i], flat[(i + 1) % self.count]) for i in range(self.count)]
        self.back = [(target, source) for source, target in self.ahead]
        self.far = self.count // 2
        self.offsets = [0]
        for distance in range(1, self.far):
            self.offsets += [-distance, distance]
        self.offsets.append(self.far)
        self.place = np.zeros((data_count, trow_count), np.int32)
        for position, (data, trow) in enumerate(self.cells):
            self.place[data, trow] = position
        self.rounds = np.zeros((self.count, data_count), np.int32)
        self.chunk, self.trow, self.data = (np.zeros((self.count, self.count), np.int32) for _ in range(3))
        for position, (data, trow) in enumerate(self.cells):
            first = trow * data_count
            near = sorted(range(first, first + data_count), key=lambda q: (abs(q - position), q))
            chunk_of = {}
            for turn, other in enumerate(near):
                self.rounds[position, turn] = self.offsets.index(other - position)
                chunk_of[self.cells[other][0]] = turn
            for index, offset in enumerate(self.offsets):
                other_data, other_trow = self.cells[(position + offset) % self.count]
                self.chunk[position, index] = chunk_of[other_data]
                self.trow[position, index] = other_trow
                self.data[position, index] = other_data

    def steps(self, value, split_rows):
        ahead = back = value
        for _ in range(1, self.far):
            ahead = lax.ppermute(ahead, ("dp", "trow"), self.ahead)
            back = lax.ppermute(back, ("dp", "trow"), self.back)
            yield ahead, back
        half = (split_rows // 2 + 15) // 16 * 16
        low = lax.ppermute(ahead[:half], ("dp", "trow"), self.ahead)
        high = lax.ppermute(back[half:split_rows], ("dp", "trow"), self.back)
        yield low, high


def split(value):
    high = value.astype(jnp.bfloat16)
    return high, (value - high.astype(jnp.float32)).astype(jnp.bfloat16)


def dot(a, b, dims):
    return lax.dot_general(a, b, dims, preferred_element_type=jnp.float32)


def product(a, b):
    (a_high, a_low), (b_high, b_low) = a, b
    return dot(a_high, b_high, NN) + (dot(a_high, b_low, NN) + dot(a_low, b_high, NN))


def tile_copies(whole_ref, tile_ref, me, piece, block, semaphores, outward=False):
    copies = []
    for start in range(0, tile_ref.shape[1], block):
        lanes = pl.ds(start, block)
        for j in range(tile_ref.shape[0] // piece):
            place = pl.ds(pl.multiple_of(jnp.bitwise_xor(me, j) * piece, 8), piece)
            pair = whole_ref.at[place, lanes], tile_ref.at[pl.ds(j * piece, piece), lanes]
            if outward:
                pair = pair[::-1]
            copies.append(pltpu.make_async_copy(*pair, semaphores.at[len(copies)]))
    return copies


def fetch_kernel(sizes, meta, gram_ref, tile_ref, come):
    piece, block = sizes
    loads = tile_copies(gram_ref, tile_ref, meta[0], piece, block, come)
    for load in loads:
        load.start()
    for load in loads:
        load.wait()


def gram_kernel(sizes, meta, *refs):
    n, tcol_count, piece, width, head_part, block, groups = sizes
    shard_refs = refs[: n + 1]
    round_refs = refs[n + 1 : n + 1 + 3 * groups]
    prior_ref, gram_ref, right_ref, image_ref, columns, rows, target, tile_ref, sent = refs[n + 1 + 3 * groups :]
    me = meta[2 * n]
    total_rows = rows.shape[1]
    count = shard_refs[0].shape[1]
    for index in range(n):
        lanes = pl.ds(pl.multiple_of(meta[index] * count, 128), count)
        base = pl.multiple_of(meta[n + index] * width, 16)
        if index < n - 1:
            columns[pl.ds(base, width), lanes] = shard_refs[index][:width, :]
        else:
            half = shard_refs[n - 1].shape[0]
            columns[pl.ds(base, half), lanes] = shard_refs[n - 1][...]
            columns[pl.ds(pl.multiple_of(base + half, 16), width - half), lanes] = shard_refs[n][...]
    turn = 0
    for group in range(groups):
        own, far, near = round_refs[3 * group : 3 * group + 3]
        for inner in range(own.shape[0]):
            lanes = slice(turn * count, (turn + 1) * count)
            parts = [own[inner], near[0, inner], far[inner], near[1, inner]]
            for j, part in enumerate(parts):
                at = pl.multiple_of(jnp.bitwise_xor(me, j) * head_part, 16)
                target[pl.ds(at, head_part), lanes] = part[:head_part, :]
            rows[:, lanes] = jnp.concatenate([part[head_part:, :] for part in parts], axis=0)
            turn += 1
    scale = 1.0 / total_rows
    stores = tile_copies(gram_ref, tile_ref, me, piece, block, sent, outward=True)
    sides = []
    for step in range(columns.shape[0] // block):
        lanes = slice(step * block, (step + 1) * block)
        column = columns[lanes, :]
        summed = dot(rows[...], column, NT)
        tile_ref[:, lanes] = prior_ref[:, lanes] + summed * scale
        for index in range(step * tcol_count, (step + 1) * tcol_count):
            stores[index].start()
        sides.append(split(dot(column, target[...], NT) * scale))
    right_ref[...] = dot(rows[:piece, :], target[...], NT) * scale
    side = [jnp.concatenate(part, axis=0) for part in zip(*sides)]
    image_ref[...] = product(split(tile_ref[...]), side)
    for store in stores:
        store.wait()


def image_kernel(sizes, meta, *refs):
    n, data_count, tcol_count, piece = sizes
    shard_refs = refs[: n + 1]
    tile_ref, start_ref, near_ref, far_ref, penalty_ref, out_ref, sums_ref, side = refs[n + 1 :]
    for index in range(n):
        base = pl.multiple_of((meta[n + index] * data_count + meta[index]) * piece, 8)
        if index < n - 1:
            side[pl.ds(base, piece), :] = shard_refs[index][...]
        else:
            half = shard_refs[n - 1].shape[0]
            side[pl.ds(base, half), :] = shard_refs[n - 1][...]
            side[pl.ds(pl.multiple_of(base + half, 8), piece - half), :] = shard_refs[n][...]
    total = product(split(tile_ref[...]), split(side[...]))
    own = shard_refs[0][...]
    others = [own, near_ref[0], far_ref[...], near_ref[1]]
    late = jnp.zeros((1, own.shape[1]), jnp.float32)
    for j in range(tcol_count):
        value = total[j * piece : (j + 1) * piece]
        if j == 0:
            value = value + penalty_ref[...] * own
        out_ref[j] = value
        late = late + jnp.sum(value * others[j], axis=0, keepdims=True)
    start = start_ref[...]
    early = [jnp.sum(a * b, axis=0, keepdims=True) for a, b in ((start, start), (start, own), (own, own))]
    sums_ref[...] = jnp.concatenate(early + [late], axis=0)


def call(body, meta, inputs, in_specs, out_specs, out_shape, scratch, vmem, flops, read):
    return pl.pallas_call(
        body,
        grid_spec=pltpu.PrefetchScalarGridSpec(
            num_scalar_prefetch=1,
            grid=(1,),
            in_specs=in_specs,
            out_specs=out_specs,
            scratch_shapes=scratch,
        ),
        out_shape=out_shape,
        compiler_params=pltpu.CompilerParams(vmem_limit_bytes=vmem),
        cost_estimate=pl.CostEstimate(flops=flops, bytes_accessed=read, transcendentals=0),
    )(meta, *inputs)


def all_sum(value, axis_names):
    count = 1
    for name in axis_names:
        count *= lax.axis_size(name)
    spread = jnp.broadcast_to(value[None], (count,) + value.shape)
    return jnp.sum(lax.all_to_all(spread, axis_names, split_axis=0, concat_axis=0, tiled=True), axis=0)


def shards(embeddings, targets, gram_prior, penalty):
    row_count = embeddings.shape[0]
    width = embeddings.shape[3]
    heads = targets.shape[1]
    data_count = lax.axis_size("dp")
    trow_count = lax.axis_size("trow")
    tcol_count = lax.axis_size("tcol")
    piece = width // data_count
    total_rows = row_count * data_count
    tile_rows = tcol_count * piece
    tile_columns = trow_count * width
    head_part = heads // tcol_count
    data_place = lax.axis_index("dp")
    me = lax.axis_index("tcol")
    ring = Ring(data_count, trow_count)
    n = ring.count
    position = jnp.asarray(ring.place)[data_place, lax.axis_index("trow")]
    lookup = np.concatenate([ring.rounds, ring.chunk, ring.trow, ring.data, ring.trow], axis=1)
    lookup = jnp.asarray(lookup)[position]
    rounds = [lookup[turn] for turn in range(data_count)]
    me_meta = jnp.reshape(me, (1,)).astype(jnp.int32)
    gram_meta = jnp.concatenate([lookup[data_count : data_count + 2 * n], me_meta])
    image_meta = jnp.concatenate([lookup[data_count + 2 * n :], me_meta])

    own = embeddings.reshape(row_count, width).T
    head_rows = lax.dynamic_slice_in_dim(targets, me * head_part, head_part, axis=1).T
    payload = jnp.concatenate([own, head_rows], axis=0)

    def piece_of(shard):
        features = lax.dynamic_slice_in_dim(shard, data_place * piece, piece, axis=0)
        return jnp.concatenate([shard[width:], features], axis=0)

    def round_piece(turn):
        choices = sorted(set(ring.rounds[:, turn].tolist()))
        value = piece_of(gathered[choices[0]])
        for choice in choices[1:]:
            value = jnp.where(rounds[turn] == choice, piece_of(gathered[choice]), value)
        return value

    split_turns = [[0], list(range(1, data_count - 1)), [data_count - 1]]
    ready = [int(np.abs(np.asarray(ring.offsets)[ring.rounds[:, turns]]).max()) for turns in split_turns]
    gathered, groups, waiting = [payload], [], []

    def near_of(mine, far, *after):
        mine, far, *after = lax.optimization_barrier((mine, far, *after))
        groups.extend([mine, far, lax.ppermute(jnp.stack([mine, far]), "tcol", swap(tcol_count, 1))])
        return after

    def open_groups(step):
        for turns, when in zip(split_turns, ready):
            if when == step:
                mine = jnp.stack([round_piece(turn) for turn in turns])
                waiting.append((mine, lax.ppermute(mine, "tcol", swap(tcol_count, 2))))

    block = 384 if tile_columns % 384 == 0 else 128
    f32, bf16 = jnp.float32, jnp.bfloat16
    tile_semaphores = pltpu.SemaphoreType.DMA((tcol_count * (tile_columns // block),))

    def fetch(whole):
        return call(
            functools.partial(fetch_kernel, (piece, block)),
            me_meta,
            [whole],
            [HBM],
            VMEM,
            jax.ShapeDtypeStruct((tile_rows, tile_columns), f32),
            [tile_semaphores],
            2**20,
            0,
            8 * tile_rows * tile_columns,
        )

    prior = gram_prior.reshape(tile_rows, tile_columns)
    open_groups(0)
    for step, arrived in enumerate(ring.steps(payload, width), 1):
        arrived = list(arrived)
        if step == 1:
            gram_meta, image_meta, rounds, arrived = lax.optimization_barrier(
                (gram_meta, image_meta, rounds, arrived)
            )
        if step == ring.far - 2:
            prior, *arrived = lax.optimization_barrier((prior, *arrived))
            prior = fetch(prior)
        if step == ring.far - 1:
            prior, *arrived = lax.optimization_barrier((prior, *arrived))
        while waiting:
            arrived = near_of(*waiting.pop(), *arrived)
        gathered += arrived
        open_groups(step)

    gram, start, partial = call(
        functools.partial(
            gram_kernel, (n, tcol_count, piece, width, head_part, block, len(split_turns))
        ),
        gram_meta,
        [*gathered, *groups, prior],
        [VMEM] * (n + 2 + len(groups)),
        [HBM] + [VMEM] * 2,
        [
            jax.ShapeDtypeStruct((tile_rows, tile_columns), f32),
            jax.ShapeDtypeStruct((piece, heads), f32),
            jax.ShapeDtypeStruct((tile_rows, heads), f32),
        ],
        [
            pltpu.VMEM((tile_columns, total_rows), bf16),
            pltpu.VMEM((tile_rows, total_rows), bf16),
            pltpu.VMEM((heads, total_rows), bf16),
            pltpu.VMEM((tile_rows, tile_columns), f32),
            tile_semaphores,
        ],
        GRAM_BYTES,
        2 * tile_rows * tile_columns * (total_rows + 3 * heads),
        12 * tile_rows * tile_columns,
    )
    penalty_rows = penalty.reshape(piece, 1)

    def owner_sum(value, beside=None):
        kept = [value[j] for j in range(tcol_count)]
        received = lax.ppermute(jnp.stack(kept[1::2]), "tcol", swap(tcol_count, 1))
        if beside is not None:
            received, beside = lax.optimization_barrier((received, beside))
        kept = [a + received[i] for i, a in enumerate(kept[0::2])]
        return kept[0] + lax.ppermute(kept[1], "tcol", swap(tcol_count, 2)), beside

    image = owner_sum(partial.reshape(tcol_count, piece, heads))[0] + penalty_rows * start
    far_image = lax.ppermute(image, "tcol", swap(tcol_count, 2))
    near_images = lax.ppermute(jnp.stack([image, far_image]), "tcol", swap(tcol_count, 1))
    images = [image]
    for step, arrived in enumerate(ring.steps(image, piece), 1):
        if step == ring.far - 1:
            arrived = lax.optimization_barrier((*arrived, gram))
            gram = arrived[2]
            tile = fetch(gram)
        images += arrived[:2]
    second, sums = call(
        functools.partial(image_kernel, (n, data_count, tcol_count, piece)),
        image_meta,
        [*images, tile, start, near_images, far_image, penalty_rows],
        [VMEM] * (n + 6),
        [VMEM] * 2,
        [jax.ShapeDtypeStruct((tcol_count, piece, heads), f32), jax.ShapeDtypeStruct((4, heads), f32)],
        [pltpu.VMEM((tile_columns, heads), f32)],
        IMAGE_BYTES,
        6 * tile_rows * tile_columns * heads,
        4 * tile_rows * tile_columns,
    )
    second, sums = owner_sum(second, sums)
    sums = all_sum(sums, ("dp", "trow", "tcol"))

    norm, curvature, image_norm, image_curvature = sums[0], sums[1], sums[2], sums[3]
    step = norm / curvature
    norm_next = step * step * image_norm - norm
    ratio = norm_next / norm
    moved_curvature = step * (step * image_curvature - (1.0 + ratio) * image_norm)
    next_step = norm_next / moved_curvature
    residual = start - step * image
    direction = residual + ratio * start
    weights = step * start + next_step * direction
    residual = residual - next_step * ((1.0 + ratio) * image - step * second)
    out_shape = (1, 1, 1, piece, heads)
    return (gram.reshape(gram_prior.shape), weights.reshape(out_shape), residual.reshape(out_shape))


def solution(mesh):
    placed = (
        P("dp", "tcol", "trow", None),
        P("dp", None),
        P(None, "trow", "dp", None, "tcol"),
        P("tcol", "trow", "dp", None),
    )
    return jax.shard_map(
        shards,
        mesh=mesh,
        in_specs=placed,
        out_specs=(
            P(None, "trow", "dp", None, "tcol"),
            P("tcol", "trow", "dp", None, None),
            P("tcol", "trow", "dp", None, None),
        ),
        check_vma=False,
    )
```

```python
import functools

import jax
import jax.numpy as jnp
import numpy as np
from jax import lax
from jax.experimental import pallas as pl
from jax.experimental.pallas import tpu as pltpu
from jax.sharding import PartitionSpec as P

NT = (((1,), (1,)), ((), ()))
NN = (((1,), (0,)), ((), ()))
VMEM = pl.BlockSpec(memory_space=pltpu.VMEM)
HBM = pl.BlockSpec(memory_space=pltpu.HBM)
EARLY_BYTES = 12 * 2**20
GRAM_BYTES = 24 * 2**20
IMAGE_BYTES = 20 * 2**20


def swap(count, bit):
    return [(place, place ^ bit) for place in range(count)]


class Ring:
    def __init__(self, data_count, trow_count):
        self.data_count = data_count
        self.count = data_count * trow_count
        self.cells = []
        for trow in range(trow_count):
            along = range(data_count) if trow % 2 == 0 else reversed(range(data_count))
            self.cells += [(data, trow) for data in along]
        flat = [data * trow_count + trow for data, trow in self.cells]
        self.ahead = [(flat[i], flat[(i + 1) % self.count]) for i in range(self.count)]
        self.back = [(target, source) for source, target in self.ahead]
        self.far = self.count // 2
        self.offsets = [0]
        for distance in range(1, self.far):
            self.offsets += [-distance, distance]
        self.offsets.append(self.far)
        self.place = np.zeros((data_count, trow_count), np.int32)
        for position, (data, trow) in enumerate(self.cells):
            self.place[data, trow] = position
        self.rounds = np.zeros((self.count, data_count), np.int32)
        self.chunk, self.trow, self.data = (np.zeros((self.count, self.count), np.int32) for _ in range(3))
        for position, (data, trow) in enumerate(self.cells):
            first = trow * data_count
            far_data = self.cells[(position + self.far) % self.count][0]
            near = sorted(
                range(first, first + data_count),
                key=lambda q: (self.cells[q][0] == far_data, abs(q - position), q),
            )
            chunk_of = {}
            for turn, other in enumerate(near):
                self.rounds[position, turn] = self.offsets.index(other - position)
                chunk_of[self.cells[other][0]] = turn
            for index, offset in enumerate(self.offsets):
                other_data, other_trow = self.cells[(position + offset) % self.count]
                self.chunk[position, index] = chunk_of[other_data]
                self.trow[position, index] = other_trow
                self.data[position, index] = other_data

    def steps(self, value, split_rows):
        ahead = back = value
        for _ in range(1, self.far):
            ahead = lax.ppermute(ahead, ("dp", "trow"), self.ahead)
            back = lax.ppermute(back, ("dp", "trow"), self.back)
            yield ahead, back
        half = (split_rows // 2 + 15) // 16 * 16
        low = lax.ppermute(ahead[:half], ("dp", "trow"), self.ahead)
        high = lax.ppermute(back[half:split_rows], ("dp", "trow"), self.back)
        yield low, high


def split(value):
    high = value.astype(jnp.bfloat16)
    return high, (value - high.astype(jnp.float32)).astype(jnp.bfloat16)


def dot(a, b, dims):
    return lax.dot_general(a, b, dims, preferred_element_type=jnp.float32)


def product(a, b):
    (a_high, a_low), (b_high, b_low) = a, b
    return dot(a_high, b_high, NN) + (dot(a_high, b_low, NN) + dot(a_low, b_high, NN))


def tile_copies(whole_ref, tile_ref, me, piece, block, semaphores, outward=False):
    copies = []
    for start in range(0, tile_ref.shape[1], block):
        lanes = pl.ds(start, block)
        for j in range(tile_ref.shape[0] // piece):
            place = pl.ds(pl.multiple_of(jnp.bitwise_xor(me, j) * piece, 8), piece)
            pair = whole_ref.at[place, lanes], tile_ref.at[pl.ds(j * piece, piece), lanes]
            if outward:
                pair = pair[::-1]
            copies.append(pltpu.make_async_copy(*pair, semaphores.at[len(copies)]))
    return copies


def fetch_kernel(sizes, meta, gram_ref, tile_ref, come):
    piece, block = sizes
    loads = tile_copies(gram_ref, tile_ref, meta[0], piece, block, come)
    for load in loads:
        load.start()
    for load in loads:
        load.wait()


def pick_kernel(sizes, meta, *refs):
    turns, choices, width, piece, data_count = sizes
    *shard_refs, out_ref = refs
    head_part = shard_refs[0].shape[0] - width
    for index, turn in enumerate(turns):
        for shard_ref, choice in zip(shard_refs, choices):

            @pl.when(meta[turn] == choice)
            def _():
                out_ref[index, :head_part, :] = shard_ref[width:, :]
                if piece % 16 == 0:
                    place = pl.ds(pl.multiple_of(meta[data_count] * piece, 16), piece)
                    out_ref[index, head_part:, :] = shard_ref[place, :]
                else:
                    for data in range(data_count):

                        @pl.when(meta[data_count] == data)
                        def _():
                            out_ref[index, head_part:, :] = shard_ref[data * piece : (data + 1) * piece, :]


def place_rows(round_refs, me, head_part, rows, target, turn, count):
    for group in range(len(round_refs) // 3):
        own, far, near = round_refs[3 * group : 3 * group + 3]
        for inner in range(own.shape[0]):
            lanes = slice(turn * count, (turn + 1) * count)
            parts = [own[inner], near[0, inner], far[inner], near[1, inner]]
            for j, part in enumerate(parts):
                at = pl.multiple_of(jnp.bitwise_xor(me, j) * head_part, 16)
                target[pl.ds(at, head_part), lanes] = part[:head_part, :]
            rows[:, lanes] = jnp.concatenate([part[head_part:, :] for part in parts], axis=0)
            turn += 1


def early_kernel(sizes, meta, *refs):
    n, width, head_part, block, groups = sizes
    shard_refs, refs = refs[: n - 1], refs[n - 1 :]
    round_refs, refs = refs[: 3 * groups], refs[3 * groups :]
    prior_ref, tile_ref, columns, rows, target = refs
    count = shard_refs[0].shape[1]
    for index in range(n - 1):
        lanes = pl.ds(pl.multiple_of(meta[index] * count, 128), count)
        base = pl.multiple_of(meta[n + index] * width, 16)
        columns[pl.ds(base, width), lanes] = shard_refs[index][:width, :]
    place_rows(round_refs, meta[2 * n], head_part, rows, target, 0, count)
    done = columns.shape[1] - count
    scale = 1.0 / columns.shape[1]
    for start in range(0, columns.shape[0], block):
        lanes = slice(start, start + block)
        tile_ref[:, lanes] = prior_ref[:, lanes] + dot(rows[:, :done], columns[lanes, :done], NT) * scale


def gram_kernel(sizes, meta, *refs):
    n, tcol_count, piece, width, head_part, block = sizes
    low_ref, high_ref, *round_refs = refs[:5]
    early_ref, columns, rows, target, gram_ref, right_ref, image_ref = refs[5:12]
    last_columns, last_rows, last_target, tile_ref, sent = refs[12:]
    me = meta[2 * n]
    total_rows = columns.shape[1]
    count = last_rows.shape[1]
    done = total_rows - count
    last_columns[...] = columns[:, done:]
    base = pl.multiple_of(meta[2 * n - 1] * width, 16)
    half = low_ref.shape[0]
    last_columns[pl.ds(base, half), :] = low_ref[...]
    last_columns[pl.ds(pl.multiple_of(base + half, 16), width - half), :] = high_ref[...]
    place_rows(round_refs, me, head_part, last_rows, last_target, 0, count)
    scale = 1.0 / total_rows
    stores = tile_copies(gram_ref, tile_ref, me, piece, block, sent, outward=True)
    sides = []
    for step in range(columns.shape[0] // block):
        lanes = slice(step * block, (step + 1) * block)
        last = last_columns[lanes, :]
        tile_ref[:, lanes] = early_ref[:, lanes] + dot(last_rows[...], last, NT) * scale
        for index in range(step * tcol_count, (step + 1) * tcol_count):
            stores[index].start()
        side = dot(columns[lanes, :done], target[:, :done], NT) + dot(last, last_target[...], NT)
        sides.append(split(side * scale))
    right = dot(rows[:piece, :done], target[:, :done], NT) + dot(last_rows[:piece, :], last_target[...], NT)
    right_ref[...] = right * scale
    side = [jnp.concatenate(part, axis=0) for part in zip(*sides)]
    image_ref[...] = product(split(tile_ref[...]), side)
    for store in stores:
        store.wait()


def image_kernel(sizes, meta, *refs):
    n, data_count, tcol_count, piece = sizes
    shard_refs = refs[: n + 1]
    tile_ref, start_ref, near_ref, far_ref, penalty_ref, out_ref, sums_ref, side = refs[n + 1 :]
    for index in range(n):
        base = pl.multiple_of((meta[n + index] * data_count + meta[index]) * piece, 8)
        if index < n - 1:
            side[pl.ds(base, piece), :] = shard_refs[index][...]
        else:
            half = shard_refs[n - 1].shape[0]
            side[pl.ds(base, half), :] = shard_refs[n - 1][...]
            side[pl.ds(pl.multiple_of(base + half, 8), piece - half), :] = shard_refs[n][...]
    total = product(split(tile_ref[...]), split(side[...]))
    own = shard_refs[0][...]
    others = [own, near_ref[0], far_ref[...], near_ref[1]]
    late = jnp.zeros((1, own.shape[1]), jnp.float32)
    for j in range(tcol_count):
        value = total[j * piece : (j + 1) * piece]
        if j == 0:
            value = value + penalty_ref[...] * own
        out_ref[j] = value
        late = late + jnp.sum(value * others[j], axis=0, keepdims=True)
    start = start_ref[...]
    early = [jnp.sum(a * b, axis=0, keepdims=True) for a, b in ((start, start), (start, own), (own, own))]
    sums_ref[...] = jnp.concatenate(early + [late], axis=0)


def call(body, meta, inputs, in_specs, out_specs, out_shape, scratch, vmem, flops, read):
    return pl.pallas_call(
        body,
        grid_spec=pltpu.PrefetchScalarGridSpec(
            num_scalar_prefetch=1,
            grid=(1,),
            in_specs=in_specs,
            out_specs=out_specs,
            scratch_shapes=scratch,
        ),
        out_shape=out_shape,
        compiler_params=pltpu.CompilerParams(vmem_limit_bytes=vmem),
        cost_estimate=pl.CostEstimate(flops=flops, bytes_accessed=read, transcendentals=0),
    )(meta, *inputs)


def all_sum(value, axis_names):
    count = 1
    for name in axis_names:
        count *= lax.axis_size(name)
    spread = jnp.broadcast_to(value[None], (count,) + value.shape)
    return jnp.sum(lax.all_to_all(spread, axis_names, split_axis=0, concat_axis=0, tiled=True), axis=0)


def shards(embeddings, targets, gram_prior, penalty):
    row_count = embeddings.shape[0]
    width = embeddings.shape[3]
    heads = targets.shape[1]
    data_count = lax.axis_size("dp")
    trow_count = lax.axis_size("trow")
    tcol_count = lax.axis_size("tcol")
    piece = width // data_count
    total_rows = row_count * data_count
    tile_rows = tcol_count * piece
    tile_columns = trow_count * width
    head_part = heads // tcol_count
    data_place = lax.axis_index("dp")
    me = lax.axis_index("tcol")
    ring = Ring(data_count, trow_count)
    n = ring.count
    position = jnp.asarray(ring.place)[data_place, lax.axis_index("trow")]
    lookup = np.concatenate([ring.rounds, ring.chunk, ring.trow, ring.data, ring.trow], axis=1)
    lookup = jnp.asarray(lookup)[position]
    pick_meta = jnp.concatenate([lookup[:data_count], jnp.reshape(data_place, (1,)).astype(jnp.int32)])
    me_meta = jnp.reshape(me, (1,)).astype(jnp.int32)
    gram_meta = jnp.concatenate([lookup[data_count : data_count + 2 * n], me_meta])
    image_meta = jnp.concatenate([lookup[data_count + 2 * n :], me_meta])

    own = embeddings.reshape(row_count, width).T
    head_rows = lax.dynamic_slice_in_dim(targets, me * head_part, head_part, axis=1).T
    payload = jnp.concatenate([own, head_rows], axis=0)

    def pieces_of(turns):
        if turns == [0]:
            features = lax.dynamic_slice_in_dim(own, data_place * piece, piece, axis=0)
            return jnp.concatenate([head_rows, features], axis=0)[None]
        choices = sorted(set(ring.rounds[:, turns].ravel().tolist()))
        return call(
            functools.partial(pick_kernel, (turns, choices, width, piece, data_count)),
            pick_meta,
            [gathered[choice] for choice in choices],
            [VMEM] * len(choices),
            VMEM,
            jax.ShapeDtypeStruct((len(turns), head_part + piece, row_count), payload.dtype),
            [],
            2**20,
            0,
            4 * len(turns) * (head_part + piece) * row_count,
        )

    split_turns = [[0], list(range(1, data_count - 1)), [data_count - 1]]
    ready = [int(np.abs(np.asarray(ring.offsets)[ring.rounds[:, turns]]).max()) for turns in split_turns]
    gathered, groups, waiting = [payload], {}, []

    def near_of(group, mine, far):
        groups[group] = [mine, far, lax.ppermute(jnp.stack([mine, far]), "tcol", swap(tcol_count, 1))]

    def open_groups(step):
        for group, (turns, when) in enumerate(zip(split_turns, ready)):
            if when == step:
                mine = pieces_of(turns)
                waiting.append((group, mine, lax.ppermute(mine, "tcol", swap(tcol_count, 2))))

    block = 384 if tile_columns % 384 == 0 else 128
    f32, bf16 = jnp.float32, jnp.bfloat16
    tile_semaphores = pltpu.SemaphoreType.DMA((tcol_count * (tile_columns // block),))

    def fetch(whole):
        return call(
            functools.partial(fetch_kernel, (piece, block)),
            me_meta,
            [whole],
            [HBM],
            VMEM,
            jax.ShapeDtypeStruct((tile_rows, tile_columns), f32),
            [tile_semaphores],
            2**20,
            0,
            8 * tile_rows * tile_columns,
        )

    prior = gram_prior.reshape(tile_rows, tile_columns)
    open_groups(0)
    for step, arrived in enumerate(ring.steps(payload, width), 1):
        arrived = list(arrived)
        if step == 1:
            gram_meta, image_meta, pick_meta, *arrived = lax.optimization_barrier(
                (gram_meta, image_meta, pick_meta, *arrived)
            )
        if step == ring.far - 2:
            prior, *arrived = lax.optimization_barrier((prior, *arrived))
            prior = fetch(prior)
        if step == ring.far - 1:
            prior, *arrived = lax.optimization_barrier((prior, *arrived))
        while waiting:
            group, mine, far = waiting.pop()
            if step == ring.far:
                early, mine, far, *arrived = lax.optimization_barrier((early, mine, far, *arrived))
            else:
                mine, far, *arrived = lax.optimization_barrier((mine, far, *arrived))
            near_of(group, mine, far)
        gathered += arrived
        open_groups(step)
        if step == ring.far - 1:
            early, columns, rows, target = call(
                functools.partial(early_kernel, (n, width, head_part, block, 2)),
                gram_meta,
                [*gathered, *groups[0], *groups[1], prior],
                [VMEM] * (n + 6),
                [VMEM] * 4,
                [
                    jax.ShapeDtypeStruct((tile_rows, tile_columns), f32),
                    jax.ShapeDtypeStruct((tile_columns, total_rows), bf16),
                    jax.ShapeDtypeStruct((tile_rows, total_rows), bf16),
                    jax.ShapeDtypeStruct((heads, total_rows), bf16),
                ],
                [],
                EARLY_BYTES,
                2 * tile_rows * tile_columns * (total_rows - row_count),
                8 * tile_rows * tile_columns,
            )
    gram, start, partial = call(
        functools.partial(gram_kernel, (n, tcol_count, piece, width, head_part, block)),
        gram_meta,
        [*gathered[-2:], *groups[2], early, columns, rows, target],
        [VMEM] * 9,
        [HBM] + [VMEM] * 2,
        [
            jax.ShapeDtypeStruct((tile_rows, tile_columns), f32),
            jax.ShapeDtypeStruct((piece, heads), f32),
            jax.ShapeDtypeStruct((tile_rows, heads), f32),
        ],
        [
            pltpu.VMEM((tile_columns, row_count), bf16),
            pltpu.VMEM((tile_rows, row_count), bf16),
            pltpu.VMEM((heads, row_count), bf16),
            pltpu.VMEM((tile_rows, tile_columns), f32),
            tile_semaphores,
        ],
        GRAM_BYTES,
        2 * tile_rows * tile_columns * (total_rows + 3 * heads),
        12 * tile_rows * tile_columns,
    )
    penalty_rows = penalty.reshape(piece, 1)

    def owner_sum(value, beside=None):
        kept = [value[j] for j in range(tcol_count)]
        received = lax.ppermute(jnp.stack(kept[1::2]), "tcol", swap(tcol_count, 1))
        if beside is not None:
            received, beside = lax.optimization_barrier((received, beside))
        kept = [a + received[i] for i, a in enumerate(kept[0::2])]
        return kept[0] + lax.ppermute(kept[1], "tcol", swap(tcol_count, 2)), beside

    image = owner_sum(partial.reshape(tcol_count, piece, heads))[0] + penalty_rows * start
    far_image = lax.ppermute(image, "tcol", swap(tcol_count, 2))
    near_images = lax.ppermute(jnp.stack([image, far_image]), "tcol", swap(tcol_count, 1))
    images = [image]
    for step, arrived in enumerate(ring.steps(image, piece), 1):
        if step == ring.far - 1:
            arrived = lax.optimization_barrier((*arrived, gram))
            gram = arrived[2]
            tile = fetch(gram)
        images += arrived[:2]
    second, sums = call(
        functools.partial(image_kernel, (n, data_count, tcol_count, piece)),
        image_meta,
        [*images, tile, start, near_images, far_image, penalty_rows],
        [VMEM] * (n + 6),
        [VMEM] * 2,
        [jax.ShapeDtypeStruct((tcol_count, piece, heads), f32), jax.ShapeDtypeStruct((4, heads), f32)],
        [pltpu.VMEM((tile_columns, heads), f32)],
        IMAGE_BYTES,
        6 * tile_rows * tile_columns * heads,
        4 * tile_rows * tile_columns,
    )
    second, sums = owner_sum(second, sums)
    sums = all_sum(sums, ("dp", "trow", "tcol"))

    norm, curvature, image_norm, image_curvature = sums[0], sums[1], sums[2], sums[3]
    step = norm / curvature
    norm_next = step * step * image_norm - norm
    ratio = norm_next / norm
    moved_curvature = step * (step * image_curvature - (1.0 + ratio) * image_norm)
    next_step = norm_next / moved_curvature
    residual = start - step * image
    direction = residual + ratio * start
    weights = step * start + next_step * direction
    residual = residual - next_step * ((1.0 + ratio) * image - step * second)
    out_shape = (1, 1, 1, piece, heads)
    return (gram.reshape(gram_prior.shape), weights.reshape(out_shape), residual.reshape(out_shape))


def solution(mesh):
    placed = (
        P("dp", "tcol", "trow", None),
        P("dp", None),
        P(None, "trow", "dp", None, "tcol"),
        P("tcol", "trow", "dp", None),
    )
    return jax.shard_map(
        shards,
        mesh=mesh,
        in_specs=placed,
        out_specs=(
            P(None, "trow", "dp", None, "tcol"),
            P("tcol", "trow", "dp", None, None),
            P("tcol", "trow", "dp", None, None),
        ),
        check_vma=False,
    )
```

```python
import functools

import jax
import jax.numpy as jnp
import numpy as np
from jax import lax
from jax.experimental import pallas as pl
from jax.experimental.pallas import tpu as pltpu
from jax.sharding import PartitionSpec as P

NT = (((1,), (1,)), ((), ()))
NN = (((1,), (0,)), ((), ()))
VMEM = pl.BlockSpec(memory_space=pltpu.VMEM)
HBM = pl.BlockSpec(memory_space=pltpu.HBM)
EARLY_BYTES = 12 * 2**20
GRAM_BYTES = 24 * 2**20
IMAGE_BYTES = 20 * 2**20


def swap(count, bit):
    return [(place, place ^ bit) for place in range(count)]


class Ring:
    def __init__(self, data_count, trow_count):
        self.data_count = data_count
        self.count = data_count * trow_count
        self.cells = []
        for trow in range(trow_count):
            along = range(data_count) if trow % 2 == 0 else reversed(range(data_count))
            self.cells += [(data, trow) for data in along]
        flat = [data * trow_count + trow for data, trow in self.cells]
        self.ahead = [(flat[i], flat[(i + 1) % self.count]) for i in range(self.count)]
        self.back = [(target, source) for source, target in self.ahead]
        self.far = self.count // 2
        self.offsets = [0]
        for distance in range(1, self.far):
            self.offsets += [-distance, distance]
        self.offsets.append(self.far)
        self.place = np.zeros((data_count, trow_count), np.int32)
        for position, (data, trow) in enumerate(self.cells):
            self.place[data, trow] = position
        self.rounds = np.zeros((self.count, data_count), np.int32)
        self.chunk, self.trow, self.data = (np.zeros((self.count, self.count), np.int32) for _ in range(3))
        for position, (data, trow) in enumerate(self.cells):
            first = trow * data_count
            far_data = self.cells[(position + self.far) % self.count][0]
            near = sorted(
                range(first, first + data_count),
                key=lambda q: (self.cells[q][0] == far_data, abs(q - position), q),
            )
            chunk_of = {}
            for turn, other in enumerate(near):
                self.rounds[position, turn] = self.offsets.index(other - position)
                chunk_of[self.cells[other][0]] = turn
            for index, offset in enumerate(self.offsets):
                other_data, other_trow = self.cells[(position + offset) % self.count]
                self.chunk[position, index] = chunk_of[other_data]
                self.trow[position, index] = other_trow
                self.data[position, index] = other_data

    def steps(self, value, split_rows):
        ahead = back = value
        for _ in range(1, self.far):
            ahead = lax.ppermute(ahead, ("dp", "trow"), self.ahead)
            back = lax.ppermute(back, ("dp", "trow"), self.back)
            yield ahead, back
        half = (split_rows // 2 + 15) // 16 * 16
        low = lax.ppermute(ahead[:half], ("dp", "trow"), self.ahead)
        high = lax.ppermute(back[half:split_rows], ("dp", "trow"), self.back)
        yield low, high


ORDER = (1, 3, 0, 2)


def split(value):
    high = value.astype(jnp.bfloat16)
    return high, (value - high.astype(jnp.float32)).astype(jnp.bfloat16)


def dot(a, b, dims):
    return lax.dot_general(a, b, dims, preferred_element_type=jnp.float32)


def product(a, b):
    (a_high, a_low), (b_high, b_low) = a, b
    return dot(a_high, b_high, NN) + (dot(a_high, b_low, NN) + dot(a_low, b_high, NN))


def tile_copies(whole_ref, tile_ref, me, piece, block, semaphores, outward=False):
    copies = []
    for start in range(0, tile_ref.shape[1], block):
        lanes = pl.ds(start, block)
        for index, j in enumerate(ORDER):
            place = pl.ds(pl.multiple_of(jnp.bitwise_xor(me, j) * piece, 8), piece)
            pair = whole_ref.at[place, lanes], tile_ref.at[pl.ds(index * piece, piece), lanes]
            if outward:
                pair = pair[::-1]
            copies.append(pltpu.make_async_copy(*pair, semaphores.at[len(copies)]))
    return copies


def fetch_kernel(sizes, meta, gram_ref, tile_ref, come):
    piece, block = sizes
    loads = tile_copies(gram_ref, tile_ref, meta[0], piece, block, come)
    for load in loads:
        load.start()
    for load in loads:
        load.wait()


def pick_kernel(sizes, meta, *refs):
    turns, choices, width, piece, data_count = sizes
    *shard_refs, out_ref = refs
    head_part = shard_refs[0].shape[0] - width
    for index, turn in enumerate(turns):
        for shard_ref, choice in zip(shard_refs, choices):

            @pl.when(meta[turn] == choice)
            def _():
                out_ref[index, :head_part, :] = shard_ref[width:, :]
                if piece % 16 == 0:
                    place = pl.ds(pl.multiple_of(meta[data_count] * piece, 16), piece)
                    out_ref[index, head_part:, :] = shard_ref[place, :]
                else:
                    for data in range(data_count):

                        @pl.when(meta[data_count] == data)
                        def _():
                            out_ref[index, head_part:, :] = shard_ref[data * piece : (data + 1) * piece, :]


def place_rows(round_refs, me, head_part, rows, target, turn, count):
    for group in range(len(round_refs) // 3):
        own, far, near = round_refs[3 * group : 3 * group + 3]
        for inner in range(own.shape[0]):
            lanes = slice(turn * count, (turn + 1) * count)
            parts = [near[0, inner], near[1, inner], own[inner], far[inner]]
            for j, part in zip(ORDER, parts):
                at = pl.multiple_of(jnp.bitwise_xor(me, j) * head_part, 16)
                target[pl.ds(at, head_part), lanes] = part[:head_part, :]
            rows[:, lanes] = jnp.concatenate([part[head_part:, :] for part in parts], axis=0)
            turn += 1


def early_kernel(sizes, meta, *refs):
    n, width, head_part, block, groups = sizes
    shard_refs, refs = refs[: n - 1], refs[n - 1 :]
    round_refs, refs = refs[: 3 * groups], refs[3 * groups :]
    prior_ref, tile_ref, columns, rows, target = refs
    count = shard_refs[0].shape[1]
    for index in range(n - 1):
        lanes = pl.ds(pl.multiple_of(meta[index] * count, 128), count)
        base = pl.multiple_of(meta[n + index] * width, 16)
        columns[pl.ds(base, width), lanes] = shard_refs[index][:width, :]
    place_rows(round_refs, meta[2 * n], head_part, rows, target, 0, count)
    done = columns.shape[1] - count
    scale = 1.0 / columns.shape[1]
    for start in range(0, columns.shape[0], block):
        lanes = slice(start, start + block)
        tile_ref[:, lanes] = prior_ref[:, lanes] + dot(rows[:, :done], columns[lanes, :done], NT) * scale


def gram_kernel(sizes, meta, *refs):
    n, tcol_count, piece, width, head_part, block = sizes
    low_ref, high_ref, *round_refs = refs[:5]
    early_ref, columns, rows, target, gram_ref, tile_ref, right_ref, side_high, side_low, image_ref = refs[5:15]
    last_columns, last_rows, last_target, sent = refs[15:]
    me = meta[2 * n]
    total_rows = columns.shape[1]
    count = last_rows.shape[1]
    done = total_rows - count
    last_columns[...] = columns[:, done:]
    base = pl.multiple_of(meta[2 * n - 1] * width, 16)
    half = low_ref.shape[0]
    last_columns[pl.ds(base, half), :] = low_ref[...]
    last_columns[pl.ds(pl.multiple_of(base + half, 16), width - half), :] = high_ref[...]
    place_rows(round_refs, me, head_part, last_rows, last_target, 0, count)
    scale = 1.0 / total_rows
    stores = tile_copies(gram_ref, tile_ref, me, piece, block, sent, outward=True)
    for step in range(columns.shape[0] // block):
        lanes = slice(step * block, (step + 1) * block)
        last = last_columns[lanes, :]
        tile_ref[:, lanes] = early_ref[:, lanes] + dot(last_rows[...], last, NT) * scale
        for index in range(step * tcol_count, (step + 1) * tcol_count):
            stores[index].start()
        side = dot(columns[lanes, :done], target[:, :done], NT) + dot(last, last_target[...], NT)
        side_high[lanes, :], side_low[lanes, :] = split(side * scale)
    own = slice(2 * piece, 3 * piece)
    right = dot(rows[own, :done], target[:, :done], NT) + dot(last_rows[own, :], last_target[...], NT)
    right_ref[...] = right * scale
    value = product(split(tile_ref[: 2 * piece, :]), (side_high[...], side_low[...]))
    image_ref[...] = value.reshape(image_ref.shape)
    for store in stores:
        store.wait()


def kept_kernel(sizes, meta, tile_ref, side_high, side_low, image_ref):
    value = product(split(tile_ref[2 * sizes :, :]), (side_high[...], side_low[...]))
    image_ref[...] = value.reshape(image_ref.shape)


def partial_kernel(sizes, meta, *refs):
    n, data_count, piece = sizes
    shard_refs = refs[: n - 1]
    tile_ref, start_ref, total_ref, sums_ref, side = refs[n - 1 :]
    for index in range(n - 1):
        base = pl.multiple_of((meta[n + index] * data_count + meta[index]) * piece, 8)
        side[pl.ds(base, piece), :] = shard_refs[index][...]
    far = pl.multiple_of((meta[2 * n - 1] * data_count + meta[n - 1]) * piece, 8)
    side[pl.ds(far, piece), :] = jnp.zeros((piece, side.shape[1]), jnp.float32)
    total_ref[...] = product(split(tile_ref[...]), split(side[...]))
    own, start = shard_refs[0][...], start_ref[...]
    early = [jnp.sum(a * b, axis=0, keepdims=True) for a, b in ((start, start), (start, own), (own, own))]
    sums_ref[...] = jnp.concatenate(early, axis=0)


def image_kernel(sizes, meta, *refs):
    n, data_count, piece, block = sizes
    low_ref, high_ref, total_ref, tile_ref, early_ref = refs[:5]
    own_ref, near_ref, far_ref, penalty_ref, out_ref, sums_ref, side = refs[5:]
    base = (meta[2 * n - 1] * data_count + meta[n - 1]) * piece
    lanes = pl.ds(pl.multiple_of(base // block * block, 128), block)
    base = pl.multiple_of(base % block, 8)
    half = low_ref.shape[0]
    side[...] = jnp.zeros_like(side)
    side[pl.ds(base, half), :] = low_ref[...]
    side[pl.ds(pl.multiple_of(base + half, 8), piece - half), :] = high_ref[...]
    total = total_ref[...] + product(split(tile_ref[:, lanes]), split(side[...]))
    own = own_ref[...]
    others = [near_ref[0], near_ref[1], own, far_ref[...]]
    late = jnp.zeros((1, own.shape[1]), jnp.float32)
    for index, j in enumerate(ORDER):
        value = total[index * piece : (index + 1) * piece]
        if j == 0:
            value = value + penalty_ref[...] * own
        out_ref[index] = value
        late = late + jnp.sum(value * others[index], axis=0, keepdims=True)
    sums = jnp.concatenate([early_ref[...], late], axis=0)
    sums_ref[...] = jnp.broadcast_to(sums[None], sums_ref.shape)


def call(body, meta, inputs, in_specs, out_specs, out_shape, scratch, vmem, flops, read):
    return pl.pallas_call(
        body,
        grid_spec=pltpu.PrefetchScalarGridSpec(
            num_scalar_prefetch=1,
            grid=(1,),
            in_specs=in_specs,
            out_specs=out_specs,
            scratch_shapes=scratch,
        ),
        out_shape=out_shape,
        compiler_params=pltpu.CompilerParams(vmem_limit_bytes=vmem),
        cost_estimate=pl.CostEstimate(flops=flops, bytes_accessed=read, transcendentals=0),
    )(meta, *inputs)


def shards(embeddings, targets, gram_prior, penalty):
    row_count = embeddings.shape[0]
    width = embeddings.shape[3]
    heads = targets.shape[1]
    data_count = lax.axis_size("dp")
    trow_count = lax.axis_size("trow")
    tcol_count = lax.axis_size("tcol")
    piece = width // data_count
    total_rows = row_count * data_count
    tile_rows = tcol_count * piece
    tile_columns = trow_count * width
    head_part = heads // tcol_count
    data_place = lax.axis_index("dp")
    me = lax.axis_index("tcol")
    ring = Ring(data_count, trow_count)
    n = ring.count
    position = jnp.asarray(ring.place)[data_place, lax.axis_index("trow")]
    lookup = np.concatenate([ring.rounds, ring.chunk, ring.trow, ring.data, ring.trow], axis=1)
    lookup = jnp.asarray(lookup)[position]
    pick_meta = jnp.concatenate([lookup[:data_count], jnp.reshape(data_place, (1,)).astype(jnp.int32)])
    me_meta = jnp.reshape(me, (1,)).astype(jnp.int32)
    gram_meta = jnp.concatenate([lookup[data_count : data_count + 2 * n], me_meta])
    image_meta = jnp.concatenate([lookup[data_count + 2 * n :], me_meta])

    own = embeddings.reshape(row_count, width).T
    head_rows = lax.dynamic_slice_in_dim(targets, me * head_part, head_part, axis=1).T
    payload = jnp.concatenate([own, head_rows], axis=0)

    def pieces_of(turns):
        if turns == [0]:
            features = lax.dynamic_slice_in_dim(own, data_place * piece, piece, axis=0)
            return jnp.concatenate([head_rows, features], axis=0)[None]
        choices = sorted(set(ring.rounds[:, turns].ravel().tolist()))
        return call(
            functools.partial(pick_kernel, (turns, choices, width, piece, data_count)),
            pick_meta,
            [gathered[choice] for choice in choices],
            [VMEM] * len(choices),
            VMEM,
            jax.ShapeDtypeStruct((len(turns), head_part + piece, row_count), payload.dtype),
            [],
            2**20,
            0,
            4 * len(turns) * (head_part + piece) * row_count,
        )

    split_turns = [[0], list(range(1, data_count - 1)), [data_count - 1]]
    ready = [int(np.abs(np.asarray(ring.offsets)[ring.rounds[:, turns]]).max()) for turns in split_turns]
    gathered, groups, waiting = [payload], {}, []

    def near_of(group, mine, far):
        groups[group] = [mine, far, lax.ppermute(jnp.stack([mine, far]), "tcol", swap(tcol_count, 1))]

    def open_groups(step):
        for group, (turns, when) in enumerate(zip(split_turns, ready)):
            if when == step:
                mine = pieces_of(turns)
                waiting.append((group, mine, lax.ppermute(mine, "tcol", swap(tcol_count, 2))))

    block = 384 if tile_columns % 384 == 0 else 128
    f32, bf16 = jnp.float32, jnp.bfloat16
    tile_semaphores = pltpu.SemaphoreType.DMA((tcol_count * (tile_columns // block),))

    def fetch(whole):
        return call(
            functools.partial(fetch_kernel, (piece, block)),
            me_meta,
            [whole],
            [HBM],
            VMEM,
            jax.ShapeDtypeStruct((tile_rows, tile_columns), f32),
            [tile_semaphores],
            2**20,
            0,
            8 * tile_rows * tile_columns,
        )

    prior = gram_prior.reshape(tile_rows, tile_columns)
    open_groups(0)
    for step, arrived in enumerate(ring.steps(payload, width), 1):
        arrived = list(arrived)
        if step == 1:
            gram_meta, image_meta, pick_meta, *arrived = lax.optimization_barrier(
                (gram_meta, image_meta, pick_meta, *arrived)
            )
        if step == ring.far - 2:
            prior, *arrived = lax.optimization_barrier((prior, *arrived))
            prior = fetch(prior)
        if step == ring.far - 1:
            prior, *arrived = lax.optimization_barrier((prior, *arrived))
        while waiting:
            group, mine, far = waiting.pop()
            if step == ring.far:
                early, mine, far, *arrived = lax.optimization_barrier((early, mine, far, *arrived))
            else:
                mine, far, *arrived = lax.optimization_barrier((mine, far, *arrived))
            near_of(group, mine, far)
        gathered += arrived
        open_groups(step)
        if step == ring.far - 1:
            early, columns, rows, target = call(
                functools.partial(early_kernel, (n, width, head_part, block, 2)),
                gram_meta,
                [*gathered, *groups[0], *groups[1], prior],
                [VMEM] * (n + 6),
                [VMEM] * 4,
                [
                    jax.ShapeDtypeStruct((tile_rows, tile_columns), f32),
                    jax.ShapeDtypeStruct((tile_columns, total_rows), bf16),
                    jax.ShapeDtypeStruct((tile_rows, total_rows), bf16),
                    jax.ShapeDtypeStruct((heads, total_rows), bf16),
                ],
                [],
                EARLY_BYTES,
                2 * tile_rows * tile_columns * (total_rows - row_count),
                8 * tile_rows * tile_columns,
            )
    half_rows = (2, piece, heads)
    gram, gram_tile, start, side_high, side_low, sent = call(
        functools.partial(gram_kernel, (n, tcol_count, piece, width, head_part, block)),
        gram_meta,
        [*gathered[-2:], *groups[2], early, columns, rows, target],
        [VMEM] * 9,
        [HBM] + [VMEM] * 5,
        [
            jax.ShapeDtypeStruct((tile_rows, tile_columns), f32),
            jax.ShapeDtypeStruct((tile_rows, tile_columns), f32),
            jax.ShapeDtypeStruct((piece, heads), f32),
            jax.ShapeDtypeStruct((tile_columns, heads), bf16),
            jax.ShapeDtypeStruct((tile_columns, heads), bf16),
            jax.ShapeDtypeStruct(half_rows, f32),
        ],
        [
            pltpu.VMEM((tile_columns, row_count), bf16),
            pltpu.VMEM((tile_rows, row_count), bf16),
            pltpu.VMEM((heads, row_count), bf16),
            tile_semaphores,
        ],
        GRAM_BYTES,
        2 * tile_rows * tile_columns * (row_count + 2 * heads),
        12 * tile_rows * tile_columns,
    )
    penalty_rows = penalty.reshape(piece, 1)
    received = lax.ppermute(sent, "tcol", swap(tcol_count, 1))
    kept = call(
        functools.partial(kept_kernel, piece),
        me_meta,
        [gram_tile, side_high, side_low],
        [VMEM] * 3,
        VMEM,
        jax.ShapeDtypeStruct(half_rows, f32),
        [],
        IMAGE_BYTES,
        3 * tile_rows * tile_columns * heads,
        2 * tile_rows * tile_columns,
    )
    image = kept[0] + received[0] + lax.ppermute(kept[1] + received[1], "tcol", swap(tcol_count, 2))
    image = image + penalty_rows * start
    far_image = lax.ppermute(image, "tcol", swap(tcol_count, 2))
    near_images = lax.ppermute(jnp.stack([image, far_image]), "tcol", swap(tcol_count, 1))
    images = [image]
    for step, arrived in enumerate(ring.steps(image, piece), 1):
        if step == ring.far - 2:
            *arrived, gram = lax.optimization_barrier((*arrived, gram))
            tile = fetch(gram)
        if step == ring.far - 1:
            *arrived, tile = lax.optimization_barrier((*arrived, tile))
        images += arrived
    total, early_sums = call(
        functools.partial(partial_kernel, (n, data_count, piece)),
        image_meta,
        [*images[:-2], tile, start],
        [VMEM] * (n + 1),
        [VMEM] * 2,
        [jax.ShapeDtypeStruct((tile_rows, heads), f32), jax.ShapeDtypeStruct((3, heads), f32)],
        [pltpu.VMEM((tile_columns, heads), f32)],
        IMAGE_BYTES,
        6 * tile_rows * tile_columns * heads,
        4 * tile_rows * tile_columns,
    )
    axes = ("dp", "trow", "tcol")
    second, sums = call(
        functools.partial(image_kernel, (n, data_count, piece, block)),
        image_meta,
        [*images[-2:], total, tile, early_sums, image, near_images, far_image, penalty_rows],
        [VMEM] * 9,
        [VMEM] * 2,
        [
            jax.ShapeDtypeStruct((tcol_count, piece, heads), f32),
            jax.ShapeDtypeStruct((n * tcol_count, 4, heads), f32),
        ],
        [pltpu.VMEM((block, heads), f32)],
        IMAGE_BYTES,
        6 * tile_rows * block * heads,
        4 * tile_rows * block,
    )
    sums, second = lax.optimization_barrier((sums, second))
    sums = lax.all_to_all(sums, axes, split_axis=0, concat_axis=0, tiled=True)
    received = lax.ppermute(second[:2], "tcol", swap(tcol_count, 1))
    far_second = lax.ppermute(second[3] + received[1], "tcol", swap(tcol_count, 2))
    far_second, sums = lax.optimization_barrier((far_second, sums))
    sums = jnp.sum(sums, axis=0)
    second = second[2] + received[0] + far_second

    norm, curvature, image_norm, image_curvature = sums[0], sums[1], sums[2], sums[3]
    step = norm / curvature
    norm_next = step * step * image_norm - norm
    ratio = norm_next / norm
    moved_curvature = step * (step * image_curvature - (1.0 + ratio) * image_norm)
    next_step = norm_next / moved_curvature
    residual = start - step * image
    direction = residual + ratio * start
    weights = step * start + next_step * direction
    residual = residual - next_step * ((1.0 + ratio) * image - step * second)
    out_shape = (1, 1, 1, piece, heads)
    return (gram.reshape(gram_prior.shape), weights.reshape(out_shape), residual.reshape(out_shape))


def solution(mesh):
    placed = (
        P("dp", "tcol", "trow", None),
        P("dp", None),
        P(None, "trow", "dp", None, "tcol"),
        P("tcol", "trow", "dp", None),
    )
    return jax.shard_map(
        shards,
        mesh=mesh,
        in_specs=placed,
        out_specs=(
            P(None, "trow", "dp", None, "tcol"),
            P("tcol", "trow", "dp", None, None),
            P("tcol", "trow", "dp", None, None),
        ),
        check_vma=False,
    )
```

```python
import functools
import math

import jax
import jax.numpy as jnp
import numpy as np
from jax import lax
from jax.experimental import pallas as pl
from jax.experimental.pallas import tpu as pltpu
from jax.sharding import PartitionSpec as P

NT = (((1,), (1,)), ((), ()))
NN = (((1,), (0,)), ((), ()))
VMEM = pl.BlockSpec(memory_space=pltpu.VMEM)
HBM = pl.BlockSpec(memory_space=pltpu.HBM)
EARLY_BYTES = 12 * 2**20
GRAM_BYTES = 10 * 2**20
IMAGE_BYTES = 10 * 2**20


def swap(count, bit):
    return [(place, place ^ bit) for place in range(count)]


class Ring:
    def __init__(self, data_count, trow_count):
        self.data_count = data_count
        self.count = data_count * trow_count
        self.cells = []
        for trow in range(trow_count):
            along = range(data_count) if trow % 2 == 0 else reversed(range(data_count))
            self.cells += [(data, trow) for data in along]
        flat = [data * trow_count + trow for data, trow in self.cells]
        self.ahead = [(flat[i], flat[(i + 1) % self.count]) for i in range(self.count)]
        self.back = [(target, source) for source, target in self.ahead]
        self.far = self.count // 2
        self.offsets = [0]
        for distance in range(1, self.far):
            self.offsets += [-distance, distance]
        self.offsets.append(self.far)
        self.place = np.zeros((data_count, trow_count), np.int32)
        for position, (data, trow) in enumerate(self.cells):
            self.place[data, trow] = position
        self.rounds = np.zeros((self.count, data_count), np.int32)
        self.chunk, self.trow, self.data = (np.zeros((self.count, self.count), np.int32) for _ in range(3))
        for position, (data, trow) in enumerate(self.cells):
            first = trow * data_count
            far_data = self.cells[(position + self.far) % self.count][0]
            near = sorted(
                range(first, first + data_count),
                key=lambda q: (self.cells[q][0] == far_data, abs(q - position), q),
            )
            chunk_of = {}
            for turn, other in enumerate(near):
                self.rounds[position, turn] = self.offsets.index(other - position)
                chunk_of[self.cells[other][0]] = turn
            for index, offset in enumerate(self.offsets):
                other_data, other_trow = self.cells[(position + offset) % self.count]
                self.chunk[position, index] = chunk_of[other_data]
                self.trow[position, index] = other_trow
                self.data[position, index] = other_data

    def move(self, ahead, back):
        axes = ("dp", "trow")
        return [lax.ppermute(ahead, axes, self.ahead), lax.ppermute(back, axes, self.back)]

    def last(self, ahead, back, rows):
        half = (rows // 2 + 15) // 16 * 16
        return self.move(ahead[:half], back[half:rows])


ORDER = (1, 3, 0, 2)


def split(value):
    high = value.astype(jnp.bfloat16)
    return high, (value - high.astype(jnp.float32)).astype(jnp.bfloat16)


def dot(a, b, dims):
    return lax.dot_general(a, b, dims, preferred_element_type=jnp.float32)


def product(a, b):
    (a_high, a_low), (b_high, b_low) = a, b
    return dot(a_high, b_high, NN) + (dot(a_high, b_low, NN) + dot(a_low, b_high, NN))


def tile_copies(whole_ref, tile_ref, me, piece, block, semaphores):
    copies = []
    for start in range(0, tile_ref.shape[1], block):
        lanes = pl.ds(start, block)
        for index, j in enumerate(ORDER):
            place = pl.ds(pl.multiple_of(jnp.bitwise_xor(me, j) * piece, 8), piece)
            pair = whole_ref.at[place, lanes], tile_ref.at[pl.ds(index * piece, piece), lanes]
            copies.append(pltpu.make_async_copy(*pair, semaphores.at[len(copies)]))
    return copies


def fetch_kernel(sizes, meta, gram_ref, tile_ref, come):
    loads = tile_copies(gram_ref, tile_ref, meta[0], *sizes, come)
    for load in loads:
        load.start()
    for load in loads:
        load.wait()


def pick_rows(out_ref, head_ref, feature_ref, data_place, data_count, piece):
    head_part = head_ref.shape[0]
    out_ref[:head_part, :] = head_ref[...]
    if piece % 16 == 0:
        out_ref[head_part:, :] = feature_ref[pl.ds(pl.multiple_of(data_place * piece, 16), piece), :]
    else:
        for data in range(data_count):

            @pl.when(data_place == data)
            def _():
                out_ref[head_part:, :] = feature_ref[data * piece : (data + 1) * piece, :]


def pick_kernel(sizes, meta, *refs):
    turns, choices, width, piece, data_count = sizes
    *shard_refs, out_ref = refs
    for index, turn in enumerate(turns):
        for shard_ref, choice in zip(shard_refs, choices):

            @pl.when(meta[turn] == choice)
            def _():
                pick_rows(out_ref.at[index], shard_ref.at[width:], shard_ref, meta[data_count], data_count, piece)


def place_rows(round_refs, me, head_part, rows, target, turn, count):
    for group in range(len(round_refs) // 3):
        own, far, near = round_refs[3 * group : 3 * group + 3]
        for inner in range(own.shape[0]):
            lanes = slice(turn * count, (turn + 1) * count)
            parts = [near[0, inner], near[1, inner], own[inner], far[inner]]
            for j, part in zip(ORDER, parts):
                at = pl.multiple_of(jnp.bitwise_xor(me, j) * head_part, 16)
                target[pl.ds(at, head_part), lanes] = part[:head_part, :]
            rows[:, lanes] = jnp.concatenate([part[head_part:, :] for part in parts], axis=0)
            turn += 1


def early_kernel(sizes, meta, *refs):
    n, width, head_part, block, groups = sizes
    shard_refs, refs = refs[: n - 1], refs[n - 1 :]
    round_refs, refs = refs[: 3 * groups], refs[3 * groups :]
    prior_ref, tile_ref, side_ref, columns, rows, target = refs
    count = shard_refs[0].shape[1]
    for index in range(n - 1):
        lanes = pl.ds(pl.multiple_of(meta[index] * count, 128), count)
        base = pl.multiple_of(meta[n + index] * width, 16)
        columns[pl.ds(base, width), lanes] = shard_refs[index][:width, :]
    place_rows(round_refs, meta[2 * n], head_part, rows, target, 0, count)
    done = columns.shape[1] - count
    scale = 1.0 / columns.shape[1]
    for start in range(0, columns.shape[0], block):
        lanes = slice(start, start + block)
        column = columns[lanes, :done]
        tile_ref[:, lanes] = prior_ref[:, lanes] + dot(rows[:, :done], column, NT) * scale
        side_ref[lanes, :] = dot(column, target[:, :done], NT)


def tile_rows_of(first, early_ref, last_rows, last_columns, block, scale, tile_ref, gram_ref, me, piece, stored):
    part = pl.ds(first * piece, tile_ref.shape[0])
    copies = []
    for start in range(0, tile_ref.shape[1], block):
        lanes = pl.ds(start, block)
        tile_ref[:, lanes] = early_ref[part, lanes] + dot(last_rows[part, :], last_columns[lanes, :], NT) * scale
        copies += store_rows(tile_ref, gram_ref, me, first, piece, lanes, stored)
    return copies


def store_rows(tile_ref, gram_ref, me, first, piece, lanes, stored):
    copies = []
    for index in range(tile_ref.shape[0] // piece):
        place = pl.ds(pl.multiple_of(jnp.bitwise_xor(me, ORDER[first + index]) * piece, 8), piece)
        part = tile_ref.at[pl.ds(index * piece, piece), lanes]
        at = lanes.start // lanes.size * 2 + index
        copies.append(pltpu.make_async_copy(part, gram_ref.at[place, lanes], stored.at[at]))
        copies[-1].start()
    return copies


def send_kernel(sizes, meta, *refs):
    n, piece, width, head_part, block = sizes
    low_ref, high_ref, *round_refs = refs[:5]
    early_ref, early_side, columns, sent_ref, gram_ref = refs[5:10]
    side_high, side_low, last_columns, last_rows, last_target, tile_ref, stored = refs[10:]
    total_rows, count = columns.shape[1], last_rows.shape[1]
    last_columns[...] = columns[:, total_rows - count :]
    base = pl.multiple_of(meta[2 * n - 1] * width, 16)
    half = low_ref.shape[0]
    last_columns[pl.ds(base, half), :] = low_ref[...]
    last_columns[pl.ds(pl.multiple_of(base + half, 16), width - half), :] = high_ref[...]
    place_rows(round_refs, meta[2 * n], head_part, last_rows, last_target, 0, count)
    scale = 1.0 / total_rows
    copies = tile_rows_of(
        0, early_ref, last_rows, last_columns, block, scale, tile_ref, gram_ref, meta[2 * n], piece, stored
    )
    side = early_side[...] + dot(last_columns[...], last_target[...], NT)
    side_high[...], side_low[...] = split(side * scale)
    value = product(split(tile_ref[...]), (side_high[...], side_low[...]))
    sent_ref[...] = value.reshape(sent_ref.shape)
    for copy in copies:
        copy.wait()


def kept_kernel(sizes, meta, *refs):
    piece, block = sizes
    early_ref, last_columns, last_rows, side_high, side_low, last_target, rows, target = refs[:8]
    _, gram_ref, right_ref, image_ref, tile_ref, stored = refs[8:]
    total_rows, count = rows.shape[1], last_rows.shape[1]
    done = total_rows - count
    scale = 1.0 / total_rows
    copies = tile_rows_of(
        2, early_ref, last_rows, last_columns, block, scale, tile_ref, gram_ref, meta[0], piece, stored
    )
    own = slice(2 * piece, 3 * piece)
    right = dot(rows[own, :done], target[:, :done], NT) + dot(last_rows[own, :], last_target[...], NT)
    right_ref[...] = right * scale
    value = product(split(tile_ref[...]), (side_high[...], side_low[...]))
    image_ref[...] = value.reshape(image_ref.shape)
    for copy in copies:
        copy.wait()


def partial_kernel(sizes, meta, *refs):
    n, data_count, piece = sizes
    shard_refs = refs[: n - 1]
    tile_ref, start_ref, total_ref, sums_ref, side = refs[n - 1 :]
    for index in range(n - 1):
        base = pl.multiple_of((meta[n + index] * data_count + meta[index]) * piece, 8)
        side[pl.ds(base, piece), :] = shard_refs[index][...]
    far = pl.multiple_of((meta[2 * n - 1] * data_count + meta[n - 1]) * piece, 8)
    side[pl.ds(far, piece), :] = jnp.zeros((piece, side.shape[1]), jnp.float32)
    total_ref[...] = product(split(tile_ref[...]), split(side[...]))
    own, start = shard_refs[0][...], start_ref[...]
    early = [jnp.sum(a * b, axis=0, keepdims=True) for a, b in ((start, start), (start, own), (own, own))]
    sums_ref[...] = jnp.concatenate(early, axis=0)


def image_kernel(sizes, meta, *refs):
    n, data_count, piece, block = sizes
    low_ref, high_ref, total_ref, tile_ref, early_ref = refs[:5]
    own_ref, near_ref, far_ref, penalty_ref, out_ref, sums_ref, side = refs[5:]
    base = (meta[2 * n - 1] * data_count + meta[n - 1]) * piece
    lanes = pl.ds(pl.multiple_of(base // block * block, 128), block)
    base = pl.multiple_of(base % block, 8)
    half = low_ref.shape[0]
    side[...] = jnp.zeros_like(side)
    side[pl.ds(base, half), :] = low_ref[...]
    side[pl.ds(pl.multiple_of(base + half, 8), piece - half), :] = high_ref[...]
    total = total_ref[...] + product(split(tile_ref[:, lanes]), split(side[...]))
    own = own_ref[...]
    others = [near_ref[0], near_ref[1], own, far_ref[...]]
    late = jnp.zeros((1, own.shape[1]), jnp.float32)
    for index, j in enumerate(ORDER):
        value = total[index * piece : (index + 1) * piece]
        if j == 0:
            value = value + penalty_ref[...] * own
        out_ref[index] = value
        late = late + jnp.sum(value * others[index], axis=0, keepdims=True)
    sums = jnp.concatenate([early_ref[...], late], axis=0)
    sums_ref[...] = jnp.broadcast_to(sums[None], sums_ref.shape)


def call(body, meta, inputs, in_specs, out_specs, out_shape, scratch, vmem, flops, read, aliases={}):
    return pl.pallas_call(
        body,
        grid_spec=pltpu.PrefetchScalarGridSpec(
            num_scalar_prefetch=1,
            grid=(1,),
            in_specs=in_specs,
            out_specs=out_specs,
            scratch_shapes=scratch,
        ),
        out_shape=out_shape,
        input_output_aliases=aliases,
        compiler_params=pltpu.CompilerParams(vmem_limit_bytes=vmem),
        cost_estimate=pl.CostEstimate(flops=flops, bytes_accessed=read, transcendentals=0),
    )(meta, *inputs)


def shards(embeddings, targets, gram_prior, penalty):
    row_count = embeddings.shape[0]
    width = embeddings.shape[3]
    heads = targets.shape[1]
    data_count = lax.axis_size("dp")
    trow_count = lax.axis_size("trow")
    tcol_count = lax.axis_size("tcol")
    piece = width // data_count
    total_rows = row_count * data_count
    tile_rows = tcol_count * piece
    tile_columns = trow_count * width
    head_part = heads // tcol_count
    data_place = lax.axis_index("dp")
    me = lax.axis_index("tcol")
    ring = Ring(data_count, trow_count)
    n = ring.count
    position = jnp.asarray(ring.place)[data_place, lax.axis_index("trow")]
    lookup = np.concatenate([ring.rounds, ring.chunk, ring.trow, ring.data, ring.trow], axis=1)
    lookup = jnp.asarray(lookup)[position]
    pick_meta = jnp.concatenate([lookup[:data_count], jnp.reshape(data_place, (1,)).astype(jnp.int32)])
    me_meta = jnp.reshape(me, (1,)).astype(jnp.int32)
    gram_meta = jnp.concatenate([lookup[data_count : data_count + 2 * n], me_meta])
    image_meta = jnp.concatenate([lookup[data_count + 2 * n :], me_meta])

    f32, bf16 = jnp.float32, jnp.bfloat16
    features = embeddings.reshape(row_count, width).T
    head_rows = lax.dynamic_slice_in_dim(targets, me * head_part, head_part, axis=1).T
    payload = jnp.concatenate([features, head_rows], axis=0)

    def pieces_of(turns):
        if turns == [0]:
            own_rows = lax.dynamic_slice_in_dim(features, data_place * piece, piece, axis=0)
            return jnp.concatenate([head_rows, own_rows], axis=0)[None]
        choices = sorted(set(ring.rounds[:, turns].ravel().tolist()))
        return call(
            functools.partial(pick_kernel, (turns, choices, width, piece, data_count)),
            pick_meta,
            [gathered[choice] for choice in choices],
            [VMEM] * len(choices),
            VMEM,
            jax.ShapeDtypeStruct((len(turns), head_part + piece, row_count), payload.dtype),
            [],
            2**20,
            0,
            4 * len(turns) * (head_part + piece) * row_count,
        )

    split_turns = [[0], list(range(1, data_count - 1)), [data_count - 1]]
    ready = [int(np.abs(np.asarray(ring.offsets)[ring.rounds[:, turns]]).max()) for turns in split_turns]
    gathered, groups, waiting = [payload], {}, []

    def near_of(group, mine, far):
        groups[group] = [mine, far, lax.ppermute(jnp.stack([mine, far]), "tcol", swap(tcol_count, 1))]

    def open_groups(step):
        for group, (turns, when) in enumerate(zip(split_turns, ready)):
            if when == step:
                mine = pieces_of(turns)
                waiting.append((group, mine, lax.ppermute(mine, "tcol", swap(tcol_count, 2))))

    block = next(size for size in (512, 256, 128) if tile_columns % size == 0)
    far_block = math.lcm(piece, 128)
    tile_semaphores = pltpu.SemaphoreType.DMA((tcol_count * (tile_columns // block),))

    def fetch(whole):
        return call(
            functools.partial(fetch_kernel, (piece, block)),
            me_meta,
            [whole],
            [HBM],
            VMEM,
            jax.ShapeDtypeStruct((tile_rows, tile_columns), f32),
            [tile_semaphores],
            2**20,
            0,
            8 * tile_rows * tile_columns,
        )

    prior = gram_prior.reshape(tile_rows, tile_columns)
    open_groups(0)
    ahead = back = payload
    for step in range(1, ring.far + 1):
        if step < ring.far:
            arrived = ahead, back = ring.move(ahead, back)
        else:
            arrived = ring.last(ahead, back, width)
        if step == 1:
            gram_meta, image_meta, pick_meta, *arrived = lax.optimization_barrier(
                (gram_meta, image_meta, pick_meta, *arrived)
            )
        if step == ring.far - 2:
            prior, *arrived = lax.optimization_barrier((prior, *arrived))
            prior = fetch(prior)
        if step == ring.far - 1:
            prior, *arrived = lax.optimization_barrier((prior, *arrived))
        while waiting:
            group, mine, far = waiting.pop()
            if step == ring.far:
                early, mine, far, *arrived = lax.optimization_barrier((early, mine, far, *arrived))
            else:
                mine, far, *arrived = lax.optimization_barrier((mine, far, *arrived))
            near_of(group, mine, far)
        gathered += arrived
        open_groups(step)
        if step == ring.far - 1:
            early, early_side, columns, rows, target = call(
                functools.partial(early_kernel, (n, width, head_part, block, 2)),
                gram_meta,
                [*gathered, *groups[0], *groups[1], prior],
                [VMEM] * (n + 6),
                [VMEM] * 5,
                [
                    jax.ShapeDtypeStruct((tile_rows, tile_columns), f32),
                    jax.ShapeDtypeStruct((tile_columns, heads), f32),
                    jax.ShapeDtypeStruct((tile_columns, total_rows), bf16),
                    jax.ShapeDtypeStruct((tile_rows, total_rows), bf16),
                    jax.ShapeDtypeStruct((heads, total_rows), bf16),
                ],
                [],
                EARLY_BYTES,
                2 * tile_rows * tile_columns * (total_rows - row_count),
                8 * tile_rows * tile_columns,
            )
    sent, gram, side_high, side_low, last_columns, last_rows, last_target = call(
        functools.partial(send_kernel, (n, piece, width, head_part, block)),
        gram_meta,
        [*gathered[-2:], *groups[2], early, early_side, columns],
        [VMEM] * 8,
        [VMEM, HBM] + [VMEM] * 5,
        [
            jax.ShapeDtypeStruct((2, piece, heads), f32),
            jax.ShapeDtypeStruct((tile_rows, tile_columns), f32),
            jax.ShapeDtypeStruct((tile_columns, heads), bf16),
            jax.ShapeDtypeStruct((tile_columns, heads), bf16),
            jax.ShapeDtypeStruct((tile_columns, row_count), bf16),
            jax.ShapeDtypeStruct((tile_rows, row_count), bf16),
            jax.ShapeDtypeStruct((heads, row_count), bf16),
        ],
        [pltpu.VMEM((2 * piece, tile_columns), f32), pltpu.SemaphoreType.DMA((2 * (tile_columns // block),))],
        GRAM_BYTES,
        tile_rows * tile_columns * (row_count + 3 * heads),
        4 * tile_rows * tile_columns,
    )
    penalty_rows = penalty.reshape(piece, 1)
    received = lax.ppermute(sent, "tcol", swap(tcol_count, 1))
    gram, start, kept = call(
        functools.partial(kept_kernel, (piece, block)),
        me_meta,
        [early, last_columns, last_rows, side_high, side_low, last_target, rows, target, gram],
        [VMEM] * 8 + [HBM],
        [HBM, VMEM, VMEM],
        [
            jax.ShapeDtypeStruct((tile_rows, tile_columns), f32),
            jax.ShapeDtypeStruct((piece, heads), f32),
            jax.ShapeDtypeStruct((2, piece, heads), f32),
        ],
        [pltpu.VMEM((2 * piece, tile_columns), f32), pltpu.SemaphoreType.DMA((2 * (tile_columns // block),))],
        GRAM_BYTES,
        tile_rows * tile_columns * (row_count + 3 * heads),
        6 * tile_rows * tile_columns,
        {9: 0},
    )
    image = kept[0] + received[0] + lax.ppermute(kept[1] + received[1], "tcol", swap(tcol_count, 2))
    image = image + penalty_rows * start
    far_image = lax.ppermute(image, "tcol", swap(tcol_count, 2))
    near_images = lax.ppermute(jnp.stack([image, far_image]), "tcol", swap(tcol_count, 1))
    images = [image]
    ahead = back = image
    for step in range(1, ring.far + 1):
        if step < ring.far:
            arrived = ahead, back = ring.move(ahead, back)
        else:
            arrived = ring.last(ahead, back, piece)
        if step == ring.far - 2:
            *arrived, gram = lax.optimization_barrier((*arrived, gram))
            tile = fetch(gram)
        if step == ring.far - 1:
            *arrived, tile = lax.optimization_barrier((*arrived, tile))
        images += arrived
    total, early_sums = call(
        functools.partial(partial_kernel, (n, data_count, piece)),
        image_meta,
        [*images[:-2], tile, start],
        [VMEM] * (n + 1),
        [VMEM] * 2,
        [jax.ShapeDtypeStruct((tile_rows, heads), f32), jax.ShapeDtypeStruct((3, heads), f32)],
        [pltpu.VMEM((tile_columns, heads), f32)],
        IMAGE_BYTES,
        6 * tile_rows * tile_columns * heads,
        4 * tile_rows * tile_columns,
    )
    axes = ("dp", "trow", "tcol")
    second, sums = call(
        functools.partial(image_kernel, (n, data_count, piece, far_block)),
        image_meta,
        [*images[-2:], total, tile, early_sums, image, near_images, far_image, penalty_rows],
        [VMEM] * 9,
        [VMEM] * 2,
        [
            jax.ShapeDtypeStruct((tcol_count, piece, heads), f32),
            jax.ShapeDtypeStruct((n * tcol_count, 4, heads), f32),
        ],
        [pltpu.VMEM((far_block, heads), f32)],
        IMAGE_BYTES,
        6 * tile_rows * far_block * heads,
        4 * tile_rows * far_block,
    )
    sums, second = lax.optimization_barrier((sums, second))
    sums = lax.all_to_all(sums, axes, split_axis=0, concat_axis=0, tiled=True)
    received = lax.ppermute(second[:2], "tcol", swap(tcol_count, 1))
    far_second = lax.ppermute(second[3] + received[1], "tcol", swap(tcol_count, 2))
    far_second, sums = lax.optimization_barrier((far_second, sums))
    sums = jnp.sum(sums, axis=0)
    second = second[2] + received[0] + far_second

    norm, curvature, image_norm, image_curvature = sums[0], sums[1], sums[2], sums[3]
    step = norm / curvature
    norm_next = step * step * image_norm - norm
    ratio = norm_next / norm
    moved_curvature = step * (step * image_curvature - (1.0 + ratio) * image_norm)
    next_step = norm_next / moved_curvature
    residual = start - step * image
    direction = residual + ratio * start
    weights = step * start + next_step * direction
    residual = residual - next_step * ((1.0 + ratio) * image - step * second)
    out_shape = (1, 1, 1, piece, heads)
    return (gram.reshape(gram_prior.shape), weights.reshape(out_shape), residual.reshape(out_shape))


def solution(mesh):
    placed = (
        P("dp", "tcol", "trow", None),
        P("dp", None),
        P(None, "trow", "dp", None, "tcol"),
        P("tcol", "trow", "dp", None),
    )
    return jax.shard_map(
        shards,
        mesh=mesh,
        in_specs=placed,
        out_specs=(
            P(None, "trow", "dp", None, "tcol"),
            P("tcol", "trow", "dp", None, None),
            P("tcol", "trow", "dp", None, None),
        ),
        check_vma=False,
    )
```

```python
import functools
import math

import jax
import jax.numpy as jnp
import numpy as np
from jax import lax
from jax.experimental import pallas as pl
from jax.experimental.pallas import tpu as pltpu
from jax.sharding import PartitionSpec as P

NT = (((1,), (1,)), ((), ()))
NN = (((1,), (0,)), ((), ()))
VMEM = pl.BlockSpec(memory_space=pltpu.VMEM)
HBM = pl.BlockSpec(memory_space=pltpu.HBM)
EARLY_BYTES = 12 * 2**20
GRAM_BYTES = 10 * 2**20
IMAGE_BYTES = 10 * 2**20


def swap(count, bit):
    return [(place, place ^ bit) for place in range(count)]


class Ring:
    def __init__(self, data_count, trow_count):
        self.data_count = data_count
        self.count = data_count * trow_count
        self.cells = []
        for trow in range(trow_count):
            along = range(data_count) if trow % 2 == 0 else reversed(range(data_count))
            self.cells += [(data, trow) for data in along]
        flat = [data * trow_count + trow for data, trow in self.cells]
        self.ahead = [(flat[i], flat[(i + 1) % self.count]) for i in range(self.count)]
        self.back = [(target, source) for source, target in self.ahead]
        self.far = self.count // 2
        self.offsets = [0]
        for distance in range(1, self.far):
            self.offsets += [-distance, distance]
        self.offsets.append(self.far)
        self.place = np.zeros((data_count, trow_count), np.int32)
        for position, (data, trow) in enumerate(self.cells):
            self.place[data, trow] = position
        self.rounds = np.zeros((self.count, data_count), np.int32)
        self.chunk, self.trow, self.data = (np.zeros((self.count, self.count), np.int32) for _ in range(3))
        for position, (data, trow) in enumerate(self.cells):
            first = trow * data_count
            far_data = self.cells[(position + self.far) % self.count][0]
            near = sorted(
                range(first, first + data_count),
                key=lambda q: (self.cells[q][0] == far_data, abs(q - position), q),
            )
            chunk_of = {}
            for turn, other in enumerate(near):
                self.rounds[position, turn] = self.offsets.index(other - position)
                chunk_of[self.cells[other][0]] = turn
            for index, offset in enumerate(self.offsets):
                other_data, other_trow = self.cells[(position + offset) % self.count]
                self.chunk[position, index] = chunk_of[other_data]
                self.trow[position, index] = other_trow
                self.data[position, index] = other_data

    def move(self, ahead, back):
        axes = ("dp", "trow")
        return [lax.ppermute(ahead, axes, self.ahead), lax.ppermute(back, axes, self.back)]

    def last(self, ahead, back, rows, more=0):
        half = (rows // 2 + 15) // 16 * 16 + more
        return self.move(ahead[:half], back[half:rows])


ORDER = (3, 2, 1, 0)


def split(value):
    high = value.astype(jnp.bfloat16)
    return high, (value - high.astype(jnp.float32)).astype(jnp.bfloat16)


def dot(a, b, dims):
    return lax.dot_general(a, b, dims, preferred_element_type=jnp.float32)


def product(a, b):
    (a_high, a_low), (b_high, b_low) = a, b
    return dot(a_high, b_high, NN) + (dot(a_high, b_low, NN) + dot(a_low, b_high, NN))


def tile_copies(whole_ref, tile_ref, me, piece, block, semaphores):
    copies = []
    for start in range(0, tile_ref.shape[1], block):
        lanes = pl.ds(start, block)
        for index, j in enumerate(ORDER):
            place = pl.ds(pl.multiple_of(jnp.bitwise_xor(me, j) * piece, 8), piece)
            pair = whole_ref.at[place, lanes], tile_ref.at[pl.ds(index * piece, piece), lanes]
            copies.append(pltpu.make_async_copy(*pair, semaphores.at[len(copies)]))
    return copies


def fetch_kernel(sizes, meta, gram_ref, tile_ref, come):
    loads = tile_copies(gram_ref, tile_ref, meta[0], *sizes, come)
    for load in loads:
        load.start()
    for load in loads:
        load.wait()


def pick_rows(out_ref, head_ref, feature_ref, data_place, data_count, piece):
    head_part = head_ref.shape[0]
    out_ref[:head_part, :] = head_ref[...]
    if piece % 16 == 0:
        out_ref[head_part:, :] = feature_ref[pl.ds(pl.multiple_of(data_place * piece, 16), piece), :]
    else:
        for data in range(data_count):

            @pl.when(data_place == data)
            def _():
                out_ref[head_part:, :] = feature_ref[data * piece : (data + 1) * piece, :]


def pick_kernel(sizes, meta, *refs):
    turns, choices, width, piece, data_count = sizes
    *shard_refs, out_ref = refs
    for index, turn in enumerate(turns):
        for shard_ref, choice in zip(shard_refs, choices):

            @pl.when(meta[turn] == choice)
            def _():
                pick_rows(out_ref.at[index], shard_ref.at[width:], shard_ref, meta[data_count], data_count, piece)


def place_rows(round_refs, me, head_part, rows, target, turn, count):
    for group in range(len(round_refs) // 3):
        own, far, near = round_refs[3 * group : 3 * group + 3]
        for inner in range(own.shape[0]):
            lanes = slice(turn * count, (turn + 1) * count)
            parts = [near[1, inner], far[inner], near[0, inner], own[inner]]
            for j, part in zip(ORDER, parts):
                at = pl.multiple_of(jnp.bitwise_xor(me, j) * head_part, 16)
                target[pl.ds(at, head_part), lanes] = part[:head_part, :]
            rows[:, lanes] = jnp.concatenate([part[head_part:, :] for part in parts], axis=0)
            turn += 1


def early_kernel(sizes, meta, *refs):
    n, width, head_part, block, groups = sizes
    shard_refs, refs = refs[: n - 1], refs[n - 1 :]
    round_refs, refs = refs[: 3 * groups], refs[3 * groups :]
    prior_ref, now_ref, later_ref, side_ref, columns, rows, target = refs
    count = shard_refs[0].shape[1]
    for index in range(n - 1):
        lanes = pl.ds(pl.multiple_of(meta[index] * count, 128), count)
        base = pl.multiple_of(meta[n + index] * width, 16)
        columns[pl.ds(base, width), lanes] = shard_refs[index][:width, :]
    place_rows(round_refs, meta[2 * n], head_part, rows, target, 0, count)
    done = columns.shape[1] - count
    scale = 1.0 / columns.shape[1]
    for start in range(0, columns.shape[0], block):
        lanes = slice(start, start + block)
        column = columns[lanes, :done]
        value = prior_ref[:, lanes] + dot(rows[:, :done], column, NT) * scale
        now_ref[:, lanes], later_ref[:, lanes] = value[: now_ref.shape[0]], value[now_ref.shape[0] :]
        side_ref[lanes, :] = dot(column, target[:, :done], NT)


def tile_rows_of(first, early, last_rows, last_columns, block, scale, tile_ref, gram_ref, me, piece, stored):
    part = pl.ds(first * piece, tile_ref.shape[0])
    copies = []
    for start in range(0, tile_ref.shape[1], block):
        lanes = pl.ds(start, block)
        tile_ref[:, lanes] = early[:, lanes] + dot(last_rows[part, :], last_columns[lanes, :], NT) * scale
        for index in range(tile_ref.shape[0] // piece):
            place = pl.ds(pl.multiple_of(jnp.bitwise_xor(me, ORDER[first + index]) * piece, 8), piece)
            made = tile_ref.at[pl.ds(index * piece, piece), lanes]
            copies.append(pltpu.make_async_copy(made, gram_ref.at[place, lanes], stored.at[len(copies)]))
            copies[-1].start()
    return copies


def first_kernel(sizes, meta, *refs):
    n, piece, width, head_part, block = sizes
    low_ref, high_ref, *round_refs = refs[:5]
    early, early_side, columns, image_ref, gram_ref, tile_ref = refs[5:11]
    side_high, side_low, last_columns, last_rows, last_target, stored = refs[11:]
    total_rows, count = columns.shape[1], last_rows.shape[1]
    last_columns[...] = columns[:, total_rows - count :]
    base = pl.multiple_of(meta[2 * n - 1] * width, 16)
    half = low_ref.shape[0]
    last_columns[pl.ds(base, half), :] = low_ref[...]
    last_columns[pl.ds(pl.multiple_of(base + half, 16), width - half), :] = high_ref[...]
    place_rows(round_refs, meta[2 * n], head_part, last_rows, last_target, 0, count)
    scale = 1.0 / total_rows
    me = meta[2 * n]
    copies = tile_rows_of(0, early, last_rows, last_columns, block, scale, tile_ref, gram_ref, me, piece, stored)
    side = early_side[...] + dot(last_columns[...], last_target[...], NT)
    side_high[...], side_low[...] = split(side * scale)
    image_ref[...] = product(split(tile_ref[:piece, :]), (side_high[...], side_low[...]))
    for copy in copies:
        copy.wait()


def second_kernel(sizes, meta, *refs):
    tile_ref, last_rows, side_high, side_low, last_target, rows, target, right_ref, image_ref = refs
    piece = sizes
    total_rows, count = rows.shape[1], last_rows.shape[1]
    done = total_rows - count
    image_ref[...] = product(split(tile_ref[piece:, :]), (side_high[...], side_low[...]))
    own = slice(3 * piece, 4 * piece)
    right = dot(rows[own, :done], target[:, :done], NT) + dot(last_rows[own, :], last_target[...], NT)
    right_ref[...] = right * (1.0 / total_rows)


def third_kernel(sizes, meta, *refs):
    piece, block, total_rows = sizes
    early, last_columns, last_rows, side_high, side_low, _, gram_ref, image_ref, tile_ref, stored = refs
    scale = 1.0 / total_rows
    me = meta[0]
    copies = tile_rows_of(2, early, last_rows, last_columns, block, scale, tile_ref, gram_ref, me, piece, stored)
    value = product(split(tile_ref[...]), (side_high[...], side_low[...]))
    image_ref[...] = value.reshape(image_ref.shape)
    for copy in copies:
        copy.wait()


def partial_kernel(sizes, meta, *refs):
    n, data_count, piece = sizes
    shard_refs = refs[: n - 1]
    tile_ref, start_ref, total_ref, sums_ref, side = refs[n - 1 :]
    for index in range(n - 1):
        base = pl.multiple_of((meta[n + index] * data_count + meta[index]) * piece, 8)
        side[pl.ds(base, piece), :] = shard_refs[index][...]
    far = pl.multiple_of((meta[2 * n - 1] * data_count + meta[n - 1]) * piece, 8)
    side[pl.ds(far, piece), :] = jnp.zeros((piece, side.shape[1]), jnp.float32)
    total_ref[...] = product(split(tile_ref[...]), split(side[...]))
    own, start = shard_refs[0][...], start_ref[...]
    early = [jnp.sum(a * b, axis=0, keepdims=True) for a, b in ((start, start), (start, own), (own, own))]
    sums_ref[...] = jnp.concatenate(early, axis=0)


def image_kernel(sizes, meta, *refs):
    n, data_count, piece, block = sizes
    low_ref, high_ref, total_ref, tile_ref, early_ref = refs[:5]
    own_ref, near_ref, far_ref, penalty_ref, out_ref, sums_ref, side = refs[5:]
    base = (meta[2 * n - 1] * data_count + meta[n - 1]) * piece
    lanes = pl.ds(pl.multiple_of(base // block * block, 128), block)
    base = pl.multiple_of(base % block, 8)
    half = low_ref.shape[0]
    side[...] = jnp.zeros_like(side)
    side[pl.ds(base, half), :] = low_ref[...]
    side[pl.ds(pl.multiple_of(base + half, 8), piece - half), :] = high_ref[...]
    total = total_ref[...] + product(split(tile_ref[:, lanes]), split(side[...]))
    own = own_ref[...]
    others = [near_ref[1], far_ref[...], near_ref[0], own]
    late = jnp.zeros((1, own.shape[1]), jnp.float32)
    for index, j in enumerate(ORDER):
        value = total[index * piece : (index + 1) * piece]
        if j == 0:
            value = value + penalty_ref[...] * own
        out_ref[(3, 1, 2, 0).index(j)] = value
        late = late + jnp.sum(value * others[index], axis=0, keepdims=True)
    sums = jnp.concatenate([early_ref[...], late], axis=0)
    sums_ref[...] = jnp.broadcast_to(sums[None], sums_ref.shape)


def call(body, meta, inputs, in_specs, out_specs, out_shape, scratch, vmem, flops, read, aliases={}):
    return pl.pallas_call(
        body,
        grid_spec=pltpu.PrefetchScalarGridSpec(
            num_scalar_prefetch=1,
            grid=(1,),
            in_specs=in_specs,
            out_specs=out_specs,
            scratch_shapes=scratch,
        ),
        out_shape=out_shape,
        input_output_aliases=aliases,
        compiler_params=pltpu.CompilerParams(vmem_limit_bytes=vmem),
        cost_estimate=pl.CostEstimate(flops=flops, bytes_accessed=read, transcendentals=0),
    )(meta, *inputs)


def shards(embeddings, targets, gram_prior, penalty):
    row_count = embeddings.shape[0]
    width = embeddings.shape[3]
    heads = targets.shape[1]
    data_count = lax.axis_size("dp")
    trow_count = lax.axis_size("trow")
    tcol_count = lax.axis_size("tcol")
    piece = width // data_count
    total_rows = row_count * data_count
    tile_rows = tcol_count * piece
    tile_columns = trow_count * width
    head_part = heads // tcol_count
    data_place = lax.axis_index("dp")
    me = lax.axis_index("tcol")
    ring = Ring(data_count, trow_count)
    n = ring.count
    position = jnp.asarray(ring.place)[data_place, lax.axis_index("trow")]
    lookup = np.concatenate([ring.rounds, ring.chunk, ring.trow, ring.data, ring.trow], axis=1)
    lookup = jnp.asarray(lookup)[position]
    pick_meta = jnp.concatenate([lookup[:data_count], jnp.reshape(data_place, (1,)).astype(jnp.int32)])
    me_meta = jnp.reshape(me, (1,)).astype(jnp.int32)
    gram_meta = jnp.concatenate([lookup[data_count : data_count + 2 * n], me_meta])
    image_meta = jnp.concatenate([lookup[data_count + 2 * n :], me_meta])

    f32, bf16 = jnp.float32, jnp.bfloat16
    features = embeddings.reshape(row_count, width).T
    head_rows = lax.dynamic_slice_in_dim(targets, me * head_part, head_part, axis=1).T
    payload = jnp.concatenate([features, head_rows], axis=0)

    def pieces_of(turns):
        if turns == [0]:
            own_rows = lax.dynamic_slice_in_dim(features, data_place * piece, piece, axis=0)
            return jnp.concatenate([head_rows, own_rows], axis=0)[None]
        choices = sorted(set(ring.rounds[:, turns].ravel().tolist()))
        return call(
            functools.partial(pick_kernel, (turns, choices, width, piece, data_count)),
            pick_meta,
            [gathered[choice] for choice in choices],
            [VMEM] * len(choices),
            VMEM,
            jax.ShapeDtypeStruct((len(turns), head_part + piece, row_count), payload.dtype),
            [],
            2**20,
            0,
            4 * len(turns) * (head_part + piece) * row_count,
        )

    split_turns = [[0], list(range(1, data_count - 1)), [data_count - 1]]
    ready = [int(np.abs(np.asarray(ring.offsets)[ring.rounds[:, turns]]).max()) for turns in split_turns]
    gathered, groups, waiting = [payload], {}, []

    def near_of(group, mine, far):
        groups[group] = [mine, far, lax.ppermute(jnp.stack([mine, far]), "tcol", swap(tcol_count, 1))]

    def open_groups(step):
        for group, (turns, when) in enumerate(zip(split_turns, ready)):
            if when == step:
                mine = pieces_of(turns)
                waiting.append((group, mine, lax.ppermute(mine, "tcol", swap(tcol_count, 2))))

    block = next(size for size in (512, 256, 128) if tile_columns % size == 0)
    far_block = math.lcm(piece, 128)
    tile_semaphores = pltpu.SemaphoreType.DMA((tcol_count * (tile_columns // block),))

    def fetch(whole):
        return call(
            functools.partial(fetch_kernel, (piece, block)),
            me_meta,
            [whole],
            [HBM],
            VMEM,
            jax.ShapeDtypeStruct((tile_rows, tile_columns), f32),
            [tile_semaphores],
            2**20,
            0,
            8 * tile_rows * tile_columns,
        )

    prior = gram_prior.reshape(tile_rows, tile_columns)
    open_groups(0)
    ahead = back = payload
    for step in range(1, ring.far + 1):
        if step < ring.far:
            arrived = ahead, back = ring.move(ahead, back)
        else:
            arrived = ring.last(ahead, back, width)
        if step == 1:
            gram_meta, image_meta, pick_meta, *arrived = lax.optimization_barrier(
                (gram_meta, image_meta, pick_meta, *arrived)
            )
        if step == ring.far - 2:
            prior, *arrived = lax.optimization_barrier((prior, *arrived))
            prior = fetch(prior)
        if step == ring.far - 1:
            prior, *arrived = lax.optimization_barrier((prior, *arrived))
        while waiting:
            group, mine, far = waiting.pop()
            if step == ring.far:
                early, mine, far, *arrived = lax.optimization_barrier((early, mine, far, *arrived))
            else:
                mine, far, *arrived = lax.optimization_barrier((mine, far, *arrived))
            near_of(group, mine, far)
        gathered += arrived
        open_groups(step)
        if step == ring.far - 1:
            early, early_later, early_side, columns, rows, target = call(
                functools.partial(early_kernel, (n, width, head_part, block, 2)),
                gram_meta,
                [*gathered, *groups[0], *groups[1], prior],
                [VMEM] * (n + 6),
                [VMEM] * 6,
                [
                    jax.ShapeDtypeStruct((2 * piece, tile_columns), f32),
                    jax.ShapeDtypeStruct((2 * piece, tile_columns), f32),
                    jax.ShapeDtypeStruct((tile_columns, heads), f32),
                    jax.ShapeDtypeStruct((tile_columns, total_rows), bf16),
                    jax.ShapeDtypeStruct((tile_rows, total_rows), bf16),
                    jax.ShapeDtypeStruct((heads, total_rows), bf16),
                ],
                [],
                EARLY_BYTES,
                2 * tile_rows * tile_columns * (total_rows - row_count),
                8 * tile_rows * tile_columns,
            )
    gram_shape = jax.ShapeDtypeStruct((tile_rows, tile_columns), f32)
    piece_shape = jax.ShapeDtypeStruct((piece, heads), f32)

    def tile_scratch(pieces):
        shape = (pieces * piece, tile_columns)
        return [pltpu.VMEM(shape, f32), pltpu.SemaphoreType.DMA((pieces * (tile_columns // block),))]

    sent, gram, first_tile, side_high, side_low, last_columns, last_rows, last_target = call(
        functools.partial(first_kernel, (n, piece, width, head_part, block)),
        gram_meta,
        [*gathered[-2:], *groups[2], early, early_side, columns],
        [VMEM] * 8,
        [VMEM, HBM] + [VMEM] * 6,
        [
            piece_shape,
            gram_shape,
            jax.ShapeDtypeStruct((2 * piece, tile_columns), f32),
            jax.ShapeDtypeStruct((tile_columns, heads), bf16),
            jax.ShapeDtypeStruct((tile_columns, heads), bf16),
            jax.ShapeDtypeStruct((tile_columns, row_count), bf16),
            jax.ShapeDtypeStruct((tile_rows, row_count), bf16),
            jax.ShapeDtypeStruct((heads, row_count), bf16),
        ],
        tile_scratch(2)[1:],
        GRAM_BYTES,
        2 * piece * tile_columns * (2 * row_count + 3 * heads),
        16 * piece * tile_columns,
    )
    penalty_rows = penalty.reshape(piece, 1)
    received = lax.ppermute(sent, "tcol", swap(tcol_count, 1))
    start, far_part = call(
        functools.partial(second_kernel, piece),
        me_meta,
        [first_tile, last_rows, side_high, side_low, last_target, rows, target],
        [VMEM] * 7,
        [VMEM, VMEM],
        [piece_shape, piece_shape],
        [],
        GRAM_BYTES,
        6 * piece * tile_columns * heads,
        4 * piece * tile_columns,
    )
    far_part, early_later = lax.optimization_barrier((far_part + received, early_later))
    far_sum = lax.ppermute(far_part, "tcol", swap(tcol_count, 2))
    gram, kept = call(
        functools.partial(third_kernel, (piece, block, total_rows)),
        me_meta,
        [early_later, last_columns, last_rows, side_high, side_low, gram],
        [VMEM] * 5 + [HBM],
        [HBM, VMEM],
        [gram_shape, jax.ShapeDtypeStruct((2, piece, heads), f32)],
        tile_scratch(2),
        GRAM_BYTES,
        4 * piece * tile_columns * (row_count + 3 * heads),
        16 * piece * tile_columns,
        {6: 0},
    )
    halves = [kept[0][: piece // 2], kept[0][piece // 2 :]]
    near_sum = jnp.concatenate([lax.ppermute(part, "tcol", swap(tcol_count, 1)) for part in halves], axis=0)
    image = kept[1] + near_sum + penalty_rows * start + far_sum
    far_image = lax.ppermute(image, "tcol", swap(tcol_count, 2))
    near_images = lax.ppermute(jnp.stack([image, far_image]), "tcol", swap(tcol_count, 1))
    images = [image]
    ahead = back = image
    for step in range(1, ring.far + 1):
        if step < ring.far:
            arrived = ahead, back = ring.move(ahead, back)
        else:
            arrived = ring.last(ahead, back, piece, 16 if piece > 32 else 0)
        if step == ring.far - 2:
            *arrived, gram = lax.optimization_barrier((*arrived, gram))
            tile = fetch(gram)
        if step == ring.far - 1:
            *arrived, tile = lax.optimization_barrier((*arrived, tile))
        images += arrived
    total, early_sums = call(
        functools.partial(partial_kernel, (n, data_count, piece)),
        image_meta,
        [*images[:-2], tile, start],
        [VMEM] * (n + 1),
        [VMEM] * 2,
        [jax.ShapeDtypeStruct((tile_rows, heads), f32), jax.ShapeDtypeStruct((3, heads), f32)],
        [pltpu.VMEM((tile_columns, heads), f32)],
        IMAGE_BYTES,
        6 * tile_rows * tile_columns * heads,
        4 * tile_rows * tile_columns,
    )
    axes = ("dp", "trow", "tcol")
    second, sums = call(
        functools.partial(image_kernel, (n, data_count, piece, far_block)),
        image_meta,
        [*images[-2:], total, tile, early_sums, image, near_images, far_image, penalty_rows],
        [VMEM] * 9,
        [VMEM] * 2,
        [
            jax.ShapeDtypeStruct((tcol_count, piece, heads), f32),
            jax.ShapeDtypeStruct((n * tcol_count, 4, heads), f32),
        ],
        [pltpu.VMEM((far_block, heads), f32)],
        IMAGE_BYTES,
        6 * tile_rows * far_block * heads,
        4 * tile_rows * far_block,
    )
    sums, second = lax.optimization_barrier((sums, second))
    sums = lax.all_to_all(sums, axes, split_axis=0, concat_axis=0, tiled=True)
    received = lax.ppermute(second[:2], "tcol", swap(tcol_count, 1))
    far_second = lax.ppermute(second[2] + received[0], "tcol", swap(tcol_count, 2))
    far_second, sums = lax.optimization_barrier((far_second, sums))
    sums = jnp.sum(sums, axis=0)
    second = second[3] + received[1] + far_second

    norm, curvature, image_norm, image_curvature = sums[0], sums[1], sums[2], sums[3]
    step = norm / curvature
    norm_next = step * step * image_norm - norm
    ratio = norm_next / norm
    moved_curvature = step * (step * image_curvature - (1.0 + ratio) * image_norm)
    next_step = norm_next / moved_curvature
    residual = start - step * image
    direction = residual + ratio * start
    weights = step * start + next_step * direction
    residual = residual - next_step * ((1.0 + ratio) * image - step * second)
    out_shape = (1, 1, 1, piece, heads)
    return (gram.reshape(gram_prior.shape), weights.reshape(out_shape), residual.reshape(out_shape))


def solution(mesh):
    placed = (
        P("dp", "tcol", "trow", None),
        P("dp", None),
        P(None, "trow", "dp", None, "tcol"),
        P("tcol", "trow", "dp", None),
    )
    return jax.shard_map(
        shards,
        mesh=mesh,
        in_specs=placed,
        out_specs=(
            P(None, "trow", "dp", None, "tcol"),
            P("tcol", "trow", "dp", None, None),
            P("tcol", "trow", "dp", None, None),
        ),
        check_vma=False,
    )
```

```python
import functools
import math

import jax
import jax.numpy as jnp
import numpy as np
from jax import lax
from jax.experimental import pallas as pl
from jax.experimental.pallas import tpu as pltpu
from jax.sharding import PartitionSpec as P

NT = (((1,), (1,)), ((), ()))
NN = (((1,), (0,)), ((), ()))
VMEM = pl.BlockSpec(memory_space=pltpu.VMEM)
HBM = pl.BlockSpec(memory_space=pltpu.HBM)
EARLY_BYTES = 12 * 2**20
GRAM_BYTES = 10 * 2**20
IMAGE_BYTES = 10 * 2**20


def swap(count, bit):
    return [(place, place ^ bit) for place in range(count)]


class Ring:
    def __init__(self, data_count, trow_count):
        self.data_count = data_count
        self.count = data_count * trow_count
        self.cells = []
        for trow in range(trow_count):
            along = range(data_count) if trow % 2 == 0 else reversed(range(data_count))
            self.cells += [(data, trow) for data in along]
        flat = [data * trow_count + trow for data, trow in self.cells]
        self.ahead = [(flat[i], flat[(i + 1) % self.count]) for i in range(self.count)]
        self.back = [(target, source) for source, target in self.ahead]
        self.far = self.count // 2
        self.offsets = [0]
        for distance in range(1, self.far):
            self.offsets += [-distance, distance]
        self.offsets.append(self.far)
        self.place = np.zeros((data_count, trow_count), np.int32)
        for position, (data, trow) in enumerate(self.cells):
            self.place[data, trow] = position
        self.rounds = np.zeros((self.count, data_count), np.int32)
        self.chunk, self.trow, self.data = (np.zeros((self.count, self.count), np.int32) for _ in range(3))
        for position, (data, trow) in enumerate(self.cells):
            first = trow * data_count
            far_data = self.cells[(position + self.far) % self.count][0]
            near = sorted(
                range(first, first + data_count),
                key=lambda q: (self.cells[q][0] == far_data, abs(q - position), q),
            )
            chunk_of = {}
            for turn, other in enumerate(near):
                self.rounds[position, turn] = self.offsets.index(other - position)
                chunk_of[self.cells[other][0]] = turn
            for index, offset in enumerate(self.offsets):
                other_data, other_trow = self.cells[(position + offset) % self.count]
                self.chunk[position, index] = chunk_of[other_data]
                self.trow[position, index] = other_trow
                self.data[position, index] = other_data

    def move(self, ahead, back):
        axes = ("dp", "trow")
        return [lax.ppermute(ahead, axes, self.ahead), lax.ppermute(back, axes, self.back)]

    def last(self, ahead, back, rows, more=0):
        half = (rows // 2 + 15) // 16 * 16 + more
        return self.move(ahead[:half], back[half:rows])


ORDER = (3, 2, 1, 0)


def split(value):
    high = value.astype(jnp.bfloat16)
    return high, (value - high.astype(jnp.float32)).astype(jnp.bfloat16)


def dot(a, b, dims):
    return lax.dot_general(a, b, dims, preferred_element_type=jnp.float32)


def product(a, b):
    (a_high, a_low), (b_high, b_low) = a, b
    return dot(a_high, b_high, NN) + (dot(a_high, b_low, NN) + dot(a_low, b_high, NN))


def tile_copies(whole_ref, tile_ref, me, piece, block, semaphores):
    copies = []
    for start in range(0, tile_ref.shape[1], block):
        lanes = pl.ds(start, block)
        for index, j in enumerate(ORDER):
            place = pl.ds(pl.multiple_of(jnp.bitwise_xor(me, j) * piece, 8), piece)
            pair = whole_ref.at[place, lanes], tile_ref.at[pl.ds(index * piece, piece), lanes]
            copies.append(pltpu.make_async_copy(*pair, semaphores.at[len(copies)]))
    return copies


def fetch_kernel(sizes, meta, gram_ref, tile_ref, come):
    loads = tile_copies(gram_ref, tile_ref, meta[0], *sizes, come)
    for load in loads:
        load.start()
    for load in loads:
        load.wait()


def pick_rows(out_ref, head_ref, feature_ref, data_place, data_count, piece):
    head_part = head_ref.shape[0]
    out_ref[:head_part, :] = head_ref[...]
    if piece % 16 == 0:
        out_ref[head_part:, :] = feature_ref[pl.ds(pl.multiple_of(data_place * piece, 16), piece), :]
    else:
        for data in range(data_count):

            @pl.when(data_place == data)
            def _():
                out_ref[head_part:, :] = feature_ref[data * piece : (data + 1) * piece, :]


def pick_kernel(sizes, meta, *refs):
    turns, choices, width, piece, data_count = sizes
    *shard_refs, out_ref = refs
    for index, turn in enumerate(turns):
        for shard_ref, choice in zip(shard_refs, choices):

            @pl.when(meta[turn] == choice)
            def _():
                pick_rows(out_ref.at[index], shard_ref.at[width:], shard_ref, meta[data_count], data_count, piece)


def place_rows(round_refs, me, head_part, rows, target, turn, count):
    for group in range(len(round_refs) // 3):
        own, far, near = round_refs[3 * group : 3 * group + 3]
        for inner in range(own.shape[0]):
            lanes = slice(turn * count, (turn + 1) * count)
            parts = [near[1, inner], far[inner], near[0, inner], own[inner]]
            for j, part in zip(ORDER, parts):
                at = pl.multiple_of(jnp.bitwise_xor(me, j) * head_part, 16)
                target[pl.ds(at, head_part), lanes] = part[:head_part, :]
            rows[:, lanes] = jnp.concatenate([part[head_part:, :] for part in parts], axis=0)
            turn += 1


def early_kernel(sizes, meta, *refs):
    n, width, head_part, block, groups = sizes
    shard_refs, refs = refs[: n - 1], refs[n - 1 :]
    round_refs, refs = refs[: 3 * groups], refs[3 * groups :]
    prior_ref, now_ref, later_ref, side_ref, columns, rows, target = refs
    count = shard_refs[0].shape[1]
    for index in range(n - 1):
        lanes = pl.ds(pl.multiple_of(meta[index] * count, 128), count)
        base = pl.multiple_of(meta[n + index] * width, 16)
        columns[pl.ds(base, width), lanes] = shard_refs[index][:width, :]
    place_rows(round_refs, meta[2 * n], head_part, rows, target, 0, count)
    done = columns.shape[1] - count
    scale = 1.0 / columns.shape[1]
    for start in range(0, columns.shape[0], block):
        lanes = slice(start, start + block)
        column = columns[lanes, :done]
        value = prior_ref[:, lanes] + dot(rows[:, :done], column, NT) * scale
        now_ref[:, lanes], later_ref[:, lanes] = value[: now_ref.shape[0]], value[now_ref.shape[0] :]
        side_ref[lanes, :] = dot(column, target[:, :done], NT)


def tile_rows_of(first, early, last_rows, last_columns, block, scale, tile_ref, gram_ref, me, piece, stored):
    part = pl.ds(first * piece, tile_ref.shape[0])
    copies = []
    for start in range(0, tile_ref.shape[1], block):
        lanes = pl.ds(start, block)
        tile_ref[:, lanes] = early[:, lanes] + dot(last_rows[part, :], last_columns[lanes, :], NT) * scale
        for index in range(tile_ref.shape[0] // piece):
            place = pl.ds(pl.multiple_of(jnp.bitwise_xor(me, ORDER[first + index]) * piece, 8), piece)
            made = tile_ref.at[pl.ds(index * piece, piece), lanes]
            copies.append(pltpu.make_async_copy(made, gram_ref.at[place, lanes], stored.at[len(copies)]))
            copies[-1].start()
    return copies


def first_kernel(sizes, meta, *refs):
    n, piece, width, head_part, block = sizes
    low_ref, high_ref, *round_refs = refs[:5]
    early, early_side, columns, image_ref, gram_ref, tile_ref = refs[5:11]
    side_high, side_low, last_columns, last_rows, last_target, stored = refs[11:]
    total_rows, count = columns.shape[1], last_rows.shape[1]
    last_columns[...] = columns[:, total_rows - count :]
    base = pl.multiple_of(meta[2 * n - 1] * width, 16)
    half = low_ref.shape[0]
    last_columns[pl.ds(base, half), :] = low_ref[...]
    last_columns[pl.ds(pl.multiple_of(base + half, 16), width - half), :] = high_ref[...]
    place_rows(round_refs, meta[2 * n], head_part, last_rows, last_target, 0, count)
    scale = 1.0 / total_rows
    me = meta[2 * n]
    copies = tile_rows_of(0, early, last_rows, last_columns, block, scale, tile_ref, gram_ref, me, piece, stored)
    side = early_side[...] + dot(last_columns[...], last_target[...], NT)
    side_high[...], side_low[...] = split(side * scale)
    image_ref[...] = product(split(tile_ref[:piece, :]), (side_high[...], side_low[...]))
    for copy in copies:
        copy.wait()


def second_kernel(sizes, meta, *refs):
    tile_ref, last_rows, side_high, side_low, last_target, rows, target, right_ref, image_ref = refs
    piece = sizes
    total_rows, count = rows.shape[1], last_rows.shape[1]
    done = total_rows - count
    image_ref[...] = product(split(tile_ref[piece:, :]), (side_high[...], side_low[...]))
    own = slice(3 * piece, 4 * piece)
    right = dot(rows[own, :done], target[:, :done], NT) + dot(last_rows[own, :], last_target[...], NT)
    right_ref[...] = right * (1.0 / total_rows)


def third_kernel(sizes, meta, *refs):
    piece, block, total_rows = sizes
    early, last_columns, last_rows, side_high, side_low, _, gram_ref, image_ref, tile_ref, stored = refs
    scale = 1.0 / total_rows
    me = meta[0]
    copies = tile_rows_of(2, early, last_rows, last_columns, block, scale, tile_ref, gram_ref, me, piece, stored)
    value = product(split(tile_ref[...]), (side_high[...], side_low[...]))
    image_ref[...] = value.reshape(image_ref.shape)
    for copy in copies:
        copy.wait()


def weighted(parts, others):
    return sum(jnp.sum(a * b, axis=0, keepdims=True) for a, b in zip(parts, others))


def partial_kernel(sizes, meta, *refs):
    n, data_count, piece, block = sizes
    shard_refs = refs[: n - 1]
    tile_ref, start_ref, near_ref, far_ref, penalty_ref, total_ref, sums_ref, far_high, far_low, side = refs[n - 1 :]
    for index in range(n - 1):
        base = pl.multiple_of((meta[n + index] * data_count + meta[index]) * piece, 8)
        side[pl.ds(base, piece), :] = shard_refs[index][...]
    base = (meta[2 * n - 1] * data_count + meta[n - 1]) * piece
    side[pl.ds(pl.multiple_of(base, 8), piece), :] = jnp.zeros((piece, side.shape[1]), jnp.float32)
    total = product(split(tile_ref[...]), split(side[...]))
    own, start = shard_refs[0][...], start_ref[...]
    others = [near_ref[1], far_ref[...], near_ref[0], own]
    parts = [total[index * piece : (index + 1) * piece] for index in range(len(ORDER))]
    parts[-1] = parts[-1] + penalty_ref[...] * own
    for index, part in enumerate(parts):
        total_ref[index] = part
    sums = [weighted([a], [b]) for a, b in ((start, start), (start, own), (own, own))]
    sums_ref[...] = jnp.concatenate(sums + [weighted(parts, others)], axis=0)
    lanes = pl.ds(pl.multiple_of(base // block * block, 128), block)
    for place in range(block // piece):

        @pl.when(base % block == place * piece)
        def _():
            far_high[...], far_low[...] = split(tile_ref[:, lanes][:, place * piece : (place + 1) * piece])


def image_kernel(sizes, meta, *refs):
    piece = sizes
    low_ref, high_ref, total_ref, far_high, far_low, early_ref, own_ref, near_ref, far_ref, out_ref, sums_ref = refs
    side = jnp.concatenate([low_ref[...], high_ref[...]], axis=0)
    value = product((far_high[...], far_low[...]), split(side))
    others = [near_ref[1], far_ref[...], near_ref[0], own_ref[...]]
    parts = [value[index * piece : (index + 1) * piece] for index in range(len(ORDER))]
    early = early_ref[...]
    sums = jnp.concatenate([early[:3], early[3:] + weighted(parts, others)], axis=0)
    sums_ref[...] = jnp.broadcast_to(sums[None], sums_ref.shape)
    for index, j in enumerate(ORDER):
        out_ref[(3, 1, 2, 0).index(j)] = total_ref[index] + parts[index]


def call(body, meta, inputs, in_specs, out_specs, out_shape, scratch, vmem, flops, read, aliases={}):
    return pl.pallas_call(
        body,
        grid_spec=pltpu.PrefetchScalarGridSpec(
            num_scalar_prefetch=1,
            grid=(1,),
            in_specs=in_specs,
            out_specs=out_specs,
            scratch_shapes=scratch,
        ),
        out_shape=out_shape,
        input_output_aliases=aliases,
        compiler_params=pltpu.CompilerParams(vmem_limit_bytes=vmem),
        cost_estimate=pl.CostEstimate(flops=flops, bytes_accessed=read, transcendentals=0),
    )(meta, *inputs)


def shards(embeddings, targets, gram_prior, penalty):
    row_count = embeddings.shape[0]
    width = embeddings.shape[3]
    heads = targets.shape[1]
    data_count = lax.axis_size("dp")
    trow_count = lax.axis_size("trow")
    tcol_count = lax.axis_size("tcol")
    piece = width // data_count
    total_rows = row_count * data_count
    tile_rows = tcol_count * piece
    tile_columns = trow_count * width
    head_part = heads // tcol_count
    data_place = lax.axis_index("dp")
    me = lax.axis_index("tcol")
    ring = Ring(data_count, trow_count)
    n = ring.count
    position = jnp.asarray(ring.place)[data_place, lax.axis_index("trow")]
    lookup = np.concatenate([ring.rounds, ring.chunk, ring.trow, ring.data, ring.trow], axis=1)
    lookup = jnp.asarray(lookup)[position]
    pick_meta = jnp.concatenate([lookup[:data_count], jnp.reshape(data_place, (1,)).astype(jnp.int32)])
    me_meta = jnp.reshape(me, (1,)).astype(jnp.int32)
    gram_meta = jnp.concatenate([lookup[data_count : data_count + 2 * n], me_meta])
    image_meta = jnp.concatenate([lookup[data_count + 2 * n :], me_meta])

    f32, bf16 = jnp.float32, jnp.bfloat16
    features = embeddings.reshape(row_count, width).T
    head_rows = lax.dynamic_slice_in_dim(targets, me * head_part, head_part, axis=1).T
    payload = jnp.concatenate([features, head_rows], axis=0)

    def pieces_of(turns):
        if turns == [0]:
            own_rows = lax.dynamic_slice_in_dim(features, data_place * piece, piece, axis=0)
            return jnp.concatenate([head_rows, own_rows], axis=0)[None]
        choices = sorted(set(ring.rounds[:, turns].ravel().tolist()))
        return call(
            functools.partial(pick_kernel, (turns, choices, width, piece, data_count)),
            pick_meta,
            [gathered[choice] for choice in choices],
            [VMEM] * len(choices),
            VMEM,
            jax.ShapeDtypeStruct((len(turns), head_part + piece, row_count), payload.dtype),
            [],
            2**20,
            0,
            4 * len(turns) * (head_part + piece) * row_count,
        )

    split_turns = [[0], list(range(1, data_count - 1)), [data_count - 1]]
    ready = [int(np.abs(np.asarray(ring.offsets)[ring.rounds[:, turns]]).max()) for turns in split_turns]
    gathered, groups, waiting = [payload], {}, []

    def near_of(group, mine, far):
        groups[group] = [mine, far, lax.ppermute(jnp.stack([mine, far]), "tcol", swap(tcol_count, 1))]

    def open_groups(step):
        for group, (turns, when) in enumerate(zip(split_turns, ready)):
            if when == step:
                mine = pieces_of(turns)
                waiting.append((group, mine, lax.ppermute(mine, "tcol", swap(tcol_count, 2))))

    block = next(size for size in (512, 256, 128) if tile_columns % size == 0)
    far_block = math.lcm(piece, 128)
    tile_semaphores = pltpu.SemaphoreType.DMA((tcol_count * (tile_columns // block),))

    def fetch(whole):
        return call(
            functools.partial(fetch_kernel, (piece, block)),
            me_meta,
            [whole],
            [HBM],
            VMEM,
            jax.ShapeDtypeStruct((tile_rows, tile_columns), f32),
            [tile_semaphores],
            2**20,
            0,
            8 * tile_rows * tile_columns,
        )

    prior = gram_prior.reshape(tile_rows, tile_columns)
    open_groups(0)
    ahead = back = payload
    for step in range(1, ring.far + 1):
        if step < ring.far:
            arrived = ahead, back = ring.move(ahead, back)
        else:
            arrived = ring.last(ahead, back, width)
        if step == 1:
            gram_meta, image_meta, pick_meta, *arrived = lax.optimization_barrier(
                (gram_meta, image_meta, pick_meta, *arrived)
            )
        if step == ring.far - 2:
            prior, *arrived = lax.optimization_barrier((prior, *arrived))
            prior = fetch(prior)
        if step == ring.far - 1:
            prior, *arrived = lax.optimization_barrier((prior, *arrived))
        while waiting:
            group, mine, far = waiting.pop()
            if step == ring.far:
                early, mine, far, *arrived = lax.optimization_barrier((early, mine, far, *arrived))
            else:
                mine, far, *arrived = lax.optimization_barrier((mine, far, *arrived))
            near_of(group, mine, far)
        gathered += arrived
        open_groups(step)
        if step == ring.far - 1:
            early, early_later, early_side, columns, rows, target = call(
                functools.partial(early_kernel, (n, width, head_part, block, 2)),
                gram_meta,
                [*gathered, *groups[0], *groups[1], prior],
                [VMEM] * (n + 6),
                [VMEM] * 6,
                [
                    jax.ShapeDtypeStruct((2 * piece, tile_columns), f32),
                    jax.ShapeDtypeStruct((2 * piece, tile_columns), f32),
                    jax.ShapeDtypeStruct((tile_columns, heads), f32),
                    jax.ShapeDtypeStruct((tile_columns, total_rows), bf16),
                    jax.ShapeDtypeStruct((tile_rows, total_rows), bf16),
                    jax.ShapeDtypeStruct((heads, total_rows), bf16),
                ],
                [],
                EARLY_BYTES,
                2 * tile_rows * tile_columns * (total_rows - row_count),
                8 * tile_rows * tile_columns,
            )
    gram_shape = jax.ShapeDtypeStruct((tile_rows, tile_columns), f32)
    piece_shape = jax.ShapeDtypeStruct((piece, heads), f32)

    def tile_scratch(pieces):
        shape = (pieces * piece, tile_columns)
        return [pltpu.VMEM(shape, f32), pltpu.SemaphoreType.DMA((pieces * (tile_columns // block),))]

    sent, gram, first_tile, side_high, side_low, last_columns, last_rows, last_target = call(
        functools.partial(first_kernel, (n, piece, width, head_part, block)),
        gram_meta,
        [*gathered[-2:], *groups[2], early, early_side, columns],
        [VMEM] * 8,
        [VMEM, HBM] + [VMEM] * 6,
        [
            piece_shape,
            gram_shape,
            jax.ShapeDtypeStruct((2 * piece, tile_columns), f32),
            jax.ShapeDtypeStruct((tile_columns, heads), bf16),
            jax.ShapeDtypeStruct((tile_columns, heads), bf16),
            jax.ShapeDtypeStruct((tile_columns, row_count), bf16),
            jax.ShapeDtypeStruct((tile_rows, row_count), bf16),
            jax.ShapeDtypeStruct((heads, row_count), bf16),
        ],
        tile_scratch(2)[1:],
        GRAM_BYTES,
        2 * piece * tile_columns * (2 * row_count + 3 * heads),
        16 * piece * tile_columns,
    )
    penalty_rows = penalty.reshape(piece, 1)
    received = lax.ppermute(sent, "tcol", swap(tcol_count, 1))
    start, far_part = call(
        functools.partial(second_kernel, piece),
        me_meta,
        [first_tile, last_rows, side_high, side_low, last_target, rows, target],
        [VMEM] * 7,
        [VMEM, VMEM],
        [piece_shape, piece_shape],
        [],
        GRAM_BYTES,
        6 * piece * tile_columns * heads,
        4 * piece * tile_columns,
    )
    far_part, early_later = lax.optimization_barrier((far_part + received, early_later))
    far_sum = lax.ppermute(far_part, "tcol", swap(tcol_count, 2))
    gram, kept = call(
        functools.partial(third_kernel, (piece, block, total_rows)),
        me_meta,
        [early_later, last_columns, last_rows, side_high, side_low, gram],
        [VMEM] * 5 + [HBM],
        [HBM, VMEM],
        [gram_shape, jax.ShapeDtypeStruct((2, piece, heads), f32)],
        tile_scratch(2),
        GRAM_BYTES,
        4 * piece * tile_columns * (row_count + 3 * heads),
        16 * piece * tile_columns,
        {6: 0},
    )
    halves = [kept[0][: piece // 2], kept[0][piece // 2 :]]
    near_sum = jnp.concatenate([lax.ppermute(part, "tcol", swap(tcol_count, 1)) for part in halves], axis=0)
    image = kept[1] + near_sum + penalty_rows * start + far_sum
    far_image = lax.ppermute(image, "tcol", swap(tcol_count, 2))
    near_images = lax.ppermute(jnp.stack([image, far_image]), "tcol", swap(tcol_count, 1))
    images = [image]
    ahead = back = image
    for step in range(1, ring.far + 1):
        if step < ring.far:
            arrived = ahead, back = ring.move(ahead, back)
        else:
            arrived = ring.last(ahead, back, piece, 16 if piece > 32 else 0)
        if step == ring.far - 2:
            *arrived, gram = lax.optimization_barrier((*arrived, gram))
            tile = fetch(gram)
        if step == ring.far - 1:
            *arrived, tile = lax.optimization_barrier((*arrived, tile))
        images += arrived
    part_shape = jax.ShapeDtypeStruct((tcol_count, piece, heads), f32)
    far_shape = jax.ShapeDtypeStruct((tile_rows, piece), bf16)
    total, early_sums, far_high, far_low = call(
        functools.partial(partial_kernel, (n, data_count, piece, far_block)),
        image_meta,
        [*images[:-2], tile, start, near_images, far_image, penalty_rows],
        [VMEM] * (n + 4),
        [VMEM] * 4,
        [part_shape, jax.ShapeDtypeStruct((4, heads), f32), far_shape, far_shape],
        [pltpu.VMEM((tile_columns, heads), f32)],
        IMAGE_BYTES,
        6 * tile_rows * tile_columns * heads,
        4 * tile_rows * tile_columns,
    )
    axes = ("dp", "trow", "tcol")
    second, sums = call(
        functools.partial(image_kernel, piece),
        image_meta,
        [*images[-2:], total, far_high, far_low, early_sums, image, near_images, far_image],
        [VMEM] * 9,
        [VMEM] * 2,
        [part_shape, jax.ShapeDtypeStruct((n * tcol_count, 4, heads), f32)],
        [],
        IMAGE_BYTES,
        6 * tile_rows * piece * heads,
        4 * tile_rows * piece,
    )
    sums, second = lax.optimization_barrier((sums, second))
    sums = lax.all_to_all(sums, axes, split_axis=0, concat_axis=0, tiled=True)
    received = lax.ppermute(second[:2], "tcol", swap(tcol_count, 1))
    far_second = lax.ppermute(second[2] + received[0], "tcol", swap(tcol_count, 2))
    far_second, sums = lax.optimization_barrier((far_second, sums))
    sums = jnp.sum(sums, axis=0)
    second = second[3] + received[1] + far_second

    norm, curvature, image_norm, image_curvature = sums[0], sums[1], sums[2], sums[3]
    step = norm / curvature
    norm_next = step * step * image_norm - norm
    ratio = norm_next / norm
    moved_curvature = step * (step * image_curvature - (1.0 + ratio) * image_norm)
    next_step = norm_next / moved_curvature
    residual = start - step * image
    direction = residual + ratio * start
    weights = step * start + next_step * direction
    residual = residual - next_step * ((1.0 + ratio) * image - step * second)
    out_shape = (1, 1, 1, piece, heads)
    return (gram.reshape(gram_prior.shape), weights.reshape(out_shape), residual.reshape(out_shape))


def solution(mesh):
    placed = (
        P("dp", "tcol", "trow", None),
        P("dp", None),
        P(None, "trow", "dp", None, "tcol"),
        P("tcol", "trow", "dp", None),
    )
    return jax.shard_map(
        shards,
        mesh=mesh,
        in_specs=placed,
        out_specs=(
            P(None, "trow", "dp", None, "tcol"),
            P("tcol", "trow", "dp", None, None),
            P("tcol", "trow", "dp", None, None),
        ),
        check_vma=False,
    )
```

```python
import functools
import math

import jax
import jax.numpy as jnp
import numpy as np
from jax import lax
from jax.experimental import pallas as pl
from jax.experimental.pallas import tpu as pltpu
from jax.sharding import PartitionSpec as P

NT = (((1,), (1,)), ((), ()))
NN = (((1,), (0,)), ((), ()))
VMEM = pl.BlockSpec(memory_space=pltpu.VMEM)
HBM = pl.BlockSpec(memory_space=pltpu.HBM)
EARLY_BYTES = 12 * 2**20
GRAM_BYTES = 10 * 2**20
IMAGE_BYTES = 10 * 2**20


def swap(count, bit):
    return [(place, place ^ bit) for place in range(count)]


class Ring:
    def __init__(self, data_count, trow_count):
        self.data_count = data_count
        self.count = data_count * trow_count
        self.cells = []
        for trow in range(trow_count):
            along = range(data_count) if trow % 2 == 0 else reversed(range(data_count))
            self.cells += [(data, trow) for data in along]
        flat = [data * trow_count + trow for data, trow in self.cells]
        self.ahead = [(flat[i], flat[(i + 1) % self.count]) for i in range(self.count)]
        self.back = [(target, source) for source, target in self.ahead]
        self.far = self.count // 2
        self.offsets = [0]
        for distance in range(1, self.far):
            self.offsets += [-distance, distance]
        self.offsets.append(self.far)
        self.place = np.zeros((data_count, trow_count), np.int32)
        for position, (data, trow) in enumerate(self.cells):
            self.place[data, trow] = position
        self.rounds = np.zeros((self.count, data_count), np.int32)
        self.chunk, self.trow, self.data = (np.zeros((self.count, self.count), np.int32) for _ in range(3))
        for position, (data, trow) in enumerate(self.cells):
            first = trow * data_count
            far_data = self.cells[(position + self.far) % self.count][0]
            near = sorted(
                range(first, first + data_count),
                key=lambda q: (self.cells[q][0] == far_data, abs(q - position), q),
            )
            chunk_of = {}
            for turn, other in enumerate(near):
                self.rounds[position, turn] = self.offsets.index(other - position)
                chunk_of[self.cells[other][0]] = turn
            for index, offset in enumerate(self.offsets):
                other_data, other_trow = self.cells[(position + offset) % self.count]
                self.chunk[position, index] = chunk_of[other_data]
                self.trow[position, index] = other_trow
                self.data[position, index] = other_data

    def move(self, ahead, back):
        axes = ("dp", "trow")
        return [lax.ppermute(ahead, axes, self.ahead), lax.ppermute(back, axes, self.back)]

    def last(self, ahead, back, rows, more=0):
        half = (rows // 2 + 15) // 16 * 16 + more
        return self.move(ahead[:half], back[half:rows])


ORDER = (3, 2, 1, 0)


def split(value):
    high = value.astype(jnp.bfloat16)
    return high, (value - high.astype(jnp.float32)).astype(jnp.bfloat16)


def dot(a, b, dims):
    return lax.dot_general(a, b, dims, preferred_element_type=jnp.float32)


def product(a, b):
    (a_high, a_low), (b_high, b_low) = a, b
    return dot(a_high, b_high, NN) + (dot(a_high, b_low, NN) + dot(a_low, b_high, NN))


def tile_copies(whole_ref, tile_ref, me, piece, block, semaphores):
    copies = []
    for start in range(0, tile_ref.shape[1], block):
        lanes = pl.ds(start, block)
        for index, j in enumerate(ORDER):
            place = pl.ds(pl.multiple_of(jnp.bitwise_xor(me, j) * piece, 8), piece)
            pair = whole_ref.at[place, lanes], tile_ref.at[pl.ds(index * piece, piece), lanes]
            copies.append(pltpu.make_async_copy(*pair, semaphores.at[len(copies)]))
    return copies


def fetch_kernel(sizes, meta, gram_ref, tile_ref, come):
    loads = tile_copies(gram_ref, tile_ref, meta[0], *sizes, come)
    for load in loads:
        load.start()
    for load in loads:
        load.wait()


def pick_rows(out_ref, head_ref, feature_ref, data_place, data_count, piece):
    head_part = head_ref.shape[0]
    out_ref[:head_part, :] = head_ref[...]
    if piece % 16 == 0:
        out_ref[head_part:, :] = feature_ref[pl.ds(pl.multiple_of(data_place * piece, 16), piece), :]
    else:
        for data in range(data_count):

            @pl.when(data_place == data)
            def _():
                out_ref[head_part:, :] = feature_ref[data * piece : (data + 1) * piece, :]


def pick_kernel(sizes, meta, *refs):
    turns, choices, width, piece, data_count = sizes
    *shard_refs, out_ref = refs
    for index, turn in enumerate(turns):
        for shard_ref, choice in zip(shard_refs, choices):

            @pl.when(meta[turn] == choice)
            def _():
                pick_rows(out_ref.at[index], shard_ref.at[width:], shard_ref, meta[data_count], data_count, piece)


def place_rows(round_refs, me, head_part, rows, target, turn, count):
    for group in range(len(round_refs) // 3):
        own, far, near = round_refs[3 * group : 3 * group + 3]
        for inner in range(own.shape[0]):
            lanes = slice(turn * count, (turn + 1) * count)
            parts = [near[1, inner], far[inner], near[0, inner], own[inner]]
            for j, part in zip(ORDER, parts):
                at = pl.multiple_of(jnp.bitwise_xor(me, j) * head_part, 16)
                target[pl.ds(at, head_part), lanes] = part[:head_part, :]
            rows[:, lanes] = jnp.concatenate([part[head_part:, :] for part in parts], axis=0)
            turn += 1


def early_kernel(sizes, meta, *refs):
    n, width, head_part, block, groups = sizes
    shard_refs, refs = refs[: n - 1], refs[n - 1 :]
    round_refs, refs = refs[: 3 * groups], refs[3 * groups :]
    prior_ref, now_ref, later_ref, side_ref, columns, rows, target = refs
    count = shard_refs[0].shape[1]
    for index in range(n - 1):
        lanes = pl.ds(pl.multiple_of(meta[index] * count, 128), count)
        base = pl.multiple_of(meta[n + index] * width, 16)
        columns[pl.ds(base, width), lanes] = shard_refs[index][:width, :]
    place_rows(round_refs, meta[2 * n], head_part, rows, target, 0, count)
    done = columns.shape[1] - count
    scale = 1.0 / columns.shape[1]
    for start in range(0, columns.shape[0], block):
        lanes = slice(start, start + block)
        column = columns[lanes, :done]
        value = prior_ref[:, lanes] + dot(rows[:, :done], column, NT) * scale
        now_ref[:, lanes], later_ref[:, lanes] = value[: now_ref.shape[0]], value[now_ref.shape[0] :]
        side_ref[lanes, :] = dot(column, target[:, :done], NT)


def tile_rows_of(first, early, last_rows, last_columns, block, scale, tile_ref, gram_ref, me, piece, stored):
    part = pl.ds(first * piece, tile_ref.shape[0])
    copies = []
    for start in range(0, tile_ref.shape[1], block):
        lanes = pl.ds(start, block)
        tile_ref[:, lanes] = early[:, lanes] + dot(last_rows[part, :], last_columns[lanes, :], NT) * scale
        for index in range(tile_ref.shape[0] // piece):
            place = pl.ds(pl.multiple_of(jnp.bitwise_xor(me, ORDER[first + index]) * piece, 8), piece)
            made = tile_ref.at[pl.ds(index * piece, piece), lanes]
            copies.append(pltpu.make_async_copy(made, gram_ref.at[place, lanes], stored.at[len(copies)]))
            copies[-1].start()
    return copies


def first_kernel(sizes, meta, *refs):
    n, piece, width, head_part, block = sizes
    low_ref, high_ref, *round_refs = refs[:5]
    early, early_side, columns, image_ref, gram_ref, tile_ref = refs[5:11]
    side_high, side_low, last_columns, last_rows, last_target, stored = refs[11:]
    total_rows, count = columns.shape[1], last_rows.shape[1]
    last_columns[...] = columns[:, total_rows - count :]
    base = pl.multiple_of(meta[2 * n - 1] * width, 16)
    half = low_ref.shape[0]
    last_columns[pl.ds(base, half), :] = low_ref[...]
    last_columns[pl.ds(pl.multiple_of(base + half, 16), width - half), :] = high_ref[...]
    place_rows(round_refs, meta[2 * n], head_part, last_rows, last_target, 0, count)
    scale = 1.0 / total_rows
    me = meta[2 * n]
    copies = tile_rows_of(0, early, last_rows, last_columns, block, scale, tile_ref, gram_ref, me, piece, stored)
    side = early_side[...] + dot(last_columns[...], last_target[...], NT)
    side_high[...], side_low[...] = split(side * scale)
    image_ref[...] = product(split(tile_ref[:piece, :]), (side_high[...], side_low[...]))
    for copy in copies:
        copy.wait()


def second_kernel(sizes, meta, *refs):
    tile_ref, last_rows, side_high, side_low, last_target, rows, target, right_ref, image_ref = refs
    piece = sizes
    total_rows, count = rows.shape[1], last_rows.shape[1]
    done = total_rows - count
    image_ref[...] = product(split(tile_ref[piece:, :]), (side_high[...], side_low[...]))
    own = slice(3 * piece, 4 * piece)
    right = dot(rows[own, :done], target[:, :done], NT) + dot(last_rows[own, :], last_target[...], NT)
    right_ref[...] = right * (1.0 / total_rows)


def third_kernel(sizes, meta, *refs):
    piece, block, total_rows = sizes
    early, last_columns, last_rows, side_high, side_low, _, gram_ref, image_ref, tile_ref, stored = refs
    scale = 1.0 / total_rows
    me = meta[0]
    copies = tile_rows_of(2, early, last_rows, last_columns, block, scale, tile_ref, gram_ref, me, piece, stored)
    value = product(split(tile_ref[...]), (side_high[...], side_low[...]))
    image_ref[...] = value.reshape(image_ref.shape)
    for copy in copies:
        copy.wait()


def weighted(parts, others):
    return sum(jnp.sum(a * b, axis=0, keepdims=True) for a, b in zip(parts, others))


def partial_kernel(sizes, meta, *refs):
    n, data_count, piece, block = sizes
    shard_refs = refs[: n - 1]
    tile_ref, start_ref, near_ref, far_ref, penalty_ref, total_ref, sums_ref, far_high, far_low, side = refs[n - 1 :]
    for index in range(n - 1):
        base = pl.multiple_of((meta[n + index] * data_count + meta[index]) * piece, 8)
        side[pl.ds(base, piece), :] = shard_refs[index][...]
    base = (meta[2 * n - 1] * data_count + meta[n - 1]) * piece
    side[pl.ds(pl.multiple_of(base, 8), piece), :] = jnp.zeros((piece, side.shape[1]), jnp.float32)
    total = product(split(tile_ref[...]), split(side[...]))
    own, start = shard_refs[0][...], start_ref[...]
    others = [near_ref[1], far_ref[...], near_ref[0], own]
    parts = [total[index * piece : (index + 1) * piece] for index in range(len(ORDER))]
    parts[-1] = parts[-1] + penalty_ref[...] * own
    for index, part in enumerate(parts):
        total_ref[index] = part
    sums = [weighted([a], [b]) for a, b in ((start, start), (start, own), (own, own))]
    sums_ref[...] = jnp.concatenate(sums + [weighted(parts, others)], axis=0)
    lanes = pl.ds(pl.multiple_of(base // block * block, 128), block)
    for place in range(block // piece):

        @pl.when(base % block == place * piece)
        def _():
            far_high[...], far_low[...] = split(tile_ref[:, lanes][:, place * piece : (place + 1) * piece])


def image_kernel(sizes, meta, *refs):
    piece = sizes
    low_ref, high_ref, total_ref, far_high, far_low, early_ref, own_ref, near_ref, far_ref, out_ref, sums_ref = refs
    side = jnp.concatenate([low_ref[...], high_ref[...]], axis=0)
    value = product((far_high[...], far_low[...]), split(side))
    others = [near_ref[1], far_ref[...], near_ref[0], own_ref[...]]
    parts = [value[index * piece : (index + 1) * piece] for index in range(len(ORDER))]
    early = early_ref[...]
    sums = jnp.concatenate([early[:3], early[3:] + weighted(parts, others)], axis=0)
    sums_ref[...] = jnp.broadcast_to(sums[None], sums_ref.shape)
    for index, j in enumerate(ORDER):
        out_ref[(3, 1, 2, 0).index(j)] = total_ref[index] + parts[index]


def call(body, meta, inputs, in_specs, out_specs, out_shape, scratch, vmem, flops, read, aliases={}):
    return pl.pallas_call(
        body,
        grid_spec=pltpu.PrefetchScalarGridSpec(
            num_scalar_prefetch=1,
            grid=(1,),
            in_specs=in_specs,
            out_specs=out_specs,
            scratch_shapes=scratch,
        ),
        out_shape=out_shape,
        input_output_aliases=aliases,
        compiler_params=pltpu.CompilerParams(vmem_limit_bytes=vmem),
        cost_estimate=pl.CostEstimate(flops=flops, bytes_accessed=read, transcendentals=0),
    )(meta, *inputs)


def shards(embeddings, targets, gram_prior, penalty):
    row_count = embeddings.shape[0]
    width = embeddings.shape[3]
    heads = targets.shape[1]
    data_count = lax.axis_size("dp")
    trow_count = lax.axis_size("trow")
    tcol_count = lax.axis_size("tcol")
    piece = width // data_count
    total_rows = row_count * data_count
    tile_rows = tcol_count * piece
    tile_columns = trow_count * width
    head_part = heads // tcol_count
    data_place = lax.axis_index("dp")
    me = lax.axis_index("tcol")
    ring = Ring(data_count, trow_count)
    n = ring.count
    position = jnp.asarray(ring.place)[data_place, lax.axis_index("trow")]
    lookup = np.concatenate([ring.rounds, ring.chunk, ring.trow, ring.data, ring.trow], axis=1)
    lookup = jnp.asarray(lookup)[position]
    pick_meta = jnp.concatenate([lookup[:data_count], jnp.reshape(data_place, (1,)).astype(jnp.int32)])
    me_meta = jnp.reshape(me, (1,)).astype(jnp.int32)
    gram_meta = jnp.concatenate([lookup[data_count : data_count + 2 * n], me_meta])
    image_meta = jnp.concatenate([lookup[data_count + 2 * n :], me_meta])

    f32, bf16 = jnp.float32, jnp.bfloat16
    features = embeddings.reshape(row_count, width).T
    head_rows = lax.dynamic_slice_in_dim(targets, me * head_part, head_part, axis=1).T
    payload = jnp.concatenate([features, head_rows], axis=0)

    def pieces_of(turns):
        if turns == [0]:
            own_rows = lax.dynamic_slice_in_dim(features, data_place * piece, piece, axis=0)
            return jnp.concatenate([head_rows, own_rows], axis=0)[None]
        choices = sorted(set(ring.rounds[:, turns].ravel().tolist()))
        return call(
            functools.partial(pick_kernel, (turns, choices, width, piece, data_count)),
            pick_meta,
            [gathered[choice] for choice in choices],
            [VMEM] * len(choices),
            VMEM,
            jax.ShapeDtypeStruct((len(turns), head_part + piece, row_count), payload.dtype),
            [],
            2**20,
            0,
            4 * len(turns) * (head_part + piece) * row_count,
        )

    split_turns = [[0], list(range(1, data_count - 1)), [data_count - 1]]
    ready = [int(np.abs(np.asarray(ring.offsets)[ring.rounds[:, turns]]).max()) for turns in split_turns]
    gathered, groups, waiting = [payload], {}, []

    def near_of(group, mine, far):
        groups[group] = [mine, far, lax.ppermute(jnp.stack([mine, far]), "tcol", swap(tcol_count, 1))]

    def open_groups(step):
        for group, (turns, when) in enumerate(zip(split_turns, ready)):
            if when == step:
                mine = pieces_of(turns)
                waiting.append((group, mine, lax.ppermute(mine, "tcol", swap(tcol_count, 2))))

    block = next(size for size in (512, 256, 128) if tile_columns % size == 0)
    far_block = math.lcm(piece, 128)
    tile_semaphores = pltpu.SemaphoreType.DMA((tcol_count * (tile_columns // block),))

    def fetch(whole):
        return call(
            functools.partial(fetch_kernel, (piece, block)),
            me_meta,
            [whole],
            [HBM],
            VMEM,
            jax.ShapeDtypeStruct((tile_rows, tile_columns), f32),
            [tile_semaphores],
            2**20,
            0,
            8 * tile_rows * tile_columns,
        )

    prior = gram_prior.reshape(tile_rows, tile_columns)
    open_groups(0)
    ahead = back = payload
    for step in range(1, ring.far + 1):
        if step < ring.far:
            arrived = ahead, back = ring.move(ahead, back)
        else:
            arrived = ring.last(ahead, back, width)
        if step == 1:
            gram_meta, image_meta, pick_meta, *arrived = lax.optimization_barrier(
                (gram_meta, image_meta, pick_meta, *arrived)
            )
        if step == ring.far - 2:
            prior, *arrived = lax.optimization_barrier((prior, *arrived))
            prior = fetch(prior)
        if step == ring.far - 1:
            prior, *arrived = lax.optimization_barrier((prior, *arrived))
        while waiting:
            group, mine, far = waiting.pop()
            if step == ring.far:
                early, mine, far, *arrived = lax.optimization_barrier((early, mine, far, *arrived))
            else:
                mine, far, *arrived = lax.optimization_barrier((mine, far, *arrived))
            near_of(group, mine, far)
        gathered += arrived
        open_groups(step)
        if step == ring.far - 1:
            early, early_later, early_side, columns, rows, target = call(
                functools.partial(early_kernel, (n, width, head_part, block, 2)),
                gram_meta,
                [*gathered, *groups[0], *groups[1], prior],
                [VMEM] * (n + 6),
                [VMEM] * 6,
                [
                    jax.ShapeDtypeStruct((2 * piece, tile_columns), f32),
                    jax.ShapeDtypeStruct((2 * piece, tile_columns), f32),
                    jax.ShapeDtypeStruct((tile_columns, heads), f32),
                    jax.ShapeDtypeStruct((tile_columns, total_rows), bf16),
                    jax.ShapeDtypeStruct((tile_rows, total_rows), bf16),
                    jax.ShapeDtypeStruct((heads, total_rows), bf16),
                ],
                [],
                EARLY_BYTES,
                2 * tile_rows * tile_columns * (total_rows - row_count),
                8 * tile_rows * tile_columns,
            )
    gram_shape = jax.ShapeDtypeStruct((tile_rows, tile_columns), f32)
    piece_shape = jax.ShapeDtypeStruct((piece, heads), f32)

    def tile_scratch(pieces):
        shape = (pieces * piece, tile_columns)
        return [pltpu.VMEM(shape, f32), pltpu.SemaphoreType.DMA((pieces * (tile_columns // block),))]

    sent, gram, first_tile, side_high, side_low, last_columns, last_rows, last_target = call(
        functools.partial(first_kernel, (n, piece, width, head_part, block)),
        gram_meta,
        [*gathered[-2:], *groups[2], early, early_side, columns],
        [VMEM] * 8,
        [VMEM, HBM] + [VMEM] * 6,
        [
            piece_shape,
            gram_shape,
            jax.ShapeDtypeStruct((2 * piece, tile_columns), f32),
            jax.ShapeDtypeStruct((tile_columns, heads), bf16),
            jax.ShapeDtypeStruct((tile_columns, heads), bf16),
            jax.ShapeDtypeStruct((tile_columns, row_count), bf16),
            jax.ShapeDtypeStruct((tile_rows, row_count), bf16),
            jax.ShapeDtypeStruct((heads, row_count), bf16),
        ],
        tile_scratch(2)[1:],
        GRAM_BYTES,
        2 * piece * tile_columns * (2 * row_count + 3 * heads),
        16 * piece * tile_columns,
    )
    penalty_rows = penalty.reshape(piece, 1)
    received = lax.ppermute(sent, "tcol", swap(tcol_count, 1))
    start, far_part = call(
        functools.partial(second_kernel, piece),
        me_meta,
        [first_tile, last_rows, side_high, side_low, last_target, rows, target],
        [VMEM] * 7,
        [VMEM, VMEM],
        [piece_shape, piece_shape],
        [],
        GRAM_BYTES,
        6 * piece * tile_columns * heads,
        4 * piece * tile_columns,
    )
    far_part, early_later = lax.optimization_barrier((far_part + received, early_later))
    far_sum = lax.ppermute(far_part, "tcol", swap(tcol_count, 2))
    gram, kept = call(
        functools.partial(third_kernel, (piece, block, total_rows)),
        me_meta,
        [early_later, last_columns, last_rows, side_high, side_low, gram],
        [VMEM] * 5 + [HBM],
        [HBM, VMEM],
        [gram_shape, jax.ShapeDtypeStruct((2, piece, heads), f32)],
        tile_scratch(2),
        GRAM_BYTES,
        4 * piece * tile_columns * (row_count + 3 * heads),
        16 * piece * tile_columns,
        {6: 0},
    )
    halves = [kept[0][: piece // 2], kept[0][piece // 2 :]]
    near_sum = jnp.concatenate([lax.ppermute(part, "tcol", swap(tcol_count, 1)) for part in halves], axis=0)
    image = kept[1] + near_sum + penalty_rows * start + far_sum
    far_image = lax.ppermute(image, "tcol", swap(tcol_count, 2))
    near_images = lax.ppermute(jnp.stack([image, far_image]), "tcol", swap(tcol_count, 1))
    images = [image]
    ahead = back = image
    for step in range(1, ring.far + 1):
        if step < ring.far:
            arrived = ahead, back = ring.move(ahead, back)
        else:
            arrived = ring.last(ahead, back, piece, piece // 6 // 16 * 16)
        if step == ring.far - 2:
            *arrived, gram = lax.optimization_barrier((*arrived, gram))
            tile = fetch(gram)
        if step == ring.far - 1:
            *arrived, tile = lax.optimization_barrier((*arrived, tile))
        images += arrived
    part_shape = jax.ShapeDtypeStruct((tcol_count, piece, heads), f32)
    far_shape = jax.ShapeDtypeStruct((tile_rows, piece), bf16)
    total, early_sums, far_high, far_low = call(
        functools.partial(partial_kernel, (n, data_count, piece, far_block)),
        image_meta,
        [*images[:-2], tile, start, near_images, far_image, penalty_rows],
        [VMEM] * (n + 4),
        [VMEM] * 4,
        [part_shape, jax.ShapeDtypeStruct((4, heads), f32), far_shape, far_shape],
        [pltpu.VMEM((tile_columns, heads), f32)],
        IMAGE_BYTES,
        6 * tile_rows * tile_columns * heads,
        4 * tile_rows * tile_columns,
    )
    axes = ("dp", "trow", "tcol")
    second, sums = call(
        functools.partial(image_kernel, piece),
        image_meta,
        [*images[-2:], total, far_high, far_low, early_sums, image, near_images, far_image],
        [VMEM] * 9,
        [VMEM] * 2,
        [part_shape, jax.ShapeDtypeStruct((n * tcol_count, 4, heads), f32)],
        [],
        IMAGE_BYTES,
        6 * tile_rows * piece * heads,
        4 * tile_rows * piece,
    )
    sums, second = lax.optimization_barrier((sums, second))
    sums = lax.all_to_all(sums, axes, split_axis=0, concat_axis=0, tiled=True)
    received = lax.ppermute(second[:2], "tcol", swap(tcol_count, 1))
    far_second = lax.ppermute(second[2] + received[0], "tcol", swap(tcol_count, 2))
    far_second, sums = lax.optimization_barrier((far_second, sums))
    sums = jnp.sum(sums, axis=0)
    second = second[3] + received[1] + far_second

    norm, curvature, image_norm, image_curvature = sums[0], sums[1], sums[2], sums[3]
    step = norm / curvature
    norm_next = step * step * image_norm - norm
    ratio = norm_next / norm
    moved_curvature = step * (step * image_curvature - (1.0 + ratio) * image_norm)
    next_step = norm_next / moved_curvature
    residual = start - step * image
    direction = residual + ratio * start
    weights = step * start + next_step * direction
    residual = residual - next_step * ((1.0 + ratio) * image - step * second)
    out_shape = (1, 1, 1, piece, heads)
    return (gram.reshape(gram_prior.shape), weights.reshape(out_shape), residual.reshape(out_shape))


def solution(mesh):
    placed = (
        P("dp", "tcol", "trow", None),
        P("dp", None),
        P(None, "trow", "dp", None, "tcol"),
        P("tcol", "trow", "dp", None),
    )
    return jax.shard_map(
        shards,
        mesh=mesh,
        in_specs=placed,
        out_specs=(
            P(None, "trow", "dp", None, "tcol"),
            P("tcol", "trow", "dp", None, None),
            P("tcol", "trow", "dp", None, None),
        ),
        check_vma=False,
    )
```

```python
import functools
import math

import jax
import jax.numpy as jnp
import numpy as np
from jax import lax
from jax.experimental import pallas as pl
from jax.experimental.pallas import tpu as pltpu
from jax.sharding import PartitionSpec as P

NT = (((1,), (1,)), ((), ()))
NN = (((1,), (0,)), ((), ()))
VMEM = pl.BlockSpec(memory_space=pltpu.VMEM)
HBM = pl.BlockSpec(memory_space=pltpu.HBM)
EARLY_BYTES = 12 * 2**20
GRAM_BYTES = 10 * 2**20
IMAGE_BYTES = 10 * 2**20


def swap(count, bit):
    return [(place, place ^ bit) for place in range(count)]


class Ring:
    def __init__(self, data_count, trow_count):
        self.data_count = data_count
        self.count = data_count * trow_count
        self.cells = []
        for trow in range(trow_count):
            along = range(data_count) if trow % 2 == 0 else reversed(range(data_count))
            self.cells += [(data, trow) for data in along]
        flat = [data * trow_count + trow for data, trow in self.cells]
        self.ahead = [(flat[i], flat[(i + 1) % self.count]) for i in range(self.count)]
        self.back = [(target, source) for source, target in self.ahead]
        self.far = self.count // 2
        self.offsets = [0]
        for distance in range(1, self.far):
            self.offsets += [-distance, distance]
        self.offsets.append(self.far)
        self.place = np.zeros((data_count, trow_count), np.int32)
        for position, (data, trow) in enumerate(self.cells):
            self.place[data, trow] = position
        self.rounds = np.zeros((self.count, data_count), np.int32)
        self.chunk, self.trow, self.data = (np.zeros((self.count, self.count), np.int32) for _ in range(3))
        for position, (data, trow) in enumerate(self.cells):
            first = trow * data_count
            far_data = self.cells[(position + self.far) % self.count][0]
            near = sorted(
                range(first, first + data_count),
                key=lambda q: (self.cells[q][0] == far_data, abs(q - position), q),
            )
            chunk_of = {}
            for turn, other in enumerate(near):
                self.rounds[position, turn] = self.offsets.index(other - position)
                chunk_of[self.cells[other][0]] = turn
            for index, offset in enumerate(self.offsets):
                other_data, other_trow = self.cells[(position + offset) % self.count]
                self.chunk[position, index] = chunk_of[other_data]
                self.trow[position, index] = other_trow
                self.data[position, index] = other_data

    def move(self, ahead, back):
        axes = ("dp", "trow")
        return [lax.ppermute(ahead, axes, self.ahead), lax.ppermute(back, axes, self.back)]

    def last(self, ahead, back, rows, more=0):
        half = (rows // 2 + 15) // 16 * 16 + more
        return self.move(ahead[:half], back[half:rows])


ORDER = (3, 2, 1, 0)


def split(value):
    high = value.astype(jnp.bfloat16)
    return high, (value - high.astype(jnp.float32)).astype(jnp.bfloat16)


def dot(a, b, dims):
    return lax.dot_general(a, b, dims, preferred_element_type=jnp.float32)


def product(a, b):
    (a_high, a_low), (b_high, b_low) = a, b
    return dot(a_high, b_high, NN) + (dot(a_high, b_low, NN) + dot(a_low, b_high, NN))


def tile_copies(whole_ref, tile_ref, me, piece, block, semaphores):
    copies = []
    for start in range(0, tile_ref.shape[1], block):
        lanes = pl.ds(start, block)
        for index, j in enumerate(ORDER):
            place = pl.ds(pl.multiple_of(jnp.bitwise_xor(me, j) * piece, 8), piece)
            pair = whole_ref.at[place, lanes], tile_ref.at[pl.ds(index * piece, piece), lanes]
            copies.append(pltpu.make_async_copy(*pair, semaphores.at[len(copies)]))
    return copies


def fetch_kernel(sizes, meta, gram_ref, tile_ref, come):
    loads = tile_copies(gram_ref, tile_ref, meta[0], *sizes, come)
    for load in loads:
        load.start()
    for load in loads:
        load.wait()


def pick_rows(out_ref, head_ref, feature_ref, data_place, data_count, piece):
    head_part = head_ref.shape[0]
    out_ref[:head_part, :] = head_ref[...]
    if piece % 16 == 0:
        out_ref[head_part:, :] = feature_ref[pl.ds(pl.multiple_of(data_place * piece, 16), piece), :]
    else:
        for data in range(data_count):

            @pl.when(data_place == data)
            def _():
                out_ref[head_part:, :] = feature_ref[data * piece : (data + 1) * piece, :]


def pick_kernel(sizes, meta, *refs):
    turns, choices, width, piece, data_count = sizes
    *shard_refs, out_ref = refs
    for index, turn in enumerate(turns):
        for shard_ref, choice in zip(shard_refs, choices):

            @pl.when(meta[turn] == choice)
            def _():
                pick_rows(out_ref.at[index], shard_ref.at[width:], shard_ref, meta[data_count], data_count, piece)


def place_rows(round_refs, me, head_part, rows, target, turn, count):
    for group in range(len(round_refs) // 3):
        own, far, near = round_refs[3 * group : 3 * group + 3]
        for inner in range(own.shape[0]):
            lanes = slice(turn * count, (turn + 1) * count)
            parts = [near[1, inner], far[inner], near[0, inner], own[inner]]
            for j, part in zip(ORDER, parts):
                at = pl.multiple_of(jnp.bitwise_xor(me, j) * head_part, 16)
                target[pl.ds(at, head_part), lanes] = part[:head_part, :]
            rows[:, lanes] = jnp.concatenate([part[head_part:, :] for part in parts], axis=0)
            turn += 1


def early_kernel(sizes, meta, *refs):
    n, width, head_part, block, groups = sizes
    shard_refs, refs = refs[: n - 1], refs[n - 1 :]
    round_refs, refs = refs[: 3 * groups], refs[3 * groups :]
    prior_ref, now_ref, later_ref, columns, rows, target = refs
    count = shard_refs[0].shape[1]
    for index in range(n - 1):
        lanes = pl.ds(pl.multiple_of(meta[index] * count, 128), count)
        base = pl.multiple_of(meta[n + index] * width, 16)
        columns[pl.ds(base, width), lanes] = shard_refs[index][:width, :]
    place_rows(round_refs, meta[2 * n], head_part, rows, target, 0, count)
    done = columns.shape[1] - count
    scale = 1.0 / columns.shape[1]
    for start in range(0, columns.shape[0], block):
        lanes = slice(start, start + block)
        column = columns[lanes, :done]
        value = prior_ref[:, lanes] + dot(rows[:, :done], column, NT) * scale
        now_ref[:, lanes], later_ref[:, lanes] = value[: now_ref.shape[0]], value[now_ref.shape[0] :]


def rest_kernel(sizes, meta, low_ref, high_ref, columns, target, side_ref, last_columns):
    n, width, block = sizes
    done = columns.shape[1] - last_columns.shape[1]
    last_columns[...] = columns[:, done:]
    base = pl.multiple_of(meta[2 * n - 1] * width, 16)
    half = low_ref.shape[0]
    last_columns[pl.ds(base, half), :] = low_ref[...]
    last_columns[pl.ds(pl.multiple_of(base + half, 16), width - half), :] = high_ref[...]
    for start in range(0, columns.shape[0], block):
        lanes = slice(start, start + block)
        side_ref[lanes, :] = dot(columns[lanes, :done], target[:, :done], NT)


def tile_rows_of(first, early, last_rows, last_columns, block, scale, tile_ref, gram_ref, me, piece, stored):
    part = pl.ds(first * piece, tile_ref.shape[0])
    copies = []
    for start in range(0, tile_ref.shape[1], block):
        lanes = pl.ds(start, block)
        tile_ref[:, lanes] = early[:, lanes] + dot(last_rows[part, :], last_columns[lanes, :], NT) * scale
        for index in range(tile_ref.shape[0] // piece):
            place = pl.ds(pl.multiple_of(jnp.bitwise_xor(me, ORDER[first + index]) * piece, 8), piece)
            made = tile_ref.at[pl.ds(index * piece, piece), lanes]
            copies.append(pltpu.make_async_copy(made, gram_ref.at[place, lanes], stored.at[len(copies)]))
            copies[-1].start()
    return copies


def first_kernel(sizes, meta, *refs):
    n, piece, total_rows, head_part, block = sizes
    round_refs = refs[:3]
    early, early_side, last_columns, image_ref, gram_ref, tile_ref = refs[3:9]
    side_high, side_low, last_rows, last_target, stored = refs[9:]
    count = last_rows.shape[1]
    place_rows(round_refs, meta[2 * n], head_part, last_rows, last_target, 0, count)
    scale = 1.0 / total_rows
    me = meta[2 * n]
    copies = tile_rows_of(0, early, last_rows, last_columns, block, scale, tile_ref, gram_ref, me, piece, stored)
    side = early_side[...] + dot(last_columns[...], last_target[...], NT)
    side_high[...], side_low[...] = split(side * scale)
    image_ref[...] = product(split(tile_ref[:piece, :]), (side_high[...], side_low[...]))
    for copy in copies:
        copy.wait()


def second_kernel(sizes, meta, *refs):
    tile_ref, last_rows, side_high, side_low, last_target, rows, target, right_ref, image_ref = refs
    piece = sizes
    total_rows, count = rows.shape[1], last_rows.shape[1]
    done = total_rows - count
    image_ref[...] = product(split(tile_ref[piece:, :]), (side_high[...], side_low[...]))
    own = slice(3 * piece, 4 * piece)
    right = dot(rows[own, :done], target[:, :done], NT) + dot(last_rows[own, :], last_target[...], NT)
    right_ref[...] = right * (1.0 / total_rows)


def third_kernel(sizes, meta, *refs):
    piece, block, total_rows = sizes
    early, last_columns, last_rows, side_high, side_low, _, gram_ref, image_ref, tile_ref, stored = refs
    scale = 1.0 / total_rows
    me = meta[0]
    copies = tile_rows_of(2, early, last_rows, last_columns, block, scale, tile_ref, gram_ref, me, piece, stored)
    value = product(split(tile_ref[...]), (side_high[...], side_low[...]))
    image_ref[...] = value.reshape(image_ref.shape)
    for copy in copies:
        copy.wait()


def weighted(parts, others):
    return sum(jnp.sum(a * b, axis=0, keepdims=True) for a, b in zip(parts, others))


def partial_kernel(sizes, meta, *refs):
    n, data_count, piece, block = sizes
    shard_refs = refs[: n - 1]
    tile_ref, start_ref, near_ref, far_ref, penalty_ref, total_ref, sums_ref, far_high, far_low, side = refs[n - 1 :]
    for index in range(n - 1):
        base = pl.multiple_of((meta[n + index] * data_count + meta[index]) * piece, 8)
        side[pl.ds(base, piece), :] = shard_refs[index][...]
    base = (meta[2 * n - 1] * data_count + meta[n - 1]) * piece
    side[pl.ds(pl.multiple_of(base, 8), piece), :] = jnp.zeros((piece, side.shape[1]), jnp.float32)
    total = product(split(tile_ref[...]), split(side[...]))
    own, start = shard_refs[0][...], start_ref[...]
    others = [near_ref[1], far_ref[...], near_ref[0], own]
    parts = [total[index * piece : (index + 1) * piece] for index in range(len(ORDER))]
    parts[-1] = parts[-1] + penalty_ref[...] * own
    for index, part in enumerate(parts):
        total_ref[index] = part
    sums = [weighted([a], [b]) for a, b in ((start, start), (start, own), (own, own))]
    sums_ref[...] = jnp.concatenate(sums + [weighted(parts, others)], axis=0)
    lanes = pl.ds(pl.multiple_of(base // block * block, 128), block)
    for place in range(block // piece):

        @pl.when(base % block == place * piece)
        def _():
            far_high[...], far_low[...] = split(tile_ref[:, lanes][:, place * piece : (place + 1) * piece])


def image_kernel(sizes, meta, *refs):
    piece = sizes
    low_ref, high_ref, total_ref, far_high, far_low, early_ref, own_ref, near_ref, far_ref, out_ref, sums_ref = refs
    side = jnp.concatenate([low_ref[...], high_ref[...]], axis=0)
    value = product((far_high[...], far_low[...]), split(side))
    others = [near_ref[1], far_ref[...], near_ref[0], own_ref[...]]
    parts = [value[index * piece : (index + 1) * piece] for index in range(len(ORDER))]
    early = early_ref[...]
    sums = jnp.concatenate([early[:3], early[3:] + weighted(parts, others)], axis=0)
    sums_ref[...] = jnp.broadcast_to(sums[None], sums_ref.shape)
    for index, j in enumerate(ORDER):
        out_ref[(3, 1, 2, 0).index(j)] = total_ref[index] + parts[index]


def call(body, meta, inputs, in_specs, out_specs, out_shape, scratch, vmem, flops, read, aliases={}):
    return pl.pallas_call(
        body,
        grid_spec=pltpu.PrefetchScalarGridSpec(
            num_scalar_prefetch=1,
            grid=(1,),
            in_specs=in_specs,
            out_specs=out_specs,
            scratch_shapes=scratch,
        ),
        out_shape=out_shape,
        input_output_aliases=aliases,
        compiler_params=pltpu.CompilerParams(vmem_limit_bytes=vmem),
        cost_estimate=pl.CostEstimate(flops=flops, bytes_accessed=read, transcendentals=0),
    )(meta, *inputs)


def shards(embeddings, targets, gram_prior, penalty):
    row_count = embeddings.shape[0]
    width = embeddings.shape[3]
    heads = targets.shape[1]
    data_count = lax.axis_size("dp")
    trow_count = lax.axis_size("trow")
    tcol_count = lax.axis_size("tcol")
    piece = width // data_count
    total_rows = row_count * data_count
    tile_rows = tcol_count * piece
    tile_columns = trow_count * width
    head_part = heads // tcol_count
    data_place = lax.axis_index("dp")
    me = lax.axis_index("tcol")
    ring = Ring(data_count, trow_count)
    n = ring.count
    position = jnp.asarray(ring.place)[data_place, lax.axis_index("trow")]
    lookup = np.concatenate([ring.rounds, ring.chunk, ring.trow, ring.data, ring.trow], axis=1)
    lookup = jnp.asarray(lookup)[position]
    pick_meta = jnp.concatenate([lookup[:data_count], jnp.reshape(data_place, (1,)).astype(jnp.int32)])
    me_meta = jnp.reshape(me, (1,)).astype(jnp.int32)
    gram_meta = jnp.concatenate([lookup[data_count : data_count + 2 * n], me_meta])
    image_meta = jnp.concatenate([lookup[data_count + 2 * n :], me_meta])

    f32, bf16 = jnp.float32, jnp.bfloat16
    features = embeddings.reshape(row_count, width).T
    head_rows = lax.dynamic_slice_in_dim(targets, me * head_part, head_part, axis=1).T
    payload = jnp.concatenate([features, head_rows], axis=0)

    def pieces_of(turns):
        if turns == [0]:
            own_rows = lax.dynamic_slice_in_dim(features, data_place * piece, piece, axis=0)
            return jnp.concatenate([head_rows, own_rows], axis=0)[None]
        choices = sorted(set(ring.rounds[:, turns].ravel().tolist()))
        return call(
            functools.partial(pick_kernel, (turns, choices, width, piece, data_count)),
            pick_meta,
            [gathered[choice] for choice in choices],
            [VMEM] * len(choices),
            VMEM,
            jax.ShapeDtypeStruct((len(turns), head_part + piece, row_count), payload.dtype),
            [],
            2**20,
            0,
            4 * len(turns) * (head_part + piece) * row_count,
        )

    split_turns = [[0], list(range(1, data_count - 1)), [data_count - 1]]
    ready = [int(np.abs(np.asarray(ring.offsets)[ring.rounds[:, turns]]).max()) for turns in split_turns]
    gathered, groups, waiting = [payload], {}, []

    def near_of(group, mine, far):
        groups[group] = [mine, far, lax.ppermute(jnp.stack([mine, far]), "tcol", swap(tcol_count, 1))]

    def open_groups(step):
        for group, (turns, when) in enumerate(zip(split_turns, ready)):
            if when == step:
                mine = pieces_of(turns)
                waiting.append((group, mine, lax.ppermute(mine, "tcol", swap(tcol_count, 2))))

    block = next(size for size in (512, 256, 128) if tile_columns % size == 0)
    far_block = math.lcm(piece, 128)
    tile_semaphores = pltpu.SemaphoreType.DMA((tcol_count * (tile_columns // block),))

    def fetch(whole):
        return call(
            functools.partial(fetch_kernel, (piece, block)),
            me_meta,
            [whole],
            [HBM],
            VMEM,
            jax.ShapeDtypeStruct((tile_rows, tile_columns), f32),
            [tile_semaphores],
            2**20,
            0,
            8 * tile_rows * tile_columns,
        )

    prior = gram_prior.reshape(tile_rows, tile_columns)
    open_groups(0)
    ahead = back = payload
    for step in range(1, ring.far + 1):
        if step < ring.far:
            arrived = ahead, back = ring.move(ahead, back)
        else:
            arrived = ring.last(ahead, back, width)
        if step == 1:
            gram_meta, image_meta, pick_meta, *arrived = lax.optimization_barrier(
                (gram_meta, image_meta, pick_meta, *arrived)
            )
        if step == ring.far - 2:
            prior, *arrived = lax.optimization_barrier((prior, *arrived))
            prior = fetch(prior)
        if step == ring.far - 1:
            prior, *arrived = lax.optimization_barrier((prior, *arrived))
        while waiting:
            group, mine, far = waiting.pop()
            if step == ring.far:
                early, mine, far, *arrived = lax.optimization_barrier((early, mine, far, *arrived))
            else:
                mine, far, *arrived = lax.optimization_barrier((mine, far, *arrived))
            near_of(group, mine, far)
        gathered += arrived
        open_groups(step)
        if step == ring.far - 1:
            early, early_later, columns, rows, target = call(
                functools.partial(early_kernel, (n, width, head_part, block, 2)),
                gram_meta,
                [*gathered, *groups[0], *groups[1], prior],
                [VMEM] * (n + 6),
                [VMEM] * 5,
                [
                    jax.ShapeDtypeStruct((2 * piece, tile_columns), f32),
                    jax.ShapeDtypeStruct((2 * piece, tile_columns), f32),
                    jax.ShapeDtypeStruct((tile_columns, total_rows), bf16),
                    jax.ShapeDtypeStruct((tile_rows, total_rows), bf16),
                    jax.ShapeDtypeStruct((heads, total_rows), bf16),
                ],
                [],
                EARLY_BYTES,
                2 * tile_rows * tile_columns * (total_rows - row_count),
                8 * tile_rows * tile_columns,
            )
    gram_shape = jax.ShapeDtypeStruct((tile_rows, tile_columns), f32)
    piece_shape = jax.ShapeDtypeStruct((piece, heads), f32)

    def tile_scratch(pieces):
        shape = (pieces * piece, tile_columns)
        return [pltpu.VMEM(shape, f32), pltpu.SemaphoreType.DMA((pieces * (tile_columns // block),))]

    early_side, last_columns = call(
        functools.partial(rest_kernel, (n, width, block)),
        gram_meta,
        [*gathered[-2:], columns, target],
        [VMEM] * 4,
        [VMEM] * 2,
        [
            jax.ShapeDtypeStruct((tile_columns, heads), f32),
            jax.ShapeDtypeStruct((tile_columns, row_count), bf16),
        ],
        [],
        EARLY_BYTES,
        2 * tile_columns * heads * (total_rows - row_count),
        2 * tile_columns * total_rows,
    )
    sent, gram, first_tile, side_high, side_low, last_rows, last_target = call(
        functools.partial(first_kernel, (n, piece, total_rows, head_part, block)),
        gram_meta,
        [*groups[2], early, early_side, last_columns],
        [VMEM] * 6,
        [VMEM, HBM] + [VMEM] * 5,
        [
            piece_shape,
            gram_shape,
            jax.ShapeDtypeStruct((2 * piece, tile_columns), f32),
            jax.ShapeDtypeStruct((tile_columns, heads), bf16),
            jax.ShapeDtypeStruct((tile_columns, heads), bf16),
            jax.ShapeDtypeStruct((tile_rows, row_count), bf16),
            jax.ShapeDtypeStruct((heads, row_count), bf16),
        ],
        tile_scratch(2)[1:],
        GRAM_BYTES,
        2 * piece * tile_columns * (2 * row_count + 3 * heads),
        16 * piece * tile_columns,
    )
    penalty_rows = penalty.reshape(piece, 1)
    received = lax.ppermute(sent, "tcol", swap(tcol_count, 1))
    start, far_part = call(
        functools.partial(second_kernel, piece),
        me_meta,
        [first_tile, last_rows, side_high, side_low, last_target, rows, target],
        [VMEM] * 7,
        [VMEM, VMEM],
        [piece_shape, piece_shape],
        [],
        GRAM_BYTES,
        6 * piece * tile_columns * heads,
        4 * piece * tile_columns,
    )
    far_part, early_later = lax.optimization_barrier((far_part + received, early_later))
    far_sum = lax.ppermute(far_part, "tcol", swap(tcol_count, 2))
    gram, kept = call(
        functools.partial(third_kernel, (piece, block, total_rows)),
        me_meta,
        [early_later, last_columns, last_rows, side_high, side_low, gram],
        [VMEM] * 5 + [HBM],
        [HBM, VMEM],
        [gram_shape, jax.ShapeDtypeStruct((2, piece, heads), f32)],
        tile_scratch(2),
        GRAM_BYTES,
        4 * piece * tile_columns * (row_count + 3 * heads),
        16 * piece * tile_columns,
        {6: 0},
    )
    halves = [kept[0][: piece // 2], kept[0][piece // 2 :]]
    near_sum = jnp.concatenate([lax.ppermute(part, "tcol", swap(tcol_count, 1)) for part in halves], axis=0)
    image = kept[1] + near_sum + penalty_rows * start + far_sum
    far_image = lax.ppermute(image, "tcol", swap(tcol_count, 2))
    near_images = lax.ppermute(jnp.stack([image, far_image]), "tcol", swap(tcol_count, 1))
    images = [image]
    ahead = back = image
    for step in range(1, ring.far + 1):
        if step < ring.far:
            arrived = ahead, back = ring.move(ahead, back)
        else:
            arrived = ring.last(ahead, back, piece, piece // 6 // 16 * 16)
        if step == ring.far - 2:
            *arrived, gram = lax.optimization_barrier((*arrived, gram))
            tile = fetch(gram)
        if step == ring.far - 1:
            *arrived, tile = lax.optimization_barrier((*arrived, tile))
        images += arrived
    part_shape = jax.ShapeDtypeStruct((tcol_count, piece, heads), f32)
    far_shape = jax.ShapeDtypeStruct((tile_rows, piece), bf16)
    total, early_sums, far_high, far_low = call(
        functools.partial(partial_kernel, (n, data_count, piece, far_block)),
        image_meta,
        [*images[:-2], tile, start, near_images, far_image, penalty_rows],
        [VMEM] * (n + 4),
        [VMEM] * 4,
        [part_shape, jax.ShapeDtypeStruct((4, heads), f32), far_shape, far_shape],
        [pltpu.VMEM((tile_columns, heads), f32)],
        IMAGE_BYTES,
        6 * tile_rows * tile_columns * heads,
        4 * tile_rows * tile_columns,
    )
    axes = ("dp", "trow", "tcol")
    second, sums = call(
        functools.partial(image_kernel, piece),
        image_meta,
        [*images[-2:], total, far_high, far_low, early_sums, image, near_images, far_image],
        [VMEM] * 9,
        [VMEM] * 2,
        [part_shape, jax.ShapeDtypeStruct((n * tcol_count, 4, heads), f32)],
        [],
        IMAGE_BYTES,
        6 * tile_rows * piece * heads,
        4 * tile_rows * piece,
    )
    sums, second = lax.optimization_barrier((sums, second))
    sums = lax.all_to_all(sums, axes, split_axis=0, concat_axis=0, tiled=True)
    received = lax.ppermute(second[:2], "tcol", swap(tcol_count, 1))
    far_second = lax.ppermute(second[2] + received[0], "tcol", swap(tcol_count, 2))
    far_second, sums = lax.optimization_barrier((far_second, sums))
    sums = jnp.sum(sums, axis=0)
    second = second[3] + received[1] + far_second

    norm, curvature, image_norm, image_curvature = sums[0], sums[1], sums[2], sums[3]
    step = norm / curvature
    norm_next = step * step * image_norm - norm
    ratio = norm_next / norm
    moved_curvature = step * (step * image_curvature - (1.0 + ratio) * image_norm)
    next_step = norm_next / moved_curvature
    residual = start - step * image
    direction = residual + ratio * start
    weights = step * start + next_step * direction
    residual = residual - next_step * ((1.0 + ratio) * image - step * second)
    out_shape = (1, 1, 1, piece, heads)
    return (gram.reshape(gram_prior.shape), weights.reshape(out_shape), residual.reshape(out_shape))


def solution(mesh):
    placed = (
        P("dp", "tcol", "trow", None),
        P("dp", None),
        P(None, "trow", "dp", None, "tcol"),
        P("tcol", "trow", "dp", None),
    )
    return jax.shard_map(
        shards,
        mesh=mesh,
        in_specs=placed,
        out_specs=(
            P(None, "trow", "dp", None, "tcol"),
            P("tcol", "trow", "dp", None, None),
            P("tcol", "trow", "dp", None, None),
        ),
        check_vma=False,
    )
```

```python
import functools
import math

import jax
import jax.numpy as jnp
import numpy as np
from jax import lax
from jax.experimental import pallas as pl
from jax.experimental.pallas import tpu as pltpu
from jax.sharding import PartitionSpec as P

NT = (((1,), (1,)), ((), ()))
NN = (((1,), (0,)), ((), ()))
VMEM = pl.BlockSpec(memory_space=pltpu.VMEM)
HBM = pl.BlockSpec(memory_space=pltpu.HBM)
EARLY_BYTES = 12 * 2**20
GRAM_BYTES = 10 * 2**20
IMAGE_BYTES = 10 * 2**20


def swap(count, bit):
    return [(place, place ^ bit) for place in range(count)]


class Ring:
    def __init__(self, data_count, trow_count):
        self.data_count = data_count
        self.count = data_count * trow_count
        self.cells = []
        for trow in range(trow_count):
            along = range(data_count) if trow % 2 == 0 else reversed(range(data_count))
            self.cells += [(data, trow) for data in along]
        flat = [data * trow_count + trow for data, trow in self.cells]
        self.ahead = [(flat[i], flat[(i + 1) % self.count]) for i in range(self.count)]
        self.back = [(target, source) for source, target in self.ahead]
        self.far = self.count // 2
        self.offsets = [0]
        for distance in range(1, self.far):
            self.offsets += [-distance, distance]
        self.offsets.append(self.far)
        self.place = np.zeros((data_count, trow_count), np.int32)
        for position, (data, trow) in enumerate(self.cells):
            self.place[data, trow] = position
        self.rounds = np.zeros((self.count, data_count), np.int32)
        self.chunk, self.trow, self.data = (np.zeros((self.count, self.count), np.int32) for _ in range(3))
        for position, (data, trow) in enumerate(self.cells):
            first = trow * data_count
            far_data = self.cells[(position + self.far) % self.count][0]
            near = sorted(
                range(first, first + data_count),
                key=lambda q: (self.cells[q][0] == far_data, abs(q - position), q),
            )
            chunk_of = {}
            for turn, other in enumerate(near):
                self.rounds[position, turn] = self.offsets.index(other - position)
                chunk_of[self.cells[other][0]] = turn
            for index, offset in enumerate(self.offsets):
                other_data, other_trow = self.cells[(position + offset) % self.count]
                self.chunk[position, index] = chunk_of[other_data]
                self.trow[position, index] = other_trow
                self.data[position, index] = other_data

    def move(self, ahead, back):
        axes = ("dp", "trow")
        return [lax.ppermute(ahead, axes, self.ahead), lax.ppermute(back, axes, self.back)]

    def last(self, ahead, back, rows, more=0):
        half = (rows // 2 + 15) // 16 * 16 + more
        return self.move(ahead[:half], back[half:rows])


ORDER = (3, 2, 1, 0)


def split(value):
    high = value.astype(jnp.bfloat16)
    return high, (value - high.astype(jnp.float32)).astype(jnp.bfloat16)


def dot(a, b, dims):
    return lax.dot_general(a, b, dims, preferred_element_type=jnp.float32)


def product(a, b):
    (a_high, a_low), (b_high, b_low) = a, b
    return dot(a_high, b_high, NN) + (dot(a_high, b_low, NN) + dot(a_low, b_high, NN))


def tile_copies(whole_ref, tile_ref, me, piece, block, semaphores):
    copies = []
    for start in range(0, tile_ref.shape[1], block):
        lanes = pl.ds(start, block)
        for index, j in enumerate(ORDER):
            place = pl.ds(pl.multiple_of(jnp.bitwise_xor(me, j) * piece, 8), piece)
            pair = whole_ref.at[place, lanes], tile_ref.at[pl.ds(index * piece, piece), lanes]
            copies.append(pltpu.make_async_copy(*pair, semaphores.at[len(copies)]))
    return copies


def fetch_kernel(sizes, meta, gram_ref, tile_ref, come):
    loads = tile_copies(gram_ref, tile_ref, meta[0], *sizes, come)
    for load in loads:
        load.start()
    for load in loads:
        load.wait()


def pick_rows(out_ref, head_ref, feature_ref, data_place, data_count, piece):
    head_part = head_ref.shape[0]
    out_ref[:head_part, :] = head_ref[...]
    if piece % 16 == 0:
        out_ref[head_part:, :] = feature_ref[pl.ds(pl.multiple_of(data_place * piece, 16), piece), :]
    else:
        for data in range(data_count):

            @pl.when(data_place == data)
            def _():
                out_ref[head_part:, :] = feature_ref[data * piece : (data + 1) * piece, :]


def pick_kernel(sizes, meta, *refs):
    turns, choices, width, piece, data_count = sizes
    *shard_refs, out_ref = refs
    for index, turn in enumerate(turns):
        for shard_ref, choice in zip(shard_refs, choices):

            @pl.when(meta[turn] == choice)
            def _():
                pick_rows(out_ref.at[index], shard_ref.at[width:], shard_ref, meta[data_count], data_count, piece)


def place_rows(round_refs, me, head_part, rows, target, turn, count):
    for group in range(len(round_refs) // 3):
        own, far, near = round_refs[3 * group : 3 * group + 3]
        for inner in range(own.shape[0]):
            lanes = slice(turn * count, (turn + 1) * count)
            parts = [near[1, inner], far[inner], near[0, inner], own[inner]]
            for j, part in zip(ORDER, parts):
                at = pl.multiple_of(jnp.bitwise_xor(me, j) * head_part, 16)
                target[pl.ds(at, head_part), lanes] = part[:head_part, :]
            rows[:, lanes] = jnp.concatenate([part[head_part:, :] for part in parts], axis=0)
            turn += 1


def early_kernel(sizes, meta, *refs):
    n, width, head_part, block, groups = sizes
    shard_refs, refs = refs[: n - 1], refs[n - 1 :]
    round_refs, refs = refs[: 3 * groups], refs[3 * groups :]
    prior_ref, now_ref, later_ref, columns, rows, target = refs
    count = shard_refs[0].shape[1]
    for index in range(n - 1):
        lanes = pl.ds(pl.multiple_of(meta[index] * count, 128), count)
        base = pl.multiple_of(meta[n + index] * width, 16)
        columns[pl.ds(base, width), lanes] = shard_refs[index][:width, :]
    place_rows(round_refs, meta[2 * n], head_part, rows, target, 0, count)
    done = columns.shape[1] - count
    scale = 1.0 / columns.shape[1]
    for start in range(0, columns.shape[0], block):
        lanes = slice(start, start + block)
        column = columns[lanes, :done]
        value = prior_ref[:, lanes] + dot(rows[:, :done], column, NT) * scale
        now_ref[:, lanes], later_ref[:, lanes] = value[: now_ref.shape[0]], value[now_ref.shape[0] :]


def rest_kernel(sizes, meta, low_ref, high_ref, columns, target, side_ref, last_columns):
    n, width, block = sizes
    done = columns.shape[1] - last_columns.shape[1]
    last_columns[...] = columns[:, done:]
    base = pl.multiple_of(meta[2 * n - 1] * width, 16)
    half = low_ref.shape[0]
    last_columns[pl.ds(base, half), :] = low_ref[...]
    last_columns[pl.ds(pl.multiple_of(base + half, 16), width - half), :] = high_ref[...]
    for start in range(0, columns.shape[0], block):
        lanes = slice(start, start + block)
        side_ref[lanes, :] = dot(columns[lanes, :done], target[:, :done], NT)


def tile_rows_of(first, early, last_rows, last_columns, block, scale, tile_ref, gram_ref, me, piece, stored):
    part = pl.ds(first * piece, tile_ref.shape[0])
    copies = []
    for start in range(0, tile_ref.shape[1], block):
        lanes = pl.ds(start, block)
        tile_ref[:, lanes] = early[:, lanes] + dot(last_rows[part, :], last_columns[lanes, :], NT) * scale
        for index in range(tile_ref.shape[0] // piece):
            place = pl.ds(pl.multiple_of(jnp.bitwise_xor(me, ORDER[first + index]) * piece, 8), piece)
            made = tile_ref.at[pl.ds(index * piece, piece), lanes]
            copies.append(pltpu.make_async_copy(made, gram_ref.at[place, lanes], stored.at[len(copies)]))
            copies[-1].start()
    return copies


def first_kernel(sizes, meta, *refs):
    n, piece, total_rows, head_part, block = sizes
    round_refs = refs[:3]
    early, early_side, last_columns, image_ref, gram_ref, tile_ref = refs[3:9]
    side_high, side_low, last_rows, last_target, stored = refs[9:]
    count = last_rows.shape[1]
    place_rows(round_refs, meta[2 * n], head_part, last_rows, last_target, 0, count)
    scale = 1.0 / total_rows
    me = meta[2 * n]
    copies = tile_rows_of(0, early, last_rows, last_columns, block, scale, tile_ref, gram_ref, me, piece, stored)
    side = early_side[...] + dot(last_columns[...], last_target[...], NT)
    side_high[...], side_low[...] = split(side * scale)
    image_ref[...] = product(split(tile_ref[:piece, :]), (side_high[...], side_low[...]))
    for copy in copies:
        copy.wait()


def second_kernel(sizes, meta, *refs):
    tile_ref, last_rows, side_high, side_low, last_target, rows, target, right_ref, image_ref = refs
    piece = sizes
    total_rows, count = rows.shape[1], last_rows.shape[1]
    done = total_rows - count
    image_ref[...] = product(split(tile_ref[piece:, :]), (side_high[...], side_low[...]))
    own = slice(3 * piece, 4 * piece)
    right = dot(rows[own, :done], target[:, :done], NT) + dot(last_rows[own, :], last_target[...], NT)
    right_ref[...] = right * (1.0 / total_rows)


def third_kernel(sizes, meta, *refs):
    piece, block, total_rows = sizes
    early, last_columns, last_rows, side_high, side_low, _, gram_ref, image_ref, tile_ref, stored = refs
    scale = 1.0 / total_rows
    me = meta[0]
    copies = tile_rows_of(2, early, last_rows, last_columns, block, scale, tile_ref, gram_ref, me, piece, stored)
    value = product(split(tile_ref[...]), (side_high[...], side_low[...]))
    image_ref[...] = value.reshape(image_ref.shape)
    for copy in copies:
        copy.wait()


def weighted(parts, others):
    return sum(jnp.sum(a * b, axis=0, keepdims=True) for a, b in zip(parts, others))


def partial_kernel(sizes, meta, *refs):
    n, data_count, piece, block = sizes
    shard_refs = refs[: n - 1]
    tile_ref, start_ref, near_ref, far_ref, penalty_ref, total_ref, sums_ref, far_high, far_low, side = refs[n - 1 :]
    for index in range(n - 1):
        base = pl.multiple_of((meta[n + index] * data_count + meta[index]) * piece, 8)
        side[pl.ds(base, piece), :] = shard_refs[index][...]
    base = (meta[2 * n - 1] * data_count + meta[n - 1]) * piece
    side[pl.ds(pl.multiple_of(base, 8), piece), :] = jnp.zeros((piece, side.shape[1]), jnp.float32)
    total = product(split(tile_ref[...]), split(side[...]))
    own, start = shard_refs[0][...], start_ref[...]
    others = [near_ref[1], far_ref[...], near_ref[0], own]
    parts = [total[index * piece : (index + 1) * piece] for index in range(len(ORDER))]
    parts[-1] = parts[-1] + penalty_ref[...] * own
    for index, part in enumerate(parts):
        total_ref[index] = part
    sums = [weighted([a], [b]) for a, b in ((start, start), (start, own), (own, own))]
    sums_ref[...] = jnp.concatenate(sums + [weighted(parts, others)], axis=0)
    lanes = pl.ds(pl.multiple_of(base // block * block, 128), block)
    for place in range(block // piece):

        @pl.when(base % block == place * piece)
        def _():
            far_high[...], far_low[...] = split(tile_ref[:, lanes][:, place * piece : (place + 1) * piece])


def image_kernel(sizes, meta, *refs):
    piece = sizes
    low_ref, high_ref, total_ref, far_high, far_low, early_ref, own_ref, near_ref, far_ref, out_ref, sums_ref = refs
    side = jnp.concatenate([low_ref[...], high_ref[...]], axis=0)
    value = product((far_high[...], far_low[...]), split(side))
    others = [near_ref[1], far_ref[...], near_ref[0], own_ref[...]]
    parts = [value[index * piece : (index + 1) * piece] for index in range(len(ORDER))]
    early = early_ref[...]
    sums = jnp.concatenate([early[:3], early[3:] + weighted(parts, others)], axis=0)
    sums_ref[...] = jnp.broadcast_to(sums[None], sums_ref.shape)
    for index, j in enumerate(ORDER):
        out_ref[(3, 1, 2, 0).index(j)] = total_ref[index] + parts[index]


def call(body, meta, inputs, in_specs, out_specs, out_shape, scratch, vmem, flops, read, aliases={}):
    return pl.pallas_call(
        body,
        grid_spec=pltpu.PrefetchScalarGridSpec(
            num_scalar_prefetch=1,
            grid=(1,),
            in_specs=in_specs,
            out_specs=out_specs,
            scratch_shapes=scratch,
        ),
        out_shape=out_shape,
        input_output_aliases=aliases,
        compiler_params=pltpu.CompilerParams(vmem_limit_bytes=vmem),
        cost_estimate=pl.CostEstimate(flops=flops, bytes_accessed=read, transcendentals=0),
    )(meta, *inputs)


def shards(embeddings, targets, gram_prior, penalty):
    row_count = embeddings.shape[0]
    width = embeddings.shape[3]
    heads = targets.shape[1]
    data_count = lax.axis_size("dp")
    trow_count = lax.axis_size("trow")
    tcol_count = lax.axis_size("tcol")
    piece = width // data_count
    total_rows = row_count * data_count
    tile_rows = tcol_count * piece
    tile_columns = trow_count * width
    head_part = heads // tcol_count
    data_place = lax.axis_index("dp")
    me = lax.axis_index("tcol")
    ring = Ring(data_count, trow_count)
    n = ring.count
    position = jnp.asarray(ring.place)[data_place, lax.axis_index("trow")]
    lookup = np.concatenate([ring.rounds, ring.chunk, ring.trow, ring.data, ring.trow], axis=1)
    lookup = jnp.asarray(lookup)[position]
    pick_meta = jnp.concatenate([lookup[:data_count], jnp.reshape(data_place, (1,)).astype(jnp.int32)])
    me_meta = jnp.reshape(me, (1,)).astype(jnp.int32)
    gram_meta = jnp.concatenate([lookup[data_count : data_count + 2 * n], me_meta])
    image_meta = jnp.concatenate([lookup[data_count + 2 * n :], me_meta])

    f32, bf16 = jnp.float32, jnp.bfloat16
    features = embeddings.reshape(row_count, width).T
    head_rows = lax.dynamic_slice_in_dim(targets, me * head_part, head_part, axis=1).T
    payload = jnp.concatenate([features, head_rows], axis=0)

    def pieces_of(turns):
        if turns == [0]:
            own_rows = lax.dynamic_slice_in_dim(features, data_place * piece, piece, axis=0)
            return jnp.concatenate([head_rows, own_rows], axis=0)[None]
        choices = sorted(set(ring.rounds[:, turns].ravel().tolist()))
        return call(
            functools.partial(pick_kernel, (turns, choices, width, piece, data_count)),
            pick_meta,
            [gathered[choice] for choice in choices],
            [VMEM] * len(choices),
            VMEM,
            jax.ShapeDtypeStruct((len(turns), head_part + piece, row_count), payload.dtype),
            [],
            2**20,
            0,
            4 * len(turns) * (head_part + piece) * row_count,
        )

    split_turns = [[0], list(range(1, data_count - 1)), [data_count - 1]]
    ready = [int(np.abs(np.asarray(ring.offsets)[ring.rounds[:, turns]]).max()) for turns in split_turns]
    gathered, groups, waiting = [payload], {}, []

    def near_of(group, mine, far):
        groups[group] = [mine, far, lax.ppermute(jnp.stack([mine, far]), "tcol", swap(tcol_count, 1))]

    def open_groups(step):
        for group, (turns, when) in enumerate(zip(split_turns, ready)):
            if when == step:
                mine = pieces_of(turns)
                waiting.append((group, mine, lax.ppermute(mine, "tcol", swap(tcol_count, 2))))

    block = next(size for size in (512, 256, 128) if tile_columns % size == 0)
    far_block = math.lcm(piece, 128)
    tile_semaphores = pltpu.SemaphoreType.DMA((tcol_count * (tile_columns // block),))

    def fetch(whole):
        return call(
            functools.partial(fetch_kernel, (piece, block)),
            me_meta,
            [whole],
            [HBM],
            VMEM,
            jax.ShapeDtypeStruct((tile_rows, tile_columns), f32),
            [tile_semaphores],
            2**20,
            0,
            8 * tile_rows * tile_columns,
        )

    prior = gram_prior.reshape(tile_rows, tile_columns)
    open_groups(0)
    ahead = back = payload
    for step in range(1, ring.far + 1):
        if step < ring.far:
            arrived = ahead, back = ring.move(ahead, back)
        else:
            arrived = ring.last(ahead, back, width)
        if step == 1:
            gram_meta, image_meta, pick_meta, *arrived = lax.optimization_barrier(
                (gram_meta, image_meta, pick_meta, *arrived)
            )
        if step == ring.far - 2:
            prior, *arrived = lax.optimization_barrier((prior, *arrived))
            prior = fetch(prior)
        if step == ring.far - 1:
            prior, *arrived = lax.optimization_barrier((prior, *arrived))
        while waiting:
            group, mine, far = waiting.pop()
            if step == ring.far:
                early, mine, far, *arrived = lax.optimization_barrier((early, mine, far, *arrived))
            else:
                mine, far, *arrived = lax.optimization_barrier((mine, far, *arrived))
            near_of(group, mine, far)
        gathered += arrived
        open_groups(step)
        if step == ring.far - 1:
            early, early_later, columns, rows, target = call(
                functools.partial(early_kernel, (n, width, head_part, block, 2)),
                gram_meta,
                [*gathered, *groups[0], *groups[1], prior],
                [VMEM] * (n + 6),
                [VMEM] * 5,
                [
                    jax.ShapeDtypeStruct((2 * piece, tile_columns), f32),
                    jax.ShapeDtypeStruct((2 * piece, tile_columns), f32),
                    jax.ShapeDtypeStruct((tile_columns, total_rows), bf16),
                    jax.ShapeDtypeStruct((tile_rows, total_rows), bf16),
                    jax.ShapeDtypeStruct((heads, total_rows), bf16),
                ],
                [],
                EARLY_BYTES,
                2 * tile_rows * tile_columns * (total_rows - row_count),
                8 * tile_rows * tile_columns,
            )
    gram_shape = jax.ShapeDtypeStruct((tile_rows, tile_columns), f32)
    piece_shape = jax.ShapeDtypeStruct((piece, heads), f32)

    def tile_scratch(pieces):
        shape = (pieces * piece, tile_columns)
        return [pltpu.VMEM(shape, f32), pltpu.SemaphoreType.DMA((pieces * (tile_columns // block),))]

    early_side, last_columns = call(
        functools.partial(rest_kernel, (n, width, block)),
        gram_meta,
        [*gathered[-2:], columns, target],
        [VMEM] * 4,
        [VMEM] * 2,
        [
            jax.ShapeDtypeStruct((tile_columns, heads), f32),
            jax.ShapeDtypeStruct((tile_columns, row_count), bf16),
        ],
        [],
        EARLY_BYTES,
        2 * tile_columns * heads * (total_rows - row_count),
        2 * tile_columns * total_rows,
    )
    sent, gram, first_tile, side_high, side_low, last_rows, last_target = call(
        functools.partial(first_kernel, (n, piece, total_rows, head_part, block)),
        gram_meta,
        [*groups[2], early, early_side, last_columns],
        [VMEM] * 6,
        [VMEM, HBM] + [VMEM] * 5,
        [
            piece_shape,
            gram_shape,
            jax.ShapeDtypeStruct((2 * piece, tile_columns), f32),
            jax.ShapeDtypeStruct((tile_columns, heads), bf16),
            jax.ShapeDtypeStruct((tile_columns, heads), bf16),
            jax.ShapeDtypeStruct((tile_rows, row_count), bf16),
            jax.ShapeDtypeStruct((heads, row_count), bf16),
        ],
        tile_scratch(2)[1:],
        GRAM_BYTES,
        2 * piece * tile_columns * (2 * row_count + 3 * heads),
        16 * piece * tile_columns,
    )
    penalty_rows = penalty.reshape(piece, 1)
    received = lax.ppermute(sent, "tcol", swap(tcol_count, 1))
    start, far_part = call(
        functools.partial(second_kernel, piece),
        me_meta,
        [first_tile, last_rows, side_high, side_low, last_target, rows, target],
        [VMEM] * 7,
        [VMEM, VMEM],
        [piece_shape, piece_shape],
        [],
        GRAM_BYTES,
        6 * piece * tile_columns * heads,
        4 * piece * tile_columns,
    )
    far_part, early_later = lax.optimization_barrier((far_part + received, early_later))
    far_sum = lax.ppermute(far_part, "tcol", swap(tcol_count, 2))
    gram, kept = call(
        functools.partial(third_kernel, (piece, block, total_rows)),
        me_meta,
        [early_later, last_columns, last_rows, side_high, side_low, gram],
        [VMEM] * 5 + [HBM],
        [HBM, VMEM],
        [gram_shape, jax.ShapeDtypeStruct((2, piece, heads), f32)],
        tile_scratch(2),
        GRAM_BYTES,
        4 * piece * tile_columns * (row_count + 3 * heads),
        16 * piece * tile_columns,
        {6: 0},
    )
    halves = [kept[0][: piece // 2], kept[0][piece // 2 :]]
    near_sum = jnp.concatenate([lax.ppermute(part, "tcol", swap(tcol_count, 1)) for part in halves], axis=0)
    image = kept[1] + near_sum + penalty_rows * start + far_sum
    far_image = lax.ppermute(image, "tcol", swap(tcol_count, 2))
    near_images = lax.ppermute(jnp.stack([image, far_image]), "tcol", swap(tcol_count, 1))
    images = [image]
    ahead = back = image
    for step in range(1, ring.far + 1):
        if step < ring.far:
            arrived = ahead, back = ring.move(ahead, back)
        else:
            arrived = ring.last(ahead, back, piece, piece // 3 // 16 * 16)
        if step == ring.far - 2:
            *arrived, gram = lax.optimization_barrier((*arrived, gram))
            tile = fetch(gram)
        if step == ring.far - 1:
            *arrived, tile = lax.optimization_barrier((*arrived, tile))
        images += arrived
    part_shape = jax.ShapeDtypeStruct((tcol_count, piece, heads), f32)
    far_shape = jax.ShapeDtypeStruct((tile_rows, piece), bf16)
    total, early_sums, far_high, far_low = call(
        functools.partial(partial_kernel, (n, data_count, piece, far_block)),
        image_meta,
        [*images[:-2], tile, start, near_images, far_image, penalty_rows],
        [VMEM] * (n + 4),
        [VMEM] * 4,
        [part_shape, jax.ShapeDtypeStruct((4, heads), f32), far_shape, far_shape],
        [pltpu.VMEM((tile_columns, heads), f32)],
        IMAGE_BYTES,
        6 * tile_rows * tile_columns * heads,
        4 * tile_rows * tile_columns,
    )
    axes = ("dp", "trow", "tcol")
    second, sums = call(
        functools.partial(image_kernel, piece),
        image_meta,
        [*images[-2:], total, far_high, far_low, early_sums, image, near_images, far_image],
        [VMEM] * 9,
        [VMEM] * 2,
        [part_shape, jax.ShapeDtypeStruct((n * tcol_count, 4, heads), f32)],
        [],
        IMAGE_BYTES,
        6 * tile_rows * piece * heads,
        4 * tile_rows * piece,
    )
    sums, second = lax.optimization_barrier((sums, second))
    sums = lax.all_to_all(sums, axes, split_axis=0, concat_axis=0, tiled=True)
    received = lax.ppermute(second[:2], "tcol", swap(tcol_count, 1))
    far_second = lax.ppermute(second[2] + received[0], "tcol", swap(tcol_count, 2))
    far_second, sums = lax.optimization_barrier((far_second, sums))
    sums = jnp.sum(sums, axis=0)
    second = second[3] + received[1] + far_second

    norm, curvature, image_norm, image_curvature = sums[0], sums[1], sums[2], sums[3]
    step = norm / curvature
    norm_next = step * step * image_norm - norm
    ratio = norm_next / norm
    moved_curvature = step * (step * image_curvature - (1.0 + ratio) * image_norm)
    next_step = norm_next / moved_curvature
    residual = start - step * image
    direction = residual + ratio * start
    weights = step * start + next_step * direction
    residual = residual - next_step * ((1.0 + ratio) * image - step * second)
    out_shape = (1, 1, 1, piece, heads)
    return (gram.reshape(gram_prior.shape), weights.reshape(out_shape), residual.reshape(out_shape))


def solution(mesh):
    placed = (
        P("dp", "tcol", "trow", None),
        P("dp", None),
        P(None, "trow", "dp", None, "tcol"),
        P("tcol", "trow", "dp", None),
    )
    return jax.shard_map(
        shards,
        mesh=mesh,
        in_specs=placed,
        out_specs=(
            P(None, "trow", "dp", None, "tcol"),
            P("tcol", "trow", "dp", None, None),
            P("tcol", "trow", "dp", None, None),
        ),
        check_vma=False,
    )
```
